32 devices in a mesh: ctx: 2 (over core), head: 16 (over z, y, x).
Axes of the slice: x: 2, y: 2, z: 4, core: 2. Of those that a mesh axis runs over, the one named last changes fastest.
Arguments:
- queries: bfloat16 [2048, 64, 128], P(('ctx', 'head')), may hold values from -6 to 6
- keys: bfloat16 [2048, 8, 128], P(('ctx', 'head')), may hold values from -6 to 6
- values: bfloat16 [2048, 8, 128], P(('ctx', 'head')), may hold values from -6 to 6
- outputs: bfloat16 [2048, 64, 128], P(('ctx', 'head')), may hold values from -6 to 6
- out_grads: bfloat16 [2048, 64, 128], P(('ctx', 'head')), may hold values from -1.5 to 1.5
- log_norms: float32 [2048, 64], P(('ctx', 'head')), may hold values from 1 to 4
- block_doc: int32 [16], replicated, may hold values from 0 to 5, never falling along the last dimension, each value on 1 to 8 neighbouring positions
Outputs:
- query_grads: bfloat16 [2048, 64, 128], P(('ctx', 'head'))
- key_grads: bfloat16 [2048, 8, 128], P(('ctx', 'head'))
- value_grads: bfloat16 [2048, 8, 128], P(('ctx', 'head'))
The draws below stay inside these ranges and needn't reach their ends.
Inputs may be any that keep to these rules, and one draw needn't show every extreme that they name: `block_doc`: block ids never fall; each document covers 1 to 8 blocks, and one covers exactly 8.
All inputs are finite; a program needn't handle non-finite values.
Results may differ from the reference program's by a relative error of at most 0.0058.
Values may be sent and summed in bfloat16 or wider, within the bound.
No kernel may reach another device: no remote copies, remote signals or barrier semaphores. Data moves between devices by JAX's collectives and lax.ppermute only.
A program may use at most 64 MiB of HBM per device.

```python
import math
import jax
import jax.numpy as jnp
import numpy as np
from jax import lax

QUERY_HEADS = 64
KEY_VALUE_HEADS = 8
HEAD_SIZE = 128
BLK = 128
TOK_DEV = 64
WINDOW_TOKENS = 2048
NBLK = 16
MAXDOC = 8
COUNT = 6
N_HEAD = 16


def shard_levels(rng, dims, split, smallest, largest):
    loudness, own = 1.0, jax.random.fold_in(rng, 6)
    for dim, blocks in split:
        heights = jnp.exp(jax.random.uniform(jax.random.fold_in(own, dim), (blocks,), jnp.float32, smallest / len(split), largest / len(split)))
        loudness = loudness * jnp.repeat(heights, dims[dim] // blocks).reshape([-1 if axis == dim else 1 for axis in range(len(dims))])
    return loudness


def split_up(amount, total, reach, slope):
    portions = [(1 << 20) // math.isqrt(standing ** slope) + 1 for standing in range(2, amount + 1)]
    surplus, counts = total - reach - (amount - 1), [1] * (amount - 1)
    while surplus > 0:
        free = [i for i in range(amount - 1) if counts[i] < reach]
        whole, remaining = sum([portions[i] for i in free]), surplus
        for i in free:
            more = min(reach - counts[i], max(1, remaining * portions[i] // whole), surplus)
            counts[i] = counts[i] + more
            surplus = surplus - more
    return np.array([reach] + counts)


def ragged_sizes(own_key, amount, total, most, skew):
    if amount == 2:
        one = jax.random.randint(own_key, (), max(1, total - most), min(most, total - 1) + 1)
        return jnp.stack([one, total - one])
    lengths = jnp.asarray(split_up(amount, total, most, skew), jnp.int32)
    twos = (amount - 1) // 2
    donor, sink = lengths[1:1 + 2 * twos:2], lengths[2:2 + 2 * twos:2]
    margin = jnp.minimum(donor - 1, most - sink)
    passed = jax.random.randint(jax.random.fold_in(own_key, 1), (twos,), 0, 1 << 20) % (margin + 1)
    lengths = lengths.at[1:1 + 2 * twos:2].set(donor - passed).at[2:2 + 2 * twos:2].set(sink + passed)
    return lengths[jax.random.permutation(jax.random.fold_in(own_key, 2), amount)]


def scatter_about(key, dims, scale, reach, split=(), kind=jnp.bfloat16):
    factor_of = shard_levels(key, dims, split, -0.22, 0.18) if split else 1.0
    result = jax.random.normal(key, dims, jnp.float32) * scale * factor_of
    return jnp.minimum(jnp.maximum(result, -reach), reach).astype(kind)


def setup_inputs(seed: int = 0) -> dict:
    splits = jax.random.split(jax.random.key(seed), 8)
    queries = scatter_about(splits[0], (WINDOW_TOKENS, QUERY_HEADS, HEAD_SIZE), 1.0, 6.0, ((0, 32),))
    keys = scatter_about(splits[1], (WINDOW_TOKENS, KEY_VALUE_HEADS, HEAD_SIZE), 1.0, 6.0, ((0, 32),))
    values = scatter_about(splits[2], (WINDOW_TOKENS, KEY_VALUE_HEADS, HEAD_SIZE), 1.0, 6.0, ((0, 32),))
    outputs = scatter_about(splits[3], (WINDOW_TOKENS, QUERY_HEADS, HEAD_SIZE), 1.0, 6.0, ((0, 32),))
    out_grads = scatter_about(splits[4], (WINDOW_TOKENS, QUERY_HEADS, HEAD_SIZE), 0.25, 1.5, ((0, 32),))
    log_norms = jnp.clip(1.0 + 3.0 * jax.random.uniform(splits[5], (WINDOW_TOKENS, QUERY_HEADS), jnp.float32) ** shard_levels(splits[5], (WINDOW_TOKENS, QUERY_HEADS), ((0, 32),), -0.2, 0.2), 1.0, 4.0)
    block_doc = jnp.searchsorted(jnp.cumsum(ragged_sizes(splits[6], COUNT, NBLK, MAXDOC, 1)), jnp.arange(NBLK), side="right").astype(jnp.int32)
    return dict(queries=queries, keys=keys, values=values, outputs=outputs, out_grads=out_grads, log_norms=log_norms, block_doc=block_doc)


def tile_pass(q_tile, grad_tile, norm_tile, delta_tile, key_tile, value_tile, visible, scale_factor):
    scores = jnp.dot(q_tile, key_tile.T, preferred_element_type=jnp.float32) * scale_factor
    soft_probs = jnp.where(visible, jnp.exp(scores - norm_tile[:, None]), 0.0)
    grad_probs = jnp.dot(grad_tile, value_tile.T, preferred_element_type=jnp.float32)
    grad_scores = (soft_probs * (grad_probs - delta_tile[:, None])).astype(jnp.bfloat16)
    query_part = jnp.dot(grad_scores, key_tile, preferred_element_type=jnp.float32) * scale_factor
    key_part = jnp.dot(grad_scores.T, q_tile, preferred_element_type=jnp.float32) * scale_factor
    value_part = jnp.dot(soft_probs.astype(jnp.bfloat16).T, grad_tile, preferred_element_type=jnp.float32)
    return query_part, key_part, value_part


def reference(queries, keys, values, outputs, out_grads, log_norms, block_doc):
    window_length = queries.shape[0]
    group_len = TOK_DEV * N_HEAD
    tile_rows = min(512, group_len)
    span_tiles = group_len // tile_rows
    tile_count = window_length // tile_rows
    query_group_factor = QUERY_HEADS // KEY_VALUE_HEADS
    scale_factor = HEAD_SIZE ** -0.5
    deltas = jnp.sum(out_grads.astype(jnp.float32) * outputs.astype(jnp.float32), axis=-1)
    token_docs = jnp.repeat(block_doc, BLK)
    offsets = jnp.arange(tile_rows, dtype=jnp.int32)

    def per_head(head_index):
        kv_index = head_index // query_group_factor
        q_head = lax.dynamic_index_in_dim(queries, head_index, 1, keepdims=False)
        grad_head = lax.dynamic_index_in_dim(out_grads, head_index, 1, keepdims=False)
        norm_head = lax.dynamic_index_in_dim(log_norms, head_index, 1, keepdims=False)
        delta_head = lax.dynamic_index_in_dim(deltas, head_index, 1, keepdims=False)
        key_head = lax.dynamic_index_in_dim(keys, kv_index, 1, keepdims=False)
        value_head = lax.dynamic_index_in_dim(values, kv_index, 1, keepdims=False)

        def over_rows(carried, row_index):
            q_start = row_index * tile_rows
            q_tile = lax.dynamic_slice_in_dim(q_head, q_start, tile_rows, 0)
            grad_tile = lax.dynamic_slice_in_dim(grad_head, q_start, tile_rows, 0)
            norm_tile = lax.dynamic_slice_in_dim(norm_head, q_start, tile_rows, 0)
            delta_tile = lax.dynamic_slice_in_dim(delta_head, q_start, tile_rows, 0)
            docs_rows = lax.dynamic_slice_in_dim(token_docs, q_start, tile_rows, 0)

            def inner_step(offset_index, inner_state):
                col_index = row_index - span_tiles + offset_index
                in_range = col_index >= 0
                k_start = jnp.maximum(col_index, 0) * tile_rows
                docs_cols = lax.dynamic_slice_in_dim(token_docs, k_start, tile_rows, 0)
                visible = (docs_rows[:, None] == docs_cols[None, :]) & ((q_start + offsets)[:, None] >= (k_start + offsets)[None, :]) & in_range

                def update(current):
                    query_acc, key_acc, value_acc = current
                    key_tile = lax.dynamic_slice_in_dim(key_head, k_start, tile_rows, 0)
                    value_tile = lax.dynamic_slice_in_dim(value_head, k_start, tile_rows, 0)
                    query_part, key_part, value_part = tile_pass(q_tile, grad_tile, norm_tile, delta_tile, key_tile, value_tile, visible, scale_factor)
                    key_acc = lax.dynamic_update_slice_in_dim(key_acc, lax.dynamic_slice_in_dim(key_acc, k_start, tile_rows, 0) + key_part, k_start, 0)
                    value_acc = lax.dynamic_update_slice_in_dim(value_acc, lax.dynamic_slice_in_dim(value_acc, k_start, tile_rows, 0) + value_part, k_start, 0)
                    return (query_acc + query_part, key_acc, value_acc)

                return lax.cond(jnp.any(visible), update, lambda current: current, inner_state)

            key_acc, value_acc = carried
            zero_tile = jnp.zeros((tile_rows, HEAD_SIZE), jnp.float32)
            query_acc, key_acc, value_acc = lax.fori_loop(0, span_tiles + 1, inner_step, (zero_tile, key_acc, value_acc))
            return (key_acc, value_acc), query_acc.astype(jnp.bfloat16)

        zero_rows = jnp.zeros((window_length, HEAD_SIZE), jnp.float32)
        (key_acc, value_acc), query_tiles = lax.scan(over_rows, (zero_rows, zero_rows), jnp.arange(tile_count, dtype=jnp.int32))
        return query_tiles.reshape(window_length, HEAD_SIZE), key_acc.astype(jnp.bfloat16), value_acc.astype(jnp.bfloat16)

    query_heads, key_head_count, value_head_count = lax.map(per_head, jnp.arange(QUERY_HEADS, dtype=jnp.int32))
    query_grads = jnp.transpose(query_heads, (1, 0, 2))
    key_grad_total = jnp.sum(key_head_count.astype(jnp.float32).reshape(KEY_VALUE_HEADS, query_group_factor, window_length, HEAD_SIZE), axis=1)
    value_grad_total = jnp.sum(value_head_count.astype(jnp.float32).reshape(KEY_VALUE_HEADS, query_group_factor, window_length, HEAD_SIZE), axis=1)
    key_grads = jnp.transpose(key_grad_total.astype(jnp.bfloat16), (1, 0, 2))
    value_grads = jnp.transpose(value_grad_total.astype(jnp.bfloat16), (1, 0, 2))
    return (query_grads, key_grads, value_grads)
```

```python
import functools

import jax
import jax.numpy as jnp
from jax import lax
from jax.experimental import pallas as pl
from jax.experimental.pallas import tpu as pltpu
from jax.sharding import PartitionSpec as P

BLK = 128
LOG2E = 1.4426950408889634
STAT_ROWS = 32


def block_steps(meta, pkg, kv, dq, dk_acc, dv_acc, dq_acc, rows, tok, q_blocks, scale):
    sources = BLK // tok
    wide = sources * rows
    group = rows // tok
    dk_acc[...] = jnp.zeros_like(dk_acc)
    dv_acc[...] = jnp.zeros_like(dv_acc)

    def over_queries(i, _):
        last, first = meta[i], meta[q_blocks + i]
        mine = pl.ds(sources * i, sources)
        q = pkg[mine, 0:rows, :].reshape(wide, 128)
        g = pkg[mine, rows : 2 * rows, :].reshape(wide, 128)
        stats = pkg[mine, 2 * rows :, :].astype(jnp.float32)
        chunks = rows // 128
        lse3, delta3 = (
            stats[:, base : base + chunks]
            + stats[:, base + chunks : base + 2 * chunks]
            + stats[:, base + 2 * chunks : base + 3 * chunks]
            for base in (0, 3 * chunks)
        )
        flat = [(s, c) for s in range(sources) for c in range(chunks)]
        lse = jnp.concatenate([lse3[s, c : c + 1, :] for s, c in flat], axis=1) * LOG2E
        delta = jnp.concatenate([delta3[s, c : c + 1, :] for s, c in flat], axis=1)
        dq_acc[...] = jnp.zeros_like(dq_acc)

        def step(j, masked):
            k = kv[pl.ds(sources * j, sources), 0].reshape(BLK, 128)
            v = kv[pl.ds(sources * j, sources), 1].reshape(BLK, 128)
            s = lax.dot_general(k, q, (((1,), (1,)), ((), ())), preferred_element_type=jnp.float32)
            p = jnp.exp2(s * (scale * LOG2E) - lse)
            if masked:
                key_at = lax.broadcasted_iota(jnp.int32, (BLK, wide), 0)
                query_at = lax.broadcasted_iota(jnp.int32, (BLK, wide), 1) // group
                p = jnp.where(query_at >= key_at, p, 0.0)
            dp = lax.dot_general(v, g, (((1,), (1,)), ((), ())), preferred_element_type=jnp.float32)
            ds = (p * (dp - delta)).astype(jnp.bfloat16)
            at = pl.ds(pl.multiple_of(j * BLK, BLK), BLK)
            dv_acc[at, :] += jnp.dot(p.astype(jnp.bfloat16), g, preferred_element_type=jnp.float32)
            dk_acc[at, :] += jnp.dot(ds, q, preferred_element_type=jnp.float32)
            dq_acc[...] += lax.dot_general(
                ds, k, (((0,), (0,)), ((), ())), preferred_element_type=jnp.float32
            )

        def inner(j, _):
            step(j, False)
            return 0

        lax.fori_loop(first, last, inner, 0)
        step(last, True)
        dq[mine] = (dq_acc[...] * scale).astype(jnp.bfloat16).reshape(sources, rows, 128)
        return 0

    lax.fori_loop(0, q_blocks, over_queries, 0)


def whole_kernel(meta, pkg, kv, dq, dkv, dk_acc, dv_acc, dq_acc, *, rows, tok, q_blocks, scale):
    block_steps(meta, pkg, kv, dq, dk_acc, dv_acc, dq_acc, rows, tok, q_blocks, scale)
    shards = dkv.shape[0]
    dkv[:, 0] = (dk_acc[...] * scale).astype(jnp.bfloat16).reshape(shards, tok, 128)
    dkv[:, 1] = dv_acc[...].astype(jnp.bfloat16).reshape(shards, tok, 128)


def planes_kernel(meta, pkg, *refs, rows, tok, q_blocks, scale, planes):
    near, (dq, *near_grads) = refs[:planes], refs[planes : 2 * planes + 1]
    kv, dkv, dk_acc, dv_acc, dq_acc, sems = refs[2 * planes + 1 :]
    team = pkg.shape[0]
    slots = team // 2
    plane = meta[2 * q_blocks]

    def place(d, b):
        return pl.ds((b * planes + (plane ^ d)) * slots, slots)

    loads = [
        pltpu.make_async_copy(near[d].at[b * slots : (b + 1) * slots], kv.at[place(d, b)], sems.at[d, b])
        for d in range(planes)
        for b in range(2)
    ]
    for copy in loads:
        copy.start()
    for copy in loads:
        copy.wait()
    block_steps(meta, pkg, kv, dq, dk_acc, dv_acc, dq_acc, rows, tok, q_blocks, scale)
    shards = dkv.shape[0]
    dkv[:, 0] = (dk_acc[...] * scale).astype(jnp.bfloat16).reshape(shards, tok, 128)
    dkv[:, 1] = dv_acc[...].astype(jnp.bfloat16).reshape(shards, tok, 128)
    stores = [
        pltpu.make_async_copy(dkv.at[place(d, b)], near_grads[d].at[b * slots : (b + 1) * slots], sems.at[d, b])
        for d in range(planes)
        for b in range(2)
    ]
    for copy in stores:
        copy.start()
    for copy in stores:
        copy.wait()


def attention(meta, pkg, kv, rows, scale):
    by_plane = isinstance(kv, tuple)
    planes = len(kv) if by_plane else 1
    first = kv[0] if by_plane else kv
    shards, _, tok, head_dim = first.shape
    shards = shards * planes
    team = pkg.shape[0]
    q_blocks = team * tok // BLK
    wide = rows * (BLK // tok)
    vmem = pl.BlockSpec(memory_space=pltpu.VMEM)
    anywhere = pl.BlockSpec(memory_space=pl.ANY)
    sizes = dict(rows=rows, tok=tok, q_blocks=q_blocks, scale=scale)
    totals = [
        pltpu.VMEM((shards * tok, head_dim), jnp.float32),
        pltpu.VMEM((shards * tok, head_dim), jnp.float32),
        pltpu.VMEM((wide, head_dim), jnp.float32),
    ]
    dq_shape = jax.ShapeDtypeStruct((team, rows, head_dim), jnp.bfloat16)
    params = pltpu.CompilerParams(vmem_limit_bytes=56 * 1024 * 1024)
    if not by_plane:
        return pl.pallas_call(
            functools.partial(whole_kernel, **sizes),
            out_shape=(dq_shape, jax.ShapeDtypeStruct(kv.shape, jnp.bfloat16)),
            in_specs=[pl.BlockSpec(memory_space=pltpu.SMEM), vmem, vmem],
            out_specs=(vmem, vmem),
            scratch_shapes=totals,
            compiler_params=params,
            name="attention_grads",
        )(meta, pkg, kv)
    whole_kv = pltpu.VMEM((shards, 2, tok, head_dim), jnp.bfloat16)
    dq, *grads = pl.pallas_call(
        functools.partial(planes_kernel, planes=planes, **sizes),
        out_shape=(dq_shape,) + (jax.ShapeDtypeStruct(first.shape, jnp.bfloat16),) * planes,
        in_specs=[pl.BlockSpec(memory_space=pltpu.SMEM), vmem] + [anywhere] * planes,
        out_specs=(vmem,) + (anywhere,) * planes,
        scratch_shapes=[whole_kv, whole_kv] + totals + [pltpu.SemaphoreType.DMA((planes, 2))],
        compiler_params=params,
        name="attention_grads_planes",
    )(meta, pkg, *kv)
    return dq, grads


def pieces(x):
    high = lax.reduce_precision(x, 8, 7)
    rest = x - high
    mid = lax.reduce_precision(rest, 8, 7)
    low = rest - mid
    return [part.astype(jnp.bfloat16) for part in (high, mid, low)]


def per_device(queries, keys, values, outputs, out_grads, log_norms, block_doc):
    tok, heads, head_dim = queries.shape
    kv_heads = keys.shape[1]
    fan = heads // kv_heads
    n_ctx, n_head = lax.axis_size("ctx"), lax.axis_size("head")
    slots = kv_heads // 2
    planes = n_head // slots
    rows = tok * fan
    scale = head_dim**-0.5
    ctx, head = lax.axis_index("ctx"), lax.axis_index("head")
    both = ("ctx", "head")
    teams = [
        [(2 * c + b) * n_head + z * slots + r for b in range(2) for r in range(slots)]
        for c in range(n_ctx // 2)
        for z in range(planes)
    ]
    pairs = [
        [(2 * c + b) * n_head + h for b in range(2) for h in range(n_head)]
        for c in range(n_ctx // 2)
    ]

    by_plane = n_ctx == 2 and planes == 4

    def across(x, distance):
        step = distance * slots
        return lax.ppermute(x, "head", [(h, h ^ step) for h in range(n_head)])

    kv = jnp.stack([keys, values], axis=0).transpose(2, 0, 1, 3)
    if by_plane:
        kv = lax.all_to_all(kv, both, 0, 0, axis_index_groups=teams, tiled=True)
        second, first = across(kv, 2), across(kv, 1)
        kv = (kv, first, second, across(second, 1))
    else:
        kv = kv.reshape(2, 1, slots, 2, tok, head_dim)
        kv = jnp.broadcast_to(kv, (2, planes, slots, 2, tok, head_dim))
        kv = kv.reshape(2 * n_head, 2, tok, head_dim)
        kv = lax.all_to_all(kv, both, 0, 0, axis_index_groups=pairs, tiled=True)

    deltas = jnp.sum(out_grads.astype(jnp.float32) * outputs.astype(jnp.float32), axis=-1)
    stats = jnp.stack(pieces(log_norms) + pieces(deltas), axis=0)
    stats = stats.reshape(6, tok, kv_heads, fan).transpose(2, 0, 1, 3)
    stats = stats.reshape(kv_heads, 6 * rows // 128, 128)
    stats = jnp.pad(stats, ((0, 0), (0, STAT_ROWS - stats.shape[1]), (0, 0)))

    def by_group(x):
        return x.reshape(tok, kv_heads, fan, head_dim).transpose(1, 0, 2, 3).reshape(kv_heads, rows, head_dim)

    pkg = jnp.concatenate([by_group(queries), by_group(out_grads), stats], axis=1)
    pkg = lax.all_to_all(pkg, both, 0, 0, axis_index_groups=teams, tiled=True)

    pair, plane = ctx // 2, head // slots
    range_blocks = n_head * tok // BLK
    team_blocks = slots * tok // BLK
    at = jnp.stack(
        [(2 * pair + b) * range_blocks + plane * team_blocks + j for b in range(2) for j in range(team_blocks)]
    )
    first_block = jnp.sum(block_doc[None, :] < block_doc[at][:, None], axis=1, dtype=jnp.int32)
    ranges_before = 1 if n_ctx > 2 else 0
    base = (2 * pair - ranges_before) * range_blocks
    meta = jnp.concatenate([at - base, first_block - base, plane[None]]).astype(jnp.int32)

    if ranges_before:
        prior = lax.ppermute(kv[n_head:], "ctx", [(c, c + 2) for c in range(n_ctx - 2)])
        kv = jnp.concatenate([prior, kv], axis=0)
    dq, dkv = attention(meta, pkg, kv, rows, scale)
    if ranges_before:
        later = lax.ppermute(dkv[:n_head], "ctx", [(c + 2, c) for c in range(n_ctx - 2)])
        last = (dkv[2 * n_head :].astype(jnp.float32) + later.astype(jnp.float32)).astype(jnp.bfloat16)
        dkv = jnp.concatenate([dkv[n_head : 2 * n_head], last], axis=0)

    if by_plane:
        wider = lambda x: x.astype(jnp.float32)
        relayed = across(dkv[3], 1)
        far = (wider(dkv[2]) + wider(relayed)).astype(jnp.bfloat16)
        far, close = across(far, 2), across(dkv[1], 1)
        dkv = (wider(dkv[0]) + wider(far) + wider(close)).astype(jnp.bfloat16)
        dq = lax.all_to_all(dq, both, 0, 0, axis_index_groups=teams, tiled=True)
        dkv = lax.all_to_all(dkv, both, 0, 0, axis_index_groups=teams, tiled=True)
    else:
        dkv = lax.all_to_all(dkv, both, 0, 0, axis_index_groups=pairs, tiled=True)
        dq = lax.all_to_all(dq, both, 0, 0, axis_index_groups=teams, tiled=True)
        dkv = dkv.reshape(2, planes, slots, 2, tok, head_dim).astype(jnp.float32).sum(axis=1)
        dkv = dkv.astype(jnp.bfloat16).reshape(kv_heads, 2, tok, head_dim)
    dkv = dkv.transpose(1, 2, 0, 3)
    dq = dq.reshape(kv_heads, tok, fan, head_dim).transpose(1, 0, 2, 3).reshape(tok, heads, head_dim)
    return dq, dkv[0], dkv[1]


def solution(mesh):
    tokens = P(("ctx", "head"), None, None)
    return jax.shard_map(
        per_device,
        mesh=mesh,
        in_specs=(tokens,) * 5 + (P(("ctx", "head"), None), P()),
        out_specs=(tokens,) * 3,
        check_vma=False,
    )
```

```python
import functools

import jax
import jax.numpy as jnp
from jax import lax
from jax.experimental import pallas as pl
from jax.experimental.pallas import tpu as pltpu
from jax.sharding import PartitionSpec as P

BLK = 128
LOG2E = 1.4426950408889634
STAT_ROWS = 32


def stats_of(stats, sources, chunks):
    stats = stats.astype(jnp.float32)
    sums = (
        stats[:, base : base + chunks]
        + stats[:, base + chunks : base + 2 * chunks]
        + stats[:, base + 2 * chunks : base + 3 * chunks]
        for base in (0, 3 * chunks)
    )
    lse, delta = (
        jnp.concatenate([x[s, c : c + 1, :] for s in range(sources) for c in range(chunks)], axis=1)
        for x in sums
    )
    return lse * LOG2E, delta


def block_pair(q, g, lse, delta, k, v, group, scale, masked):
    s = lax.dot_general(k, q, (((1,), (1,)), ((), ())), preferred_element_type=jnp.float32)
    p = jnp.exp2(s * (scale * LOG2E) - lse)
    if masked:
        key_at = lax.broadcasted_iota(jnp.int32, p.shape, 0)
        query_at = lax.broadcasted_iota(jnp.int32, p.shape, 1) // group
        p = jnp.where(query_at >= key_at, p, 0.0)
    dp = lax.dot_general(v, g, (((1,), (1,)), ((), ())), preferred_element_type=jnp.float32)
    ds = (p * (dp - delta)).astype(jnp.bfloat16)
    dv = jnp.dot(p.astype(jnp.bfloat16), g, preferred_element_type=jnp.float32)
    dk = jnp.dot(ds, q, preferred_element_type=jnp.float32)
    dq = lax.dot_general(ds, k, (((0,), (0,)), ((), ())), preferred_element_type=jnp.float32)
    return dq, dk, dv


def whole_kernel(meta, pkg, kv, dq, dkv, dk_acc, dv_acc, dq_acc, *, rows, tok, q_blocks, scale):
    sources = BLK // tok
    wide = sources * rows
    dk_acc[...] = jnp.zeros_like(dk_acc)
    dv_acc[...] = jnp.zeros_like(dv_acc)

    def over_queries(i, _):
        last, first = meta[i], meta[q_blocks + i]
        mine = pl.ds(sources * i, sources)
        q = pkg[mine, 0:rows, :].reshape(wide, 128)
        g = pkg[mine, rows : 2 * rows, :].reshape(wide, 128)
        lse, delta = stats_of(pkg[mine, 2 * rows :, :], sources, rows // 128)
        dq_acc[...] = jnp.zeros_like(dq_acc)

        def step(j, masked):
            k = kv[pl.ds(sources * j, sources), 0].reshape(BLK, 128)
            v = kv[pl.ds(sources * j, sources), 1].reshape(BLK, 128)
            dq_part, dk, dv = block_pair(q, g, lse, delta, k, v, rows // tok, scale, masked)
            at = pl.ds(pl.multiple_of(j * BLK, BLK), BLK)
            dv_acc[at, :] += dv
            dk_acc[at, :] += dk
            dq_acc[...] += dq_part

        def inner(j, _):
            step(j, False)
            return 0

        lax.fori_loop(first, last, inner, 0)
        step(last, True)
        dq[mine] = (dq_acc[...] * scale).astype(jnp.bfloat16).reshape(sources, rows, 128)
        return 0

    lax.fori_loop(0, q_blocks, over_queries, 0)
    shards = dkv.shape[0]
    dkv[:, 0] = (dk_acc[...] * scale).astype(jnp.bfloat16).reshape(shards, tok, 128)
    dkv[:, 1] = dv_acc[...].astype(jnp.bfloat16).reshape(shards, tok, 128)


def planes_kernel(meta, pkg, *refs, rows, tok, q_blocks, scale, distances, planes):
    count = len(distances)
    ends = 0 in distances
    near, refs = refs[:count], refs[count:]
    if ends:
        dq_before, refs = refs[0], refs[1:]
    dq, near_grads, (kv, dk_acc, dv_acc, dq_acc, sems) = refs[0], refs[1 : 1 + count], refs[1 + count :]
    team = pkg.shape[0]
    sources = BLK // tok
    wide = sources * rows
    plane = meta[2 * q_blocks]
    team_blocks = team // 2 // sources
    range_blocks = team_blocks * planes
    loads = [
        pltpu.make_async_copy(near[n], kv.at[n * team : (n + 1) * team], sems.at[n]) for n in range(count)
    ]
    for copy in loads:
        copy.start()
    dk_acc[...] = jnp.zeros_like(dk_acc)
    dv_acc[...] = jnp.zeros_like(dv_acc)
    for copy in loads:
        copy.wait()

    def over_queries(i, _):
        last, first = meta[i], meta[q_blocks + i]
        mine = pl.ds(sources * i, sources)
        q = pkg[mine, 0:rows, :].reshape(wide, 128)
        g = pkg[mine, rows : 2 * rows, :].reshape(wide, 128)
        lse, delta = stats_of(pkg[mine, 2 * rows :, :], sources, rows // 128)
        if ends:
            dq_acc[...] = dq_before[i]
        else:
            dq_acc[...] = jnp.zeros_like(dq_acc)

        def step(j, distance, masked):
            within = (j // range_blocks) * team_blocks + j % team_blocks
            block = (distance - distances[0]) * (2 * team_blocks) + within
            at_shards = pl.ds(sources * block, sources)
            k = kv[at_shards, 0].reshape(BLK, 128)
            v = kv[at_shards, 1].reshape(BLK, 128)
            dq_part, dk, dv = block_pair(q, g, lse, delta, k, v, rows // tok, scale, masked)
            at = pl.ds(pl.multiple_of(block * BLK, BLK), BLK)
            dv_acc[at, :] += dv
            dk_acc[at, :] += dk
            dq_acc[...] += dq_part

        def inner(j, _):
            distance = ((j % range_blocks) // team_blocks) ^ plane

            @pl.when((distance >= distances[0]) & (distance <= distances[-1]))
            def _():
                step(j, distance, False)

            return 0

        lax.fori_loop(first, last, inner, 0)
        if ends:
            step(last, 0, True)
            dq[mine] = (dq_acc[...] * scale).astype(jnp.bfloat16).reshape(sources, rows, 128)
        else:
            dq[i] = dq_acc[...]
        return 0

    lax.fori_loop(0, q_blocks, over_queries, 0)
    for n in range(count):
        at = pl.ds(n * team * tok, team * tok)
        near_grads[n][:, 0] = (dk_acc[at, :] * scale).astype(jnp.bfloat16).reshape(team, tok, 128)
        near_grads[n][:, 1] = dv_acc[at, :].astype(jnp.bfloat16).reshape(team, tok, 128)


VMEM = pl.BlockSpec(memory_space=pltpu.VMEM)
SMEM = pl.BlockSpec(memory_space=pltpu.SMEM)


def totals(shards, tok, wide, head_dim):
    return [
        pltpu.VMEM((shards * tok, head_dim), jnp.float32),
        pltpu.VMEM((shards * tok, head_dim), jnp.float32),
        pltpu.VMEM((wide, head_dim), jnp.float32),
    ]


def attention(meta, pkg, kv, rows, scale):
    shards, _, tok, head_dim = kv.shape
    team = pkg.shape[0]
    q_blocks = team * tok // BLK
    return pl.pallas_call(
        functools.partial(whole_kernel, rows=rows, tok=tok, q_blocks=q_blocks, scale=scale),
        out_shape=(
            jax.ShapeDtypeStruct((team, rows, head_dim), jnp.bfloat16),
            jax.ShapeDtypeStruct(kv.shape, jnp.bfloat16),
        ),
        in_specs=[SMEM, VMEM, VMEM],
        out_specs=(VMEM, VMEM),
        scratch_shapes=totals(shards, tok, rows * (BLK // tok), head_dim),
        compiler_params=pltpu.CompilerParams(vmem_limit_bytes=56 * 1024 * 1024),
        name="attention_grads",
    )(meta, pkg, kv)


def attention_part(meta, pkg, kv, distances, dq_before, rows, scale, planes):
    team, _, tok, head_dim = kv[0].shape
    count = len(distances)
    q_blocks = team * tok // BLK
    wide = rows * (BLK // tok)
    ends = 0 in distances
    if ends:
        dq_shape = jax.ShapeDtypeStruct((team, rows, head_dim), jnp.bfloat16)
    else:
        dq_shape = jax.ShapeDtypeStruct((q_blocks, wide, head_dim), jnp.float32)
    pairs = 2 * q_blocks * count
    dq, *grads = pl.pallas_call(
        functools.partial(
            planes_kernel, rows=rows, tok=tok, q_blocks=q_blocks, scale=scale, distances=distances, planes=planes
        ),
        out_shape=(dq_shape,) + (jax.ShapeDtypeStruct(kv[0].shape, jnp.bfloat16),) * count,
        in_specs=[SMEM, VMEM] + [pl.BlockSpec(memory_space=pl.ANY)] * count + [VMEM] * ends,
        out_specs=(VMEM,) * (1 + count),
        scratch_shapes=[pltpu.VMEM((count * team, 2, tok, head_dim), jnp.bfloat16)]
        + totals(count * team, tok, wide, head_dim)
        + [pltpu.SemaphoreType.DMA((count,))],
        compiler_params=pltpu.CompilerParams(vmem_limit_bytes=32 * 1024 * 1024),
        cost_estimate=pl.CostEstimate(
            flops=pairs * 10 * BLK * wide * head_dim,
            bytes_accessed=4 * 1024 * 1024,
            transcendentals=pairs * BLK * wide,
        ),
        name="attention_part_" + "_".join(str(d) for d in distances),
    )(meta, pkg, *kv, *([dq_before] if ends else []))
    return dq, grads


def pieces(x):
    high = lax.reduce_precision(x, 8, 7)
    rest = x - high
    mid = lax.reduce_precision(rest, 8, 7)
    low = rest - mid
    return [part.astype(jnp.bfloat16) for part in (high, mid, low)]


def add(*terms):
    return sum(x.astype(jnp.float32) for x in terms).astype(jnp.bfloat16)


def exchange(x, slots):
    n_ctx, n_head = lax.axis_size("ctx"), lax.axis_size("head")
    me = (lax.axis_index("ctx") % 2) * slots + lax.axis_index("head") % slots
    order = me ^ jnp.arange(2 * slots)
    x = x[order]
    arrived = [x[0]]
    for d in range(1, 2 * slots):
        db, dr = divmod(d, slots)
        moves = [
            (c * n_head + h, (c ^ db) * n_head + (h ^ dr)) for c in range(n_ctx) for h in range(n_head)
        ]
        arrived.append(lax.ppermute(x[d], ("ctx", "head"), moves))
    return jnp.stack(arrived)[order]


def by_token(dq, dkv, kv_heads, fan):
    _, _, tok, head_dim = dkv.shape
    dq = dq.reshape(kv_heads, tok, fan, head_dim).transpose(1, 0, 2, 3).reshape(tok, kv_heads * fan, head_dim)
    dkv = dkv.transpose(1, 2, 0, 3)
    return dq, dkv[0], dkv[1]


def per_device(queries, keys, values, outputs, out_grads, log_norms, block_doc):
    tok, heads, head_dim = queries.shape
    kv_heads = keys.shape[1]
    fan = heads // kv_heads
    n_ctx, n_head = lax.axis_size("ctx"), lax.axis_size("head")
    slots = kv_heads // 2
    planes = n_head // slots
    rows = tok * fan
    scale = head_dim**-0.5
    ctx, head = lax.axis_index("ctx"), lax.axis_index("head")
    both = ("ctx", "head")
    teams = [
        [(2 * c + b) * n_head + z * slots + r for b in range(2) for r in range(slots)]
        for c in range(n_ctx // 2)
        for z in range(planes)
    ]
    pairs = [
        [(2 * c + b) * n_head + h for b in range(2) for h in range(n_head)]
        for c in range(n_ctx // 2)
    ]

    by_plane = n_ctx == 2 and planes == 4

    def across(x, distance):
        step = distance * slots
        return lax.ppermute(x, "head", [(h, h ^ step) for h in range(n_head)])

    kv = jnp.stack([keys, values], axis=0).transpose(2, 0, 1, 3)
    if by_plane:
        kv = lax.all_to_all(kv, both, 0, 0, axis_index_groups=teams, tiled=True)
        second, first = across(kv, 2), across(kv, 1)
        kv = (kv, first, second, across(second, 1))
    else:
        kv = kv.reshape(2, 1, slots, 2, tok, head_dim)
        kv = jnp.broadcast_to(kv, (2, planes, slots, 2, tok, head_dim))
        kv = kv.reshape(2 * n_head, 2, tok, head_dim)
        kv = lax.all_to_all(kv, both, 0, 0, axis_index_groups=pairs, tiled=True)

    deltas = jnp.sum(out_grads.astype(jnp.float32) * outputs.astype(jnp.float32), axis=-1)
    stats = jnp.stack(pieces(log_norms) + pieces(deltas), axis=0)
    stats = stats.reshape(6, tok, kv_heads, fan).transpose(2, 0, 1, 3)
    stats = stats.reshape(kv_heads, 6 * rows // 128, 128)
    stats = jnp.pad(stats, ((0, 0), (0, STAT_ROWS - stats.shape[1]), (0, 0)))

    def by_group(x):
        return x.reshape(tok, kv_heads, fan, head_dim).transpose(1, 0, 2, 3).reshape(kv_heads, rows, head_dim)

    pkg = jnp.concatenate([by_group(queries), by_group(out_grads), stats], axis=1)
    pkg = lax.all_to_all(pkg, both, 0, 0, axis_index_groups=teams, tiled=True)

    pair, plane = ctx // 2, head // slots
    range_blocks = n_head * tok // BLK
    team_blocks = slots * tok // BLK
    at = jnp.stack(
        [(2 * pair + b) * range_blocks + plane * team_blocks + j for b in range(2) for j in range(team_blocks)]
    )
    first_block = jnp.sum(block_doc[None, :] < block_doc[at][:, None], axis=1, dtype=jnp.int32)
    ranges_before = 1 if n_ctx > 2 else 0
    base = (2 * pair - ranges_before) * range_blocks
    meta = jnp.concatenate([at - base, first_block - base, plane[None]]).astype(jnp.int32)

    if by_plane:
        dq_before, (grads_3,) = attention_part(meta, pkg, kv[3:], (3,), None, rows, scale, planes)
        relayed = across(grads_3, 1)
        dq, (grads_0, grads_1, grads_2) = attention_part(
            meta, pkg, kv[:3], (0, 1, 2), dq_before, rows, scale, planes
        )
        close = across(grads_1, 1)
        far = across(add(grads_2, relayed), 2)
        dq = lax.all_to_all(dq, both, 0, 0, axis_index_groups=teams, tiled=True)
        dkv = exchange(add(grads_0, close, far), slots)
        return by_token(dq, dkv, kv_heads, fan)

    if ranges_before:
        prior = lax.ppermute(kv[n_head:], "ctx", [(c, c + 2) for c in range(n_ctx - 2)])
        kv = jnp.concatenate([prior, kv], axis=0)
    dq, dkv = attention(meta, pkg, kv, rows, scale)
    if ranges_before:
        later = lax.ppermute(dkv[:n_head], "ctx", [(c + 2, c) for c in range(n_ctx - 2)])
        dkv = jnp.concatenate([dkv[n_head : 2 * n_head], add(dkv[2 * n_head :], later)], axis=0)

    dkv = lax.all_to_all(dkv, both, 0, 0, axis_index_groups=pairs, tiled=True)
    dq = lax.all_to_all(dq, both, 0, 0, axis_index_groups=teams, tiled=True)
    dkv = dkv.reshape(2, planes, slots, 2, tok, head_dim).astype(jnp.float32).sum(axis=1)
    dkv = dkv.astype(jnp.bfloat16).reshape(kv_heads, 2, tok, head_dim)
    return by_token(dq, dkv, kv_heads, fan)


def solution(mesh):
    tokens = P(("ctx", "head"), None, None)
    return jax.shard_map(
        per_device,
        mesh=mesh,
        in_specs=(tokens,) * 5 + (P(("ctx", "head"), None), P()),
        out_specs=(tokens,) * 3,
        check_vma=False,
    )
```

```python
import functools

import jax
import jax.numpy as jnp
from jax import lax
from jax.experimental import pallas as pl
from jax.experimental.pallas import tpu as pltpu
from jax.sharding import PartitionSpec as P

BLK = 128
LOG2E = 1.4426950408889634
STAT_ROWS = 32


def stats_of(stats, sources, chunks):
    stats = stats.astype(jnp.float32)
    sums = (
        stats[:, base : base + chunks]
        + stats[:, base + chunks : base + 2 * chunks]
        + stats[:, base + 2 * chunks : base + 3 * chunks]
        for base in (0, 3 * chunks)
    )
    lse, delta = (
        jnp.concatenate([x[s, c : c + 1, :] for s in range(sources) for c in range(chunks)], axis=1)
        for x in sums
    )
    return lse * LOG2E, delta


def block_pair(q, g, lse, delta, k, v, group, scale, masked):
    s = lax.dot_general(k, q, (((1,), (1,)), ((), ())), preferred_element_type=jnp.float32)
    p = jnp.exp2(s * (scale * LOG2E) - lse)
    if masked:
        key_at = lax.broadcasted_iota(jnp.int32, p.shape, 0)
        query_at = lax.broadcasted_iota(jnp.int32, p.shape, 1) // group
        p = jnp.where(query_at >= key_at, p, 0.0)
    dp = lax.dot_general(v, g, (((1,), (1,)), ((), ())), preferred_element_type=jnp.float32)
    ds = (p * (dp - delta)).astype(jnp.bfloat16)
    dv = jnp.dot(p.astype(jnp.bfloat16), g, preferred_element_type=jnp.float32)
    dk = jnp.dot(ds, q, preferred_element_type=jnp.float32)
    dq = lax.dot_general(ds, k, (((0,), (0,)), ((), ())), preferred_element_type=jnp.float32)
    return dq, dk, dv


def whole_kernel(meta, pkg, kv, dq, dkv, dk_acc, dv_acc, dq_acc, *, rows, tok, q_blocks, scale):
    sources = BLK // tok
    wide = sources * rows
    dk_acc[...] = jnp.zeros_like(dk_acc)
    dv_acc[...] = jnp.zeros_like(dv_acc)

    def over_queries(i, _):
        last, first = meta[i], meta[q_blocks + i]
        mine = pl.ds(sources * i, sources)
        q = pkg[mine, 0:rows, :].reshape(wide, 128)
        g = pkg[mine, rows : 2 * rows, :].reshape(wide, 128)
        lse, delta = stats_of(pkg[mine, 2 * rows :, :], sources, rows // 128)
        dq_acc[...] = jnp.zeros_like(dq_acc)

        def step(j, masked):
            k = kv[pl.ds(sources * j, sources), 0].reshape(BLK, 128)
            v = kv[pl.ds(sources * j, sources), 1].reshape(BLK, 128)
            dq_part, dk, dv = block_pair(q, g, lse, delta, k, v, rows // tok, scale, masked)
            at = pl.ds(pl.multiple_of(j * BLK, BLK), BLK)
            dv_acc[at, :] += dv
            dk_acc[at, :] += dk
            dq_acc[...] += dq_part

        def inner(j, _):
            step(j, False)
            return 0

        lax.fori_loop(first, last, inner, 0)
        step(last, True)
        dq[mine] = (dq_acc[...] * scale).astype(jnp.bfloat16).reshape(sources, rows, 128)
        return 0

    lax.fori_loop(0, q_blocks, over_queries, 0)
    shards = dkv.shape[0]
    dkv[:, 0] = (dk_acc[...] * scale).astype(jnp.bfloat16).reshape(shards, tok, 128)
    dkv[:, 1] = dv_acc[...].astype(jnp.bfloat16).reshape(shards, tok, 128)


def planes_kernel(meta, pkg, *refs, rows, tok, q_blocks, scale, odd, planes):
    halves = planes // 2
    team = pkg.shape[0]
    near, refs = refs[:halves], refs[halves:]
    if odd:
        dq, grads, kv, dk_acc, dv_acc, dq_acc, sems = refs
    else:
        dq_before, refs = refs[0], refs[1:]
        dq_out, (grads, kv, dk_acc, dv_acc, dq_acc, sems, dq, dq_sems) = refs[:team], refs[team:]
    sources = BLK // tok
    wide = sources * rows
    plane, place = meta[2 * q_blocks], meta[2 * q_blocks + 1]
    team_blocks = team // 2 // sources
    range_blocks = team_blocks * planes
    loads = [
        pltpu.make_async_copy(near[n], kv.at[pl.ds(((plane // 2) ^ n) * team, team)], sems.at[n])
        for n in range(halves)
    ]
    for copy in loads:
        copy.start()
    dk_acc[...] = jnp.zeros_like(dk_acc)
    dv_acc[...] = jnp.zeros_like(dv_acc)
    for copy in loads:
        copy.wait()

    def over_queries(i, _):
        last, first = meta[i], meta[q_blocks + i]
        mine = pl.ds(sources * i, sources)
        q = pkg[mine, 0:rows, :].reshape(wide, 128)
        g = pkg[mine, rows : 2 * rows, :].reshape(wide, 128)
        lse, delta = stats_of(pkg[mine, 2 * rows :, :], sources, rows // 128)
        if odd:
            dq_acc[...] = jnp.zeros_like(dq_acc)
        else:
            dq_acc[...] = dq_before[i]

        def step(j, half, masked):
            within = (j // range_blocks) * team_blocks + j % team_blocks
            block = half * (2 * team_blocks) + within
            at_shards = pl.ds(sources * block, sources)
            k = kv[at_shards, 0].reshape(BLK, 128)
            v = kv[at_shards, 1].reshape(BLK, 128)
            dq_part, dk, dv = block_pair(q, g, lse, delta, k, v, rows // tok, scale, masked)
            at = pl.ds(pl.multiple_of(block * BLK, BLK), BLK)
            dv_acc[at, :] += dv
            dk_acc[at, :] += dk
            dq_acc[...] += dq_part

        def inner(j, _):
            key_plane = (j % range_blocks) // team_blocks

            @pl.when((key_plane ^ plane) & 1 == odd)
            def _():
                step(j, key_plane // 2, False)

            return 0

        lax.fori_loop(first, last, inner, 0)
        if odd:
            dq[i] = dq_acc[...]
        else:
            step(last, plane // 2, True)
            dq[mine] = (dq_acc[...] * scale).astype(jnp.bfloat16).reshape(sources, rows, 128)
        return 0

    lax.fori_loop(0, q_blocks, over_queries, 0)
    if not odd:
        stores = [pltpu.make_async_copy(dq.at[place ^ d], dq_out[d], dq_sems.at[d]) for d in range(team)]
        for copy in stores:
            copy.start()
    for half in range(halves):
        at = pl.ds(half * team * tok, team * tok)
        grads[half, :, 0] = (dk_acc[at, :] * scale).astype(jnp.bfloat16).reshape(team, tok, 128)
        grads[half, :, 1] = dv_acc[at, :].astype(jnp.bfloat16).reshape(team, tok, 128)
    if not odd:
        for copy in stores:
            copy.wait()


VMEM = pl.BlockSpec(memory_space=pltpu.VMEM)
SMEM = pl.BlockSpec(memory_space=pltpu.SMEM)


def totals(shards, tok, wide, head_dim):
    return [
        pltpu.VMEM((shards * tok, head_dim), jnp.float32),
        pltpu.VMEM((shards * tok, head_dim), jnp.float32),
        pltpu.VMEM((wide, head_dim), jnp.float32),
    ]


def attention(meta, pkg, kv, rows, scale):
    shards, _, tok, head_dim = kv.shape
    team = pkg.shape[0]
    q_blocks = team * tok // BLK
    return pl.pallas_call(
        functools.partial(whole_kernel, rows=rows, tok=tok, q_blocks=q_blocks, scale=scale),
        out_shape=(
            jax.ShapeDtypeStruct((team, rows, head_dim), jnp.bfloat16),
            jax.ShapeDtypeStruct(kv.shape, jnp.bfloat16),
        ),
        in_specs=[SMEM, VMEM, VMEM],
        out_specs=(VMEM, VMEM),
        scratch_shapes=totals(shards, tok, rows * (BLK // tok), head_dim),
        compiler_params=pltpu.CompilerParams(vmem_limit_bytes=56 * 1024 * 1024),
        name="attention_grads",
    )(meta, pkg, kv)


def attention_part(meta, pkg, kv, dq_before, rows, scale, planes):
    team, _, tok, head_dim = kv[0].shape
    halves = planes // 2
    q_blocks = team * tok // BLK
    wide = rows * (BLK // tok)
    odd = dq_before is None
    if odd:
        dq_shapes = (jax.ShapeDtypeStruct((q_blocks, wide, head_dim), jnp.float32),)
    else:
        dq_shapes = (jax.ShapeDtypeStruct((rows, head_dim), jnp.bfloat16),) * team
    pairs = 2 * q_blocks * halves
    anywhere = pl.BlockSpec(memory_space=pl.ANY)
    *dq, grads = pl.pallas_call(
        functools.partial(
            planes_kernel, rows=rows, tok=tok, q_blocks=q_blocks, scale=scale, odd=int(odd), planes=planes
        ),
        out_shape=dq_shapes + (jax.ShapeDtypeStruct((halves,) + kv[0].shape, jnp.bfloat16),),
        in_specs=[SMEM, VMEM] + [anywhere] * halves + ([] if odd else [VMEM]),
        out_specs=((VMEM,) if odd else (anywhere,) * team) + (VMEM,),
        scratch_shapes=[pltpu.VMEM((halves * team, 2, tok, head_dim), jnp.bfloat16)]
        + totals(halves * team, tok, wide, head_dim)
        + [pltpu.SemaphoreType.DMA((halves,))]
        + ([] if odd else [pltpu.VMEM((team, rows, head_dim), jnp.bfloat16), pltpu.SemaphoreType.DMA((team,))]),
        compiler_params=pltpu.CompilerParams(vmem_limit_bytes=32 * 1024 * 1024),
        cost_estimate=pl.CostEstimate(
            flops=pairs * 10 * BLK * wide * head_dim,
            bytes_accessed=4 * 1024 * 1024,
            transcendentals=pairs * BLK * wide,
        ),
        name="attention_odd" if odd else "attention_even",
    )(meta, pkg, *kv, *([] if odd else [dq_before]))
    return (dq[0] if odd else dq), grads


def place_kernel(place, *refs):
    *arrived, out = refs
    for d, block in enumerate(arrived):
        out[:, place[0] ^ d] = block[...]


def place_blocks(place, arrived, tok):
    rows, head_dim = arrived[0].shape
    fan = rows // tok
    out = pl.pallas_call(
        place_kernel,
        out_shape=jax.ShapeDtypeStruct((tok, len(arrived), fan, head_dim), jnp.bfloat16),
        in_specs=[SMEM] + [VMEM] * len(arrived),
        out_specs=VMEM,
        name="place_dq",
    )(place, *[x.reshape(tok, fan, head_dim) for x in arrived])
    return out.reshape(tok, len(arrived) * fan, head_dim)


def pieces(x):
    high = lax.reduce_precision(x, 8, 7)
    rest = x - high
    mid = lax.reduce_precision(rest, 8, 7)
    low = rest - mid
    return [part.astype(jnp.bfloat16) for part in (high, mid, low)]


def add(*terms):
    return sum(x.astype(jnp.float32) for x in terms).astype(jnp.bfloat16)


def exchange(blocks, slots):
    n_ctx, n_head = lax.axis_size("ctx"), lax.axis_size("head")
    arrived = [blocks[0]]
    for d in range(1, 2 * slots):
        db, dr = divmod(d, slots)
        moves = [
            (c * n_head + h, (c ^ db) * n_head + (h ^ dr)) for c in range(n_ctx) for h in range(n_head)
        ]
        arrived.append(lax.ppermute(blocks[d], ("ctx", "head"), moves))
    return arrived


def dq_by_token(dq, tok, fan):
    kv_heads, _, head_dim = dq.shape
    return dq.reshape(kv_heads, tok, fan, head_dim).transpose(1, 0, 2, 3).reshape(tok, kv_heads * fan, head_dim)


def dkv_by_token(parts):
    dkv = parts.astype(jnp.float32).sum(axis=0).astype(jnp.bfloat16).transpose(1, 2, 0, 3)
    return dkv[0], dkv[1]


def per_device(queries, keys, values, outputs, out_grads, log_norms, block_doc):
    tok, heads, head_dim = queries.shape
    kv_heads = keys.shape[1]
    fan = heads // kv_heads
    n_ctx, n_head = lax.axis_size("ctx"), lax.axis_size("head")
    slots = kv_heads // 2
    planes = n_head // slots
    rows = tok * fan
    scale = head_dim**-0.5
    ctx, head = lax.axis_index("ctx"), lax.axis_index("head")
    both = ("ctx", "head")
    teams = [
        [(2 * c + b) * n_head + z * slots + r for b in range(2) for r in range(slots)]
        for c in range(n_ctx // 2)
        for z in range(planes)
    ]
    pairs = [
        [(2 * c + b) * n_head + h for b in range(2) for h in range(n_head)]
        for c in range(n_ctx // 2)
    ]

    by_plane = n_ctx == 2 and planes == 4

    def across(x, distance):
        step = distance * slots
        return lax.ppermute(x, "head", [(h, h ^ step) for h in range(n_head)])

    alternate = [
        [
            (2 * c + b) * n_head + z * slots + r
            for z in range(parity, planes, 2)
            for b in range(2)
            for r in range(slots)
        ]
        for c in range(n_ctx // 2)
        for parity in range(2)
    ]

    kv = jnp.stack([keys, values], axis=0).transpose(2, 0, 1, 3)
    if by_plane:
        kv = lax.all_to_all(kv, both, 0, 0, axis_index_groups=teams, tiled=True)
        second, first = across(kv, 2), across(kv, 1)
        kv = (kv, first, second, across(second, 1))
    else:
        kv = kv.reshape(2, 1, slots, 2, tok, head_dim)
        kv = jnp.broadcast_to(kv, (2, planes, slots, 2, tok, head_dim))
        kv = kv.reshape(2 * n_head, 2, tok, head_dim)
        kv = lax.all_to_all(kv, both, 0, 0, axis_index_groups=pairs, tiled=True)

    deltas = jnp.sum(out_grads.astype(jnp.float32) * outputs.astype(jnp.float32), axis=-1)
    stats = jnp.stack(pieces(log_norms) + pieces(deltas), axis=0)
    stats = stats.reshape(6, tok, kv_heads, fan).transpose(2, 0, 1, 3)
    stats = stats.reshape(kv_heads, 6 * rows // 128, 128)
    stats = jnp.pad(stats, ((0, 0), (0, STAT_ROWS - stats.shape[1]), (0, 0)))

    def by_group(x):
        return x.reshape(tok, kv_heads, fan, head_dim).transpose(1, 0, 2, 3).reshape(kv_heads, rows, head_dim)

    pkg = jnp.concatenate([by_group(queries), by_group(out_grads), stats], axis=1)
    pkg = lax.all_to_all(pkg, both, 0, 0, axis_index_groups=teams, tiled=True)

    pair, plane = ctx // 2, head // slots
    range_blocks = n_head * tok // BLK
    team_blocks = slots * tok // BLK
    at = jnp.stack(
        [(2 * pair + b) * range_blocks + plane * team_blocks + j for b in range(2) for j in range(team_blocks)]
    )
    first_block = jnp.sum(block_doc[None, :] < block_doc[at][:, None], axis=1, dtype=jnp.int32)
    ranges_before = 1 if n_ctx > 2 else 0
    base = (2 * pair - ranges_before) * range_blocks
    place = (ctx % 2) * slots + head % slots
    meta = jnp.concatenate([at - base, first_block - base, plane[None], place[None]]).astype(jnp.int32)

    if by_plane:
        dq_before, odd_grads = attention_part(meta, pkg, (kv[1], kv[3]), None, rows, scale, planes)
        arrived = across(odd_grads, 1)
        dq, even_grads = attention_part(meta, pkg, (kv[0], kv[2]), dq_before, rows, scale, planes)
        dkv = add(arrived, even_grads).reshape(planes // 2 * kv_heads, 2, tok, head_dim)
        dkv = lax.all_to_all(dkv, both, 0, 0, axis_index_groups=alternate, tiled=True)
        dq = place_blocks(place[None], exchange(dq, slots), tok)
        return (dq,) + dkv_by_token(dkv.reshape(planes // 2, kv_heads, 2, tok, head_dim))

    if ranges_before:
        prior = lax.ppermute(kv[n_head:], "ctx", [(c, c + 2) for c in range(n_ctx - 2)])
        kv = jnp.concatenate([prior, kv], axis=0)
    dq, dkv = attention(meta, pkg, kv, rows, scale)
    if ranges_before:
        later = lax.ppermute(dkv[:n_head], "ctx", [(c + 2, c) for c in range(n_ctx - 2)])
        dkv = jnp.concatenate([dkv[n_head : 2 * n_head], add(dkv[2 * n_head :], later)], axis=0)

    dkv = lax.all_to_all(dkv, both, 0, 0, axis_index_groups=pairs, tiled=True)
    dq = lax.all_to_all(dq, both, 0, 0, axis_index_groups=teams, tiled=True)
    dkv = dkv.reshape(2, planes, slots, 2, tok, head_dim).transpose(1, 0, 2, 3, 4, 5)
    return (dq_by_token(dq, tok, fan),) + dkv_by_token(dkv.reshape(planes, kv_heads, 2, tok, head_dim))


def solution(mesh):
    tokens = P(("ctx", "head"), None, None)
    return jax.shard_map(
        per_device,
        mesh=mesh,
        in_specs=(tokens,) * 5 + (P(("ctx", "head"), None), P()),
        out_specs=(tokens,) * 3,
        check_vma=False,
    )
```

```python
import functools

import jax
import jax.numpy as jnp
from jax import lax
from jax.experimental import pallas as pl
from jax.experimental.pallas import tpu as pltpu
from jax.sharding import PartitionSpec as P

BLK = 128
LOG2E = 1.4426950408889634
STAT_ROWS = 32
LIMIT = 56 * 1024 * 1024
PART_LIMIT = 24 * 1024 * 1024
SMALL_LIMIT = 6 * 1024 * 1024


def stats_of(stats, sources, chunks):
    stats = stats.astype(jnp.float32)
    sums = (
        stats[:, base : base + chunks]
        + stats[:, base + chunks : base + 2 * chunks]
        + stats[:, base + 2 * chunks : base + 3 * chunks]
        for base in (0, 3 * chunks)
    )
    lse, delta = (
        jnp.concatenate([x[s, c : c + 1, :] for s in range(sources) for c in range(chunks)], axis=1)
        for x in sums
    )
    return lse * LOG2E, delta


def block_pair(q, g, lse, delta, k, v, group, scale, masked):
    s = lax.dot_general(k, q, (((1,), (1,)), ((), ())), preferred_element_type=jnp.float32)
    p = jnp.exp2(s * (scale * LOG2E) - lse)
    if masked:
        key_at = lax.broadcasted_iota(jnp.int32, p.shape, 0)
        query_at = lax.broadcasted_iota(jnp.int32, p.shape, 1) // group
        p = jnp.where(query_at >= key_at, p, 0.0)
    dp = lax.dot_general(v, g, (((1,), (1,)), ((), ())), preferred_element_type=jnp.float32)
    ds = (p * (dp - delta)).astype(jnp.bfloat16)
    dv = jnp.dot(p.astype(jnp.bfloat16), g, preferred_element_type=jnp.float32)
    dk = jnp.dot(ds, q, preferred_element_type=jnp.float32)
    dq = lax.dot_general(ds, k, (((0,), (0,)), ((), ())), preferred_element_type=jnp.float32)
    return dq, dk, dv


def whole_kernel(meta, pkg, kv, dq, dkv, dk_acc, dv_acc, dq_acc, *, rows, tok, q_blocks, scale):
    sources = BLK // tok
    wide = sources * rows
    dk_acc[...] = jnp.zeros_like(dk_acc)
    dv_acc[...] = jnp.zeros_like(dv_acc)

    def over_queries(i, _):
        last, first = meta[i], meta[q_blocks + i]
        mine = pl.ds(sources * i, sources)
        q = pkg[mine, 0:rows, :].reshape(wide, 128)
        g = pkg[mine, rows : 2 * rows, :].reshape(wide, 128)
        lse, delta = stats_of(pkg[mine, 2 * rows :, :], sources, rows // 128)
        dq_acc[...] = jnp.zeros_like(dq_acc)

        def step(j, masked):
            k = kv[pl.ds(sources * j, sources), 0].reshape(BLK, 128)
            v = kv[pl.ds(sources * j, sources), 1].reshape(BLK, 128)
            dq_part, dk, dv = block_pair(q, g, lse, delta, k, v, rows // tok, scale, masked)
            at = pl.ds(pl.multiple_of(j * BLK, BLK), BLK)
            dv_acc[at, :] += dv
            dk_acc[at, :] += dk
            dq_acc[...] += dq_part

        def inner(j, _):
            step(j, False)
            return 0

        lax.fori_loop(first, last, inner, 0)
        step(last, True)
        dq[mine] = (dq_acc[...] * scale).astype(jnp.bfloat16).reshape(sources, rows, 128)
        return 0

    lax.fori_loop(0, q_blocks, over_queries, 0)
    shards = dkv.shape[0]
    dkv[:, 0] = (dk_acc[...] * scale).astype(jnp.bfloat16).reshape(shards, tok, 128)
    dkv[:, 1] = dv_acc[...].astype(jnp.bfloat16).reshape(shards, tok, 128)


def planes_kernel(meta, pkg, kv, *refs, rows, tok, q_blocks, scale, odd, planes):
    halves = planes // 2
    team = pkg.shape[0]
    if odd:
        dq, grads, dk_acc, dv_acc, dq_acc = refs
    else:
        dq_before, refs = refs[0], refs[1:]
        dq_out, (grads, dk_acc, dv_acc, dq_acc, dq, out_sems) = refs[:team], refs[team:]
    sources = BLK // tok
    wide = sources * rows
    plane, place = meta[2 * q_blocks], meta[2 * q_blocks + 1]
    team_blocks = team // 2 // sources
    range_blocks = team_blocks * planes
    dk_acc[...] = jnp.zeros_like(dk_acc)
    dv_acc[...] = jnp.zeros_like(dv_acc)

    def over_queries(i, _):
        last, first = meta[i], meta[q_blocks + i]
        mine = pl.ds(sources * i, sources)
        q = pkg[mine, 0:rows, :].reshape(wide, 128)
        g = pkg[mine, rows : 2 * rows, :].reshape(wide, 128)
        lse, delta = stats_of(pkg[mine, 2 * rows :, :], sources, rows // 128)
        if odd:
            dq_acc[...] = jnp.zeros_like(dq_acc)
        else:
            dq_acc[...] = dq_before[i]

        def step(j, half, masked):
            within = lax.div(j, range_blocks) * team_blocks + lax.rem(j, team_blocks)
            block = half * (2 * team_blocks) + within
            at_shards = pl.ds(sources * block, sources)
            k = kv[at_shards, 0].reshape(BLK, 128)
            v = kv[at_shards, 1].reshape(BLK, 128)
            dq_part, dk, dv = block_pair(q, g, lse, delta, k, v, rows // tok, scale, masked)
            at = pl.ds(pl.multiple_of(block * BLK, BLK), BLK)
            dv_acc[at, :] += dv
            dk_acc[at, :] += dk
            dq_acc[...] += dq_part

        def inner(j, _):
            key_plane = lax.div(lax.rem(j, range_blocks), team_blocks)

            @pl.when((key_plane ^ plane) & 1 == odd)
            def _():
                step(j, key_plane // 2, False)

            return 0

        lax.fori_loop(first, last, inner, 0)
        if odd:
            dq[i] = dq_acc[...]
        else:
            step(last, plane // 2, True)
            dq[mine] = (dq_acc[...] * scale).astype(jnp.bfloat16).reshape(sources, rows, 128)
        return 0

    lax.fori_loop(0, q_blocks, over_queries, 0)
    if not odd:
        stores = [pltpu.make_async_copy(dq.at[place ^ d], dq_out[d], out_sems.at[d]) for d in range(team)]
        for copy in stores:
            copy.start()
    for half in range(halves):
        at = pl.ds(half * team * tok, team * tok)
        grads[half, :, 0] = (dk_acc[at, :] * scale).astype(jnp.bfloat16).reshape(team, tok, 128)
        grads[half, :, 1] = dv_acc[at, :].astype(jnp.bfloat16).reshape(team, tok, 128)
    if not odd:
        for copy in stores:
            copy.wait()


VMEM = pl.BlockSpec(memory_space=pltpu.VMEM)
SMEM = pl.BlockSpec(memory_space=pltpu.SMEM)


def totals(shards, tok, wide, head_dim):
    return [
        pltpu.VMEM((shards * tok, head_dim), jnp.float32),
        pltpu.VMEM((shards * tok, head_dim), jnp.float32),
        pltpu.VMEM((wide, head_dim), jnp.float32),
    ]


def attention(meta, pkg, kv, rows, scale):
    shards, _, tok, head_dim = kv.shape
    team = pkg.shape[0]
    q_blocks = team * tok // BLK
    return pl.pallas_call(
        functools.partial(whole_kernel, rows=rows, tok=tok, q_blocks=q_blocks, scale=scale),
        out_shape=(
            jax.ShapeDtypeStruct((team, rows, head_dim), jnp.bfloat16),
            jax.ShapeDtypeStruct(kv.shape, jnp.bfloat16),
        ),
        in_specs=[SMEM, VMEM, VMEM],
        out_specs=(VMEM, VMEM),
        scratch_shapes=totals(shards, tok, rows * (BLK // tok), head_dim),
        compiler_params=pltpu.CompilerParams(vmem_limit_bytes=LIMIT),
        name="attention_grads",
    )(meta, pkg, kv)


def attention_part(meta, pkg, kv, dq_before, rows, scale, planes):
    shards, _, tok, head_dim = kv.shape
    team = pkg.shape[0]
    halves = planes // 2
    q_blocks = team * tok // BLK
    wide = rows * (BLK // tok)
    odd = dq_before is None
    if odd:
        dq_shapes = (jax.ShapeDtypeStruct((q_blocks, wide, head_dim), jnp.float32),)
    else:
        dq_shapes = (jax.ShapeDtypeStruct((rows, head_dim), jnp.bfloat16),) * team
    pairs = 2 * q_blocks * halves
    *dq, grads = pl.pallas_call(
        functools.partial(
            planes_kernel, rows=rows, tok=tok, q_blocks=q_blocks, scale=scale, odd=int(odd), planes=planes
        ),
        out_shape=dq_shapes + (jax.ShapeDtypeStruct((halves, team, 2, tok, head_dim), jnp.bfloat16),),
        in_specs=[SMEM] + [VMEM] * (2 + (not odd)),
        out_specs=((VMEM,) if odd else (pl.BlockSpec(memory_space=pl.ANY),) * team) + (VMEM,),
        scratch_shapes=totals(shards, tok, wide, head_dim)
        + (
            []
            if odd
            else [pltpu.VMEM((team, rows, head_dim), jnp.bfloat16), pltpu.SemaphoreType.DMA((team,))]
        ),
        compiler_params=pltpu.CompilerParams(vmem_limit_bytes=PART_LIMIT),
        cost_estimate=pl.CostEstimate(
            flops=pairs * 10 * BLK * wide * head_dim,
            bytes_accessed=4 * 1024 * 1024,
            transcendentals=pairs * BLK * wide,
        ),
        name="attention_odd" if odd else "attention_even",
    )(meta, pkg, kv, *([] if odd else [dq_before]))
    return (dq[0] if odd else dq), grads


def place_dq_kernel(place, *refs):
    *arrived, out = refs
    for d, block in enumerate(arrived):
        out[:, place[0] ^ d] = block[...]


def place_dq(place, arrived, tok):
    rows, head_dim = arrived[0].shape
    fan = rows // tok
    out = pl.pallas_call(
        place_dq_kernel,
        out_shape=jax.ShapeDtypeStruct((tok, len(arrived), fan, head_dim), jnp.bfloat16),
        in_specs=[SMEM] + [VMEM] * len(arrived),
        out_specs=VMEM,
        compiler_params=pltpu.CompilerParams(vmem_limit_bytes=SMALL_LIMIT),
        name="place_dq",
    )(place, *[x.reshape(tok, fan, head_dim) for x in arrived])
    return out.reshape(tok, len(arrived) * fan, head_dim)


def place_dkv_kernel(parts, dk, dv, wide):
    halves, kv_heads = parts.shape[:2]
    for n, out in enumerate((dk, dv)):
        for h in range(kv_heads):
            wide[:, h, :] = sum(parts[p, h, n].astype(jnp.float32) for p in range(halves))
        out[...] = wide[...].astype(jnp.bfloat16)


def place_dkv(parts):
    _, kv_heads, _, tok, head_dim = parts.shape
    shape = (tok, kv_heads, head_dim)
    return pl.pallas_call(
        place_dkv_kernel,
        out_shape=(jax.ShapeDtypeStruct(shape, jnp.bfloat16),) * 2,
        in_specs=[VMEM],
        out_specs=(VMEM, VMEM),
        scratch_shapes=[pltpu.VMEM(shape, jnp.float32)],
        compiler_params=pltpu.CompilerParams(vmem_limit_bytes=SMALL_LIMIT),
        name="place_dkv",
    )(parts)


def pieces(x):
    high = lax.reduce_precision(x, 8, 7)
    rest = x - high
    mid = lax.reduce_precision(rest, 8, 7)
    low = rest - mid
    return [part.astype(jnp.bfloat16) for part in (high, mid, low)]


def add(*terms):
    return sum(x.astype(jnp.float32) for x in terms).astype(jnp.bfloat16)


def to_member(block, d, slots):
    n_ctx, n_head = lax.axis_size("ctx"), lax.axis_size("head")
    db, dr = divmod(d, slots)
    moves = [(c * n_head + h, (c ^ db) * n_head + (h ^ dr)) for c in range(n_ctx) for h in range(n_head)]
    return lax.ppermute(block, ("ctx", "head"), moves)


def dq_by_token(dq, tok, fan):
    kv_heads, _, head_dim = dq.shape
    return dq.reshape(kv_heads, tok, fan, head_dim).transpose(1, 0, 2, 3).reshape(tok, kv_heads * fan, head_dim)


def dkv_by_token(parts):
    dkv = parts.astype(jnp.float32).sum(axis=0).astype(jnp.bfloat16).transpose(1, 2, 0, 3)
    return dkv[0], dkv[1]


def per_device(queries, keys, values, outputs, out_grads, log_norms, block_doc):
    tok, heads, head_dim = queries.shape
    kv_heads = keys.shape[1]
    fan = heads // kv_heads
    n_ctx, n_head = lax.axis_size("ctx"), lax.axis_size("head")
    slots = kv_heads // 2
    planes = n_head // slots
    rows = tok * fan
    scale = head_dim**-0.5
    ctx, head = lax.axis_index("ctx"), lax.axis_index("head")
    both = ("ctx", "head")
    teams = [
        [(2 * c + b) * n_head + z * slots + r for b in range(2) for r in range(slots)]
        for c in range(n_ctx // 2)
        for z in range(planes)
    ]
    pairs = [
        [(2 * c + b) * n_head + h for b in range(2) for h in range(n_head)]
        for c in range(n_ctx // 2)
    ]

    by_plane = n_ctx == 2 and planes == 4

    def across(x, distance):
        step = distance * slots
        return lax.ppermute(x, "head", [(h, h ^ step) for h in range(n_head)])

    alternate = [
        [
            (2 * c + b) * n_head + z * slots + r
            for z in range(parity, planes, 2)
            for b in range(2)
            for r in range(slots)
        ]
        for c in range(n_ctx // 2)
        for parity in range(2)
    ]

    kv = jnp.stack([keys, values], axis=0).transpose(2, 0, 1, 3)
    if by_plane:
        kv = lax.all_to_all(kv, both, 0, 0, axis_index_groups=teams, tiled=True)
        second, first = across(kv, 2), across(kv, 1)
        kv = (kv, first, second, across(second, 1))
    else:
        kv = kv.reshape(2, 1, slots, 2, tok, head_dim)
        kv = jnp.broadcast_to(kv, (2, planes, slots, 2, tok, head_dim))
        kv = kv.reshape(2 * n_head, 2, tok, head_dim)
        kv = lax.all_to_all(kv, both, 0, 0, axis_index_groups=pairs, tiled=True)

    def by_group(x):
        return x.reshape(tok, kv_heads, fan, head_dim).transpose(1, 0, 2, 3).reshape(kv_heads, rows, head_dim)

    deltas = jnp.sum(out_grads.astype(jnp.float32) * outputs.astype(jnp.float32), axis=-1)
    stats = jnp.stack(pieces(log_norms) + pieces(deltas), axis=0)
    stats = stats.reshape(6, tok, kv_heads, fan).transpose(2, 0, 1, 3)
    stats = stats.reshape(kv_heads, 6 * rows // 128, 128)
    stats = jnp.pad(stats, ((0, 0), (0, STAT_ROWS - stats.shape[1]), (0, 0)))
    pkg = jnp.concatenate([by_group(queries), by_group(out_grads), stats], axis=1)
    pkg = lax.all_to_all(pkg, both, 0, 0, axis_index_groups=teams, tiled=True)

    pair, plane = lax.div(ctx, 2), lax.div(head, slots)
    range_blocks = n_head * tok // BLK
    team_blocks = slots * tok // BLK
    at = jnp.stack(
        [(2 * pair + b) * range_blocks + plane * team_blocks + j for b in range(2) for j in range(team_blocks)]
    )
    first_block = jnp.sum(block_doc[None, :] < block_doc[at][:, None], axis=1, dtype=jnp.int32)
    ranges_before = 1 if n_ctx > 2 else 0
    base = (2 * pair - ranges_before) * range_blocks
    place = lax.rem(ctx, 2) * slots + lax.rem(head, slots)
    meta = jnp.concatenate([at - base, first_block - base, plane[None], place[None]]).astype(jnp.int32)

    if by_plane:
        upper = plane // 2 == 1

        def in_order(near, far):
            return jnp.where(upper, jnp.concatenate([far, near]), jnp.concatenate([near, far]))

        dq_before, odd_grads = attention_part(meta, pkg, in_order(kv[1], kv[3]), None, rows, scale, planes)
        arrived = across(odd_grads, 1)
        dq, even_grads = attention_part(meta, pkg, in_order(kv[0], kv[2]), dq_before, rows, scale, planes)
        dkv = add(arrived, even_grads).reshape(planes // 2 * kv_heads, 2, tok, head_dim)
        dkv = lax.all_to_all(dkv, both, 0, 0, axis_index_groups=alternate, tiled=True)
        dq = [dq[0]] + [to_member(dq[d], d, slots) for d in range(1, kv_heads)]
        dk, dv = place_dkv(dkv.reshape(planes // 2, kv_heads, 2, tok, head_dim))
        dk, dv, *dq = lax.optimization_barrier((dk, dv, *dq))
        return place_dq(place[None], dq, tok), dk, dv

    if ranges_before:
        prior = lax.ppermute(kv[n_head:], "ctx", [(c, c + 2) for c in range(n_ctx - 2)])
        kv = jnp.concatenate([prior, kv], axis=0)
    dq, dkv = attention(meta, pkg, kv, rows, scale)
    if ranges_before:
        later = lax.ppermute(dkv[:n_head], "ctx", [(c + 2, c) for c in range(n_ctx - 2)])
        dkv = jnp.concatenate([dkv[n_head : 2 * n_head], add(dkv[2 * n_head :], later)], axis=0)

    dkv = lax.all_to_all(dkv, both, 0, 0, axis_index_groups=pairs, tiled=True)
    dq = lax.all_to_all(dq, both, 0, 0, axis_index_groups=teams, tiled=True)
    dkv = dkv.reshape(2, planes, slots, 2, tok, head_dim).transpose(1, 0, 2, 3, 4, 5)
    return (dq_by_token(dq, tok, fan),) + dkv_by_token(dkv.reshape(planes, kv_heads, 2, tok, head_dim))


def solution(mesh):
    tokens = P(("ctx", "head"), None, None)
    return jax.shard_map(
        per_device,
        mesh=mesh,
        in_specs=(tokens,) * 5 + (P(("ctx", "head"), None), P()),
        out_specs=(tokens,) * 3,
        check_vma=False,
    )
```

```python
import functools

import jax
import jax.numpy as jnp
from jax import lax
from jax.experimental import pallas as pl
from jax.experimental.pallas import tpu as pltpu
from jax.sharding import PartitionSpec as P

BLK = 128
LOG2E = 1.4426950408889634
STAT_ROWS = 32
LIMIT = 56 * 1024 * 1024
PART_LIMIT = 12 * 1024 * 1024
SMALL_LIMIT = 6 * 1024 * 1024


def stats_of(stats, sources, chunks):
    stats = stats.astype(jnp.float32)
    sums = (
        stats[:, base : base + chunks]
        + stats[:, base + chunks : base + 2 * chunks]
        + stats[:, base + 2 * chunks : base + 3 * chunks]
        for base in (0, 3 * chunks)
    )
    lse, delta = (
        jnp.concatenate([x[s, c : c + 1, :] for s in range(sources) for c in range(chunks)], axis=1)
        for x in sums
    )
    return lse * LOG2E, delta


def block_pair(q, g, lse, delta, k, v, group, scale, mask):
    s = lax.dot_general(k, q, (((1,), (1,)), ((), ())), preferred_element_type=jnp.float32)
    p = jnp.exp2(s * (scale * LOG2E) - lse)
    if mask is True:
        key_at = lax.broadcasted_iota(jnp.int32, p.shape, 0)
        query_at = lax.broadcasted_iota(jnp.int32, p.shape, 1) // group
        p = jnp.where(query_at >= key_at, p, 0.0)
    elif mask is not None:
        p = jnp.where(mask, p, 0.0)
    dp = lax.dot_general(v, g, (((1,), (1,)), ((), ())), preferred_element_type=jnp.float32)
    ds = (p * (dp - delta)).astype(jnp.bfloat16)
    dv = jnp.dot(p.astype(jnp.bfloat16), g, preferred_element_type=jnp.float32)
    dk = jnp.dot(ds, q, preferred_element_type=jnp.float32)
    dq = lax.dot_general(ds, k, (((0,), (0,)), ((), ())), preferred_element_type=jnp.float32)
    return dq, dk, dv


def whole_kernel(meta, pkg, kv, dq, dkv, dk_acc, dv_acc, dq_acc, *, rows, tok, q_blocks, scale):
    sources = BLK // tok
    wide = sources * rows
    dk_acc[...] = jnp.zeros_like(dk_acc)
    dv_acc[...] = jnp.zeros_like(dv_acc)

    def over_queries(i, _):
        last, first = meta[i], meta[q_blocks + i]
        mine = pl.ds(sources * i, sources)
        q = pkg[mine, 0:rows, :].reshape(wide, 128)
        g = pkg[mine, rows : 2 * rows, :].reshape(wide, 128)
        lse, delta = stats_of(pkg[mine, 2 * rows :, :], sources, rows // 128)
        dq_acc[...] = jnp.zeros_like(dq_acc)

        def step(j, masked):
            k = kv[pl.ds(sources * j, sources), 0].reshape(BLK, 128)
            v = kv[pl.ds(sources * j, sources), 1].reshape(BLK, 128)
            dq_part, dk, dv = block_pair(q, g, lse, delta, k, v, rows // tok, scale, masked or None)
            at = pl.ds(pl.multiple_of(j * BLK, BLK), BLK)
            dv_acc[at, :] += dv
            dk_acc[at, :] += dk
            dq_acc[...] += dq_part

        def inner(j, _):
            step(j, False)
            return 0

        lax.fori_loop(first, last, inner, 0)
        step(last, True)
        dq[mine] = (dq_acc[...] * scale).astype(jnp.bfloat16).reshape(sources, rows, 128)
        return 0

    lax.fori_loop(0, q_blocks, over_queries, 0)
    shards = dkv.shape[0]
    dkv[:, 0] = (dk_acc[...] * scale).astype(jnp.bfloat16).reshape(shards, tok, 128)
    dkv[:, 1] = dv_acc[...].astype(jnp.bfloat16).reshape(shards, tok, 128)


def planes_kernel(meta, pkg, *refs, rows, tok, q_blocks, scale, distances, planes):
    team = pkg.shape[0]
    slots = team // 2
    count = len(distances)
    starts, ends = planes - 1 in distances, 0 in distances
    near, refs = refs[:count], refs[count:]
    if not starts:
        dq_before, refs = refs[0], refs[1:]
    outs = slots if ends else 1
    dq_out, grads_out, refs = refs[:outs], refs[outs : outs + count], refs[outs + count :]
    kv, grads, dk_acc, dv_acc, dq_acc, lse, delta, kv_sems, grad_sems = refs[:9]
    if ends:
        dq, out_sems = refs[9:]
    sources = BLK // tok
    wide = sources * rows
    group = rows // tok
    plane, slot = meta[2 * q_blocks], meta[2 * q_blocks + 1]
    range_blocks = 2 * planes
    loads = [pltpu.make_async_copy(near[n], kv.at[n], kv_sems.at[n]) for n in range(count)]
    for copy in loads:
        copy.start()
    dk_acc[...] = jnp.zeros_like(dk_acc)
    dv_acc[...] = jnp.zeros_like(dv_acc)
    for copy in loads:
        copy.wait()

    def over_range(r, _):
        lasts = [meta[2 * r + x] for x in range(2)]
        firsts = [meta[q_blocks + 2 * r + x] for x in range(2)]
        for x in range(2):
            stats = pkg[pl.ds(sources * (2 * r + x), sources), 2 * rows :, :]
            lse[x], delta[x] = stats_of(stats, sources, rows // 128)
            dq_acc[x] = jnp.zeros_like(dq_acc[x]) if starts else dq_before[2 * r + x]

        def queries(x):
            mine = pl.ds(sources * (2 * r + x), sources)
            q = pkg[mine, 0:rows, :].reshape(wide, 128)
            g = pkg[mine, rows : 2 * rows, :].reshape(wide, 128)
            return q, g, lse[x], delta[x]

        def keys(n, block, blocks):
            at = pl.ds(sources * block, sources * blocks)
            return kv[n, at, 0].reshape(blocks * BLK, 128), kv[n, at, 1].reshape(blocks * BLK, 128)

        def add_keys(n, block, dk, dv):
            at = pl.ds(pl.multiple_of(block * BLK, BLK), dk.shape[0])
            dk_acc[n, at, :] += dk
            dv_acc[n, at, :] += dv

        def both(n, half):
            k, v = keys(n, 2 * half, 2)
            parts = [block_pair(*queries(x), k, v, group, scale, None) for x in range(2)]
            for x in range(2):
                dq_acc[x] += parts[x][0]
            add_keys(n, 2 * half, parts[0][1] + parts[1][1], parts[0][2] + parts[1][2])

        def one(x, n, block):
            dq_part, dk, dv = block_pair(*queries(x), *keys(n, block, 1), group, scale, None)
            dq_acc[x] += dq_part
            add_keys(n, block, dk, dv)

        def inner(t, _):
            half, n = lax.div(t, count), lax.rem(t, count)
            base = half * range_blocks + 2 * ((n + distances[0]) ^ plane)
            seen = [
                [(base + y >= firsts[x]) & (base + y <= lasts[x]) for y in range(2)] for x in range(2)
            ]
            every = seen[0][0] & seen[0][1] & seen[1][0] & seen[1][1]
            if ends:
                own = base == lasts[0]
                every = every & jnp.logical_not(own)

            @pl.when(every)
            def _():
                both(n, half)

            for y in range(2):
                some = [seen[x][y] & jnp.logical_not(every) for x in range(2)]
                if ends:
                    some = [z & jnp.logical_not(own) for z in some]

                def single(x, _, y=y, some=some):
                    @pl.when(jnp.where(x == 0, some[0], some[1]))
                    def _():
                        one(x, n, 2 * half + y)

                    return 0

                lax.fori_loop(0, 2, single, 0)
            return 0

        lax.fori_loop(0, (r + 1) * count, inner, 0)
        if ends:
            n = distances.index(0)
            lower = [keys(n, 2 * r + y, 1) for y in range(2)]
            first_dq, dk, dv = block_pair(*queries(0), *lower[0], group, scale, True)
            cross = block_pair(*queries(1), *lower[0], group, scale, firsts[1] <= lasts[0])
            last_dq, dk_1, dv_1 = block_pair(*queries(1), *lower[1], group, scale, True)
            dq_acc[0] += first_dq
            dq_acc[1] += cross[0] + last_dq
            add_keys(n, 2 * r, dk + cross[1], dv + cross[2])
            add_keys(n, 2 * r + 1, dk_1, dv_1)
        for x in range(2):
            if ends:
                done = (dq_acc[x] * scale).astype(jnp.bfloat16).reshape(sources, rows, 128)
                dq[pl.ds(sources * (2 * r + x), sources)] = done
            else:
                dq_out[0][2 * r + x] = dq_acc[x]
        return 0

    lax.fori_loop(0, 2, over_range, 0)
    if ends:
        stores = [
            pltpu.make_async_copy(dq.at[b * slots + (slot ^ d)], dq_out[d].at[b], out_sems.at[b, d])
            for b in range(2)
            for d in range(slots)
        ]
        for copy in stores:
            copy.start()
    grad_stores = [pltpu.make_async_copy(grads.at[n], grads_out[n], grad_sems.at[n]) for n in range(count)]
    for n in reversed(range(count)):
        grads[n, :, 0] = (dk_acc[n] * scale).astype(jnp.bfloat16).reshape(team, tok, 128)
        grads[n, :, 1] = dv_acc[n].astype(jnp.bfloat16).reshape(team, tok, 128)
        grad_stores[n].start()
    if ends:
        for copy in stores:
            copy.wait()
    for copy in grad_stores:
        copy.wait()


VMEM = pl.BlockSpec(memory_space=pltpu.VMEM)
SMEM = pl.BlockSpec(memory_space=pltpu.SMEM)


def totals(shards, tok, wide, head_dim):
    return [
        pltpu.VMEM((shards * tok, head_dim), jnp.float32),
        pltpu.VMEM((shards * tok, head_dim), jnp.float32),
        pltpu.VMEM((wide, head_dim), jnp.float32),
    ]


def attention(meta, pkg, kv, rows, scale):
    shards, _, tok, head_dim = kv.shape
    team = pkg.shape[0]
    q_blocks = team * tok // BLK
    return pl.pallas_call(
        functools.partial(whole_kernel, rows=rows, tok=tok, q_blocks=q_blocks, scale=scale),
        out_shape=(
            jax.ShapeDtypeStruct((team, rows, head_dim), jnp.bfloat16),
            jax.ShapeDtypeStruct(kv.shape, jnp.bfloat16),
        ),
        in_specs=[SMEM, VMEM, VMEM],
        out_specs=(VMEM, VMEM),
        scratch_shapes=totals(shards, tok, rows * (BLK // tok), head_dim),
        compiler_params=pltpu.CompilerParams(vmem_limit_bytes=LIMIT),
        name="attention_grads",
    )(meta, pkg, kv)


def attention_part(meta, pkg, kv, distances, dq_before, rows, scale, planes):
    team, _, tok, head_dim = kv[0].shape
    slots = team // 2
    count = len(distances)
    q_blocks = team * tok // BLK
    wide = rows * (BLK // tok)
    scratch = [
        pltpu.VMEM((count,) + kv[0].shape, jnp.bfloat16),
        pltpu.VMEM((count,) + kv[0].shape, jnp.bfloat16),
        pltpu.VMEM((count, team * tok, head_dim), jnp.float32),
        pltpu.VMEM((count, team * tok, head_dim), jnp.float32),
        pltpu.VMEM((2, wide, head_dim), jnp.float32),
        pltpu.VMEM((2, 1, wide), jnp.float32),
        pltpu.VMEM((2, 1, wide), jnp.float32),
        pltpu.SemaphoreType.DMA((count,)),
        pltpu.SemaphoreType.DMA((count,)),
    ]
    hbm = pl.BlockSpec(memory_space=pltpu.HBM)
    ends = 0 in distances
    if ends:
        dq_shapes = (jax.ShapeDtypeStruct((2, rows, head_dim), jnp.bfloat16),) * slots
        dq_specs = (hbm,) * slots
        scratch += [pltpu.VMEM((team, rows, head_dim), jnp.bfloat16), pltpu.SemaphoreType.DMA((2, slots))]
    else:
        dq_shapes = (jax.ShapeDtypeStruct((q_blocks, wide, head_dim), jnp.float32),)
        dq_specs = (VMEM,)
    before = [] if dq_before is None else [dq_before]
    pairs = q_blocks * count
    out = pl.pallas_call(
        functools.partial(
            planes_kernel, rows=rows, tok=tok, q_blocks=q_blocks, scale=scale, distances=distances, planes=planes
        ),
        out_shape=dq_shapes + (jax.ShapeDtypeStruct(kv[0].shape, jnp.bfloat16),) * count,
        in_specs=[SMEM, VMEM] + [hbm] * count + [VMEM] * len(before),
        out_specs=dq_specs + (hbm,) * count,
        scratch_shapes=scratch,
        compiler_params=pltpu.CompilerParams(vmem_limit_bytes=PART_LIMIT),
        cost_estimate=pl.CostEstimate(
            flops=pairs * 10 * BLK * wide * head_dim,
            bytes_accessed=4 * 1024 * 1024,
            transcendentals=pairs * BLK * wide,
        ),
        name="attention_" + "_".join(str(d) for d in distances),
    )(meta, pkg, *kv, *before)
    dq, grads = out[:-count], out[-count:]
    return (dq if ends else dq[0]), grads


def place_dq_kernel(place, *refs):
    *arrived, swapped, out = refs
    slots = len(arrived)
    core, slot = place[0], place[1]
    for d, blocks in enumerate(arrived):
        out[:, core * slots + (slot ^ d)] = blocks[core]
        out[:, (1 - core) * slots + (slot ^ d)] = swapped[d]


def place_dq(place, arrived, swapped, tok):
    slots, rows, head_dim = swapped.shape
    fan = rows // tok
    out = pl.pallas_call(
        place_dq_kernel,
        out_shape=jax.ShapeDtypeStruct((tok, 2 * slots, fan, head_dim), jnp.bfloat16),
        in_specs=[SMEM] + [VMEM] * (slots + 1),
        out_specs=VMEM,
        compiler_params=pltpu.CompilerParams(vmem_limit_bytes=SMALL_LIMIT),
        name="place_dq",
    )(place, *[x.reshape(2, tok, fan, head_dim) for x in arrived], swapped.reshape(slots, tok, fan, head_dim))
    return out.reshape(tok, 2 * slots * fan, head_dim)


def place_dkv_kernel(parts, dk, dv, wide):
    halves, kv_heads = parts.shape[:2]
    for n, out in enumerate((dk, dv)):
        for h in range(kv_heads):
            wide[:, h, :] = sum(parts[p, h, n].astype(jnp.float32) for p in range(halves))
        out[...] = wide[...].astype(jnp.bfloat16)


def place_dkv(parts):
    _, kv_heads, _, tok, head_dim = parts.shape
    shape = (tok, kv_heads, head_dim)
    dk, dv = pl.pallas_call(
        place_dkv_kernel,
        out_shape=(jax.ShapeDtypeStruct(shape, jnp.bfloat16),) * 2,
        in_specs=[VMEM],
        out_specs=(VMEM, VMEM),
        scratch_shapes=[pltpu.VMEM(shape, jnp.float32)],
        compiler_params=pltpu.CompilerParams(vmem_limit_bytes=SMALL_LIMIT),
        name="place_dkv",
    )(parts)
    return dk, dv


def pieces(x):
    high = lax.reduce_precision(x, 8, 7)
    rest = x - high
    mid = lax.reduce_precision(rest, 8, 7)
    low = rest - mid
    return [part.astype(jnp.bfloat16) for part in (high, mid, low)]


def add(*terms):
    return sum(x.astype(jnp.float32) for x in terms).astype(jnp.bfloat16)


def dq_by_token(dq, tok, fan):
    kv_heads, _, head_dim = dq.shape
    return dq.reshape(kv_heads, tok, fan, head_dim).transpose(1, 0, 2, 3).reshape(tok, kv_heads * fan, head_dim)


def dkv_by_token(parts):
    dkv = parts.astype(jnp.float32).sum(axis=0).astype(jnp.bfloat16).transpose(1, 2, 0, 3)
    return dkv[0], dkv[1]


def per_device(queries, keys, values, outputs, out_grads, log_norms, block_doc):
    tok, heads, head_dim = queries.shape
    kv_heads = keys.shape[1]
    fan = heads // kv_heads
    n_ctx, n_head = lax.axis_size("ctx"), lax.axis_size("head")
    slots = kv_heads // 2
    planes = n_head // slots
    rows = tok * fan
    scale = head_dim**-0.5
    ctx, head = lax.axis_index("ctx"), lax.axis_index("head")
    both = ("ctx", "head")
    teams = [
        [(2 * c + b) * n_head + z * slots + r for b in range(2) for r in range(slots)]
        for c in range(n_ctx // 2)
        for z in range(planes)
    ]
    pairs = [
        [(2 * c + b) * n_head + h for b in range(2) for h in range(n_head)]
        for c in range(n_ctx // 2)
    ]

    by_plane = n_ctx == 2 and planes == 4 and slots * tok == 2 * BLK

    def across(x, distance):
        step = distance * slots
        return lax.ppermute(x, "head", [(h, h ^ step) for h in range(n_head)])

    kv = jnp.stack([keys, values], axis=0).transpose(2, 0, 1, 3)
    if by_plane:
        kv = lax.all_to_all(kv, both, 0, 0, axis_index_groups=teams, tiled=True)
        second, first = across(kv, 2), across(kv, 1)
        kv = (kv, first, second, across(second, 1))
    else:
        kv = kv.reshape(2, 1, slots, 2, tok, head_dim)
        kv = jnp.broadcast_to(kv, (2, planes, slots, 2, tok, head_dim))
        kv = kv.reshape(2 * n_head, 2, tok, head_dim)
        kv = lax.all_to_all(kv, both, 0, 0, axis_index_groups=pairs, tiled=True)

    def by_group(x):
        return x.reshape(tok, kv_heads, fan, head_dim).transpose(1, 0, 2, 3).reshape(kv_heads, rows, head_dim)

    deltas = jnp.sum(out_grads.astype(jnp.float32) * outputs.astype(jnp.float32), axis=-1)
    stats = jnp.stack(pieces(log_norms) + pieces(deltas), axis=0)
    stats = stats.reshape(6, tok, kv_heads, fan).transpose(2, 0, 1, 3)
    stats = stats.reshape(kv_heads, 6 * rows // 128, 128)
    stats = jnp.pad(stats, ((0, 0), (0, STAT_ROWS - stats.shape[1]), (0, 0)))
    pkg = jnp.concatenate([by_group(queries), by_group(out_grads), stats], axis=1)
    pkg = lax.all_to_all(pkg, both, 0, 0, axis_index_groups=teams, tiled=True)

    pair, plane = lax.div(ctx, 2), lax.div(head, slots)
    range_blocks = n_head * tok // BLK
    team_blocks = slots * tok // BLK
    at = jnp.stack(
        [(2 * pair + b) * range_blocks + plane * team_blocks + j for b in range(2) for j in range(team_blocks)]
    )
    first_block = jnp.sum(block_doc[None, :] < block_doc[at][:, None], axis=1, dtype=jnp.int32)
    ranges_before = 1 if n_ctx > 2 else 0
    base = (2 * pair - ranges_before) * range_blocks
    meta = jnp.concatenate([at - base, first_block - base, plane[None], lax.rem(head, slots)[None]]).astype(jnp.int32)

    if by_plane:
        def part(distances, dq_before):
            return attention_part(
                meta, pkg, [kv[d] for d in distances], distances, dq_before, rows, scale, planes
            )

        dq, (grads_3,) = part((3,), None)
        relayed = across(grads_3, 1)
        dq, (grads_0, grads_1, grads_2) = part((0, 1, 2), dq)
        far = add(grads_2, relayed)
        far, *dq = lax.optimization_barrier((far, *dq))
        far = across(far, 2)
        close = across(grads_1, 1)
        dq = [lax.ppermute(x, "head", [(h, h ^ d) for h in range(n_head)]) if d else x for d, x in enumerate(dq)]
        dkv = add(grads_0, close, far)
        dkv, *dq = lax.optimization_barrier((dkv, *dq))
        dkv = lax.all_to_all(dkv, both, 0, 0, axis_index_groups=teams, tiled=True)
        other = jnp.where(ctx == 0, jnp.stack([x[1] for x in dq]), jnp.stack([x[0] for x in dq]))
        swapped = lax.ppermute(other, "ctx", [(0, 1), (1, 0)])
        dq = place_dq(jnp.stack([ctx, lax.rem(head, slots)]), dq, swapped, tok)
        dkv, dq = lax.optimization_barrier((dkv, dq))
        return (dq,) + place_dkv(dkv[None])

    if ranges_before:
        prior = lax.ppermute(kv[n_head:], "ctx", [(c, c + 2) for c in range(n_ctx - 2)])
        kv = jnp.concatenate([prior, kv], axis=0)
    dq, dkv = attention(meta, pkg, kv, rows, scale)
    if ranges_before:
        later = lax.ppermute(dkv[:n_head], "ctx", [(c + 2, c) for c in range(n_ctx - 2)])
        dkv = jnp.concatenate([dkv[n_head : 2 * n_head], add(dkv[2 * n_head :], later)], axis=0)

    dkv = lax.all_to_all(dkv, both, 0, 0, axis_index_groups=pairs, tiled=True)
    dq = lax.all_to_all(dq, both, 0, 0, axis_index_groups=teams, tiled=True)
    dkv = dkv.reshape(2, planes, slots, 2, tok, head_dim).transpose(1, 0, 2, 3, 4, 5)
    return (dq_by_token(dq, tok, fan),) + dkv_by_token(dkv.reshape(planes, kv_heads, 2, tok, head_dim))


def solution(mesh):
    tokens = P(("ctx", "head"), None, None)
    return jax.shard_map(
        per_device,
        mesh=mesh,
        in_specs=(tokens,) * 5 + (P(("ctx", "head"), None), P()),
        out_specs=(tokens,) * 3,
        check_vma=False,
    )
```

```python
import functools

import jax
import jax.numpy as jnp
from jax import lax
from jax.experimental import pallas as pl
from jax.experimental.pallas import tpu as pltpu
from jax.sharding import PartitionSpec as P

BLK = 128
LOG2E = 1.4426950408889634
STAT_ROWS = 32
LIMIT = 56 * 1024 * 1024
PART_LIMIT = 12 * 1024 * 1024
SMALL_LIMIT = 6 * 1024 * 1024


def stats_of(stats, sources, chunks):
    stats = stats.astype(jnp.float32)
    sums = (
        stats[:, base : base + chunks]
        + stats[:, base + chunks : base + 2 * chunks]
        + stats[:, base + 2 * chunks : base + 3 * chunks]
        for base in (0, 3 * chunks)
    )
    lse, delta = (
        jnp.concatenate([x[s, c : c + 1, :] for s in range(sources) for c in range(chunks)], axis=1)
        for x in sums
    )
    return lse * LOG2E, delta


def block_pair(q, g, lse, delta, k, v, group, scale, mask):
    s = lax.dot_general(k, q, (((1,), (1,)), ((), ())), preferred_element_type=jnp.float32)
    p = jnp.exp2(s * (scale * LOG2E) - lse)
    if mask is not None:
        lead, from_key = mask
        key_at = lax.broadcasted_iota(jnp.int32, p.shape, 0)
        query_at = lax.broadcasted_iota(jnp.int32, p.shape, 1) // group + lead
        p = jnp.where((query_at >= key_at) & (key_at >= from_key), p, 0.0)
    dp = lax.dot_general(v, g, (((1,), (1,)), ((), ())), preferred_element_type=jnp.float32)
    ds = (p * (dp - delta)).astype(jnp.bfloat16)
    dv = jnp.dot(p.astype(jnp.bfloat16), g, preferred_element_type=jnp.float32)
    dk = jnp.dot(ds, q, preferred_element_type=jnp.float32)
    dq = lax.dot_general(ds, k, (((0,), (0,)), ((), ())), preferred_element_type=jnp.float32)
    return dq, dk, dv


def whole_kernel(meta, pkg, kv, dq, dkv, dk_acc, dv_acc, dq_acc, *, rows, tok, q_blocks, scale):
    sources = BLK // tok
    wide = sources * rows
    dk_acc[...] = jnp.zeros_like(dk_acc)
    dv_acc[...] = jnp.zeros_like(dv_acc)

    def over_queries(i, _):
        last, first = meta[i], meta[q_blocks + i]
        mine = pl.ds(sources * i, sources)
        q = pkg[mine, 0:rows, :].reshape(wide, 128)
        g = pkg[mine, rows : 2 * rows, :].reshape(wide, 128)
        lse, delta = stats_of(pkg[mine, 2 * rows :, :], sources, rows // 128)
        dq_acc[...] = jnp.zeros_like(dq_acc)

        def step(j, masked):
            k = kv[pl.ds(sources * j, sources), 0].reshape(BLK, 128)
            v = kv[pl.ds(sources * j, sources), 1].reshape(BLK, 128)
            dq_part, dk, dv = block_pair(q, g, lse, delta, k, v, rows // tok, scale, (0, 0) if masked else None)
            at = pl.ds(pl.multiple_of(j * BLK, BLK), BLK)
            dv_acc[at, :] += dv
            dk_acc[at, :] += dk
            dq_acc[...] += dq_part

        def inner(j, _):
            step(j, False)
            return 0

        lax.fori_loop(first, last, inner, 0)
        step(last, True)
        dq[mine] = (dq_acc[...] * scale).astype(jnp.bfloat16).reshape(sources, rows, 128)
        return 0

    lax.fori_loop(0, q_blocks, over_queries, 0)
    shards = dkv.shape[0]
    dkv[:, 0] = (dk_acc[...] * scale).astype(jnp.bfloat16).reshape(shards, tok, 128)
    dkv[:, 1] = dv_acc[...].astype(jnp.bfloat16).reshape(shards, tok, 128)


def planes_kernel(meta, pkg, *refs, rows, tok, q_blocks, scale, distances, planes):
    team = pkg.shape[0]
    slots = team // 2
    count = len(distances)
    starts, ends = planes - 1 in distances, 0 in distances
    near, refs = refs[:count], refs[count:]
    if not starts:
        dq_before, refs = refs[0], refs[1:]
    outs = slots if ends else 1
    dq_out, grads_out, refs = refs[:outs], refs[outs : outs + count], refs[outs + count :]
    kv, grads, dk_acc, dv_acc, dq_acc, lse, delta, kv_sems, grad_sems = refs[:9]
    if ends:
        dq, out_sems = refs[9:]
    sources = BLK // tok
    wide = sources * rows
    group = rows // tok
    plane, slot = meta[2 * q_blocks], meta[2 * q_blocks + 1]
    range_blocks = 2 * planes
    dk_acc[...] = jnp.zeros_like(dk_acc)
    dv_acc[...] = jnp.zeros_like(dv_acc)
    if ends:
        loads = [pltpu.make_async_copy(near[n], kv.at[n], kv_sems.at[n]) for n in range(count)]
        for copy in loads:
            copy.start()
        for copy in loads:
            copy.wait()

    def over_range(r, _):
        lasts = [meta[2 * r + x] for x in range(2)]
        firsts = [meta[q_blocks + 2 * r + x] for x in range(2)]
        for x in range(2):
            stats = pkg[pl.ds(sources * (2 * r + x), sources), 2 * rows :, :]
            lse[x], delta[x] = stats_of(stats, sources, rows // 128)
            dq_acc[x] = jnp.zeros_like(dq_acc[x]) if starts else dq_before[2 * r + x]

        def queries(x):
            mine = pl.ds(sources * (2 * r + x), sources)
            q = pkg[mine, 0:rows, :].reshape(wide, 128)
            g = pkg[mine, rows : 2 * rows, :].reshape(wide, 128)
            return q, g, lse[x], delta[x]

        def keys(n, block, blocks):
            at = pl.ds(sources * block, sources * blocks)
            held = kv.at[n] if ends else near[0]
            return held[at, 0].reshape(blocks * BLK, 128), held[at, 1].reshape(blocks * BLK, 128)

        def add_keys(n, block, dk, dv):
            at = pl.ds(pl.multiple_of(block * BLK, BLK), dk.shape[0])
            dk_acc[n, at, :] += dk
            dv_acc[n, at, :] += dv

        def both(n, half):
            k, v = keys(n, 2 * half, 2)
            parts = [block_pair(*queries(x), k, v, group, scale, None) for x in range(2)]
            for x in range(2):
                dq_acc[x] += parts[x][0]
            add_keys(n, 2 * half, parts[0][1] + parts[1][1], parts[0][2] + parts[1][2])

        def one(x, n, block):
            dq_part, dk, dv = block_pair(*queries(x), *keys(n, block, 1), group, scale, None)
            dq_acc[x] += dq_part
            add_keys(n, block, dk, dv)

        def inner(t, _):
            half, n = lax.div(t, count), lax.rem(t, count)
            base = half * range_blocks + 2 * ((n + distances[0]) ^ plane)
            seen = [
                [(base + y >= firsts[x]) & (base + y <= lasts[x]) for y in range(2)] for x in range(2)
            ]
            every = seen[0][0] & seen[0][1] & seen[1][0] & seen[1][1]
            if ends:
                own = base == lasts[0]
                every = every & jnp.logical_not(own)

            @pl.when(every)
            def _():
                both(n, half)

            for y in range(2):
                some = [seen[x][y] & jnp.logical_not(every) for x in range(2)]
                if ends:
                    some = [z & jnp.logical_not(own) for z in some]

                def single(x, _, y=y, some=some):
                    @pl.when(jnp.where(x == 0, some[0], some[1]))
                    def _():
                        one(x, n, 2 * half + y)

                    return 0

                lax.fori_loop(0, 2, single, 0)
            return 0

        lax.fori_loop(0, (r + 1) * count, inner, 0)
        if ends:
            n = distances.index(0)
            from_key = jnp.where(firsts[1] <= lasts[0], 0, BLK)
            dq_0, dk, dv = block_pair(*queries(0), *keys(n, 2 * r, 1), group, scale, (0, 0))
            dq_1, dk_1, dv_1 = block_pair(*queries(1), *keys(n, 2 * r, 2), group, scale, (BLK, from_key))
            dq_acc[0] += dq_0
            dq_acc[1] += dq_1
            add_keys(n, 2 * r, dk + dk_1[0:BLK], dv + dv_1[0:BLK])
            add_keys(n, 2 * r + 1, dk_1[BLK:], dv_1[BLK:])
        for x in range(2):
            if ends:
                done = (dq_acc[x] * scale).astype(jnp.bfloat16).reshape(sources, rows, 128)
                dq[pl.ds(sources * (2 * r + x), sources)] = done
            else:
                dq_out[0][2 * r + x] = dq_acc[x]
        return 0

    lax.fori_loop(0, 2, over_range, 0)
    if ends:
        stores = [
            pltpu.make_async_copy(dq.at[b * slots + (slot ^ d)], dq_out[d].at[b], out_sems.at[b, d])
            for b in range(2)
            for d in range(slots)
        ]
        for copy in stores:
            copy.start()
    if not ends:
        grads_out[0][:, 0] = (dk_acc[0] * scale).astype(jnp.bfloat16).reshape(team, tok, 128)
        grads_out[0][:, 1] = dv_acc[0].astype(jnp.bfloat16).reshape(team, tok, 128)
        return
    grad_stores = [pltpu.make_async_copy(grads.at[n], grads_out[n], grad_sems.at[n]) for n in range(count)]
    for n in reversed(range(count)):
        grads[n, :, 0] = (dk_acc[n] * scale).astype(jnp.bfloat16).reshape(team, tok, 128)
        grads[n, :, 1] = dv_acc[n].astype(jnp.bfloat16).reshape(team, tok, 128)
        grad_stores[n].start()
    for copy in stores + grad_stores:
        copy.wait()


VMEM = pl.BlockSpec(memory_space=pltpu.VMEM)
SMEM = pl.BlockSpec(memory_space=pltpu.SMEM)


def totals(shards, tok, wide, head_dim):
    return [
        pltpu.VMEM((shards * tok, head_dim), jnp.float32),
        pltpu.VMEM((shards * tok, head_dim), jnp.float32),
        pltpu.VMEM((wide, head_dim), jnp.float32),
    ]


def attention(meta, pkg, kv, rows, scale):
    shards, _, tok, head_dim = kv.shape
    team = pkg.shape[0]
    q_blocks = team * tok // BLK
    return pl.pallas_call(
        functools.partial(whole_kernel, rows=rows, tok=tok, q_blocks=q_blocks, scale=scale),
        out_shape=(
            jax.ShapeDtypeStruct((team, rows, head_dim), jnp.bfloat16),
            jax.ShapeDtypeStruct(kv.shape, jnp.bfloat16),
        ),
        in_specs=[SMEM, VMEM, VMEM],
        out_specs=(VMEM, VMEM),
        scratch_shapes=totals(shards, tok, rows * (BLK // tok), head_dim),
        compiler_params=pltpu.CompilerParams(vmem_limit_bytes=LIMIT),
        name="attention_grads",
    )(meta, pkg, kv)


def attention_part(meta, pkg, kv, distances, dq_before, rows, scale, planes):
    team, _, tok, head_dim = kv[0].shape
    slots = team // 2
    count = len(distances)
    q_blocks = team * tok // BLK
    wide = rows * (BLK // tok)
    scratch = [
        pltpu.VMEM((count,) + kv[0].shape, jnp.bfloat16),
        pltpu.VMEM((count,) + kv[0].shape, jnp.bfloat16),
        pltpu.VMEM((count, team * tok, head_dim), jnp.float32),
        pltpu.VMEM((count, team * tok, head_dim), jnp.float32),
        pltpu.VMEM((2, wide, head_dim), jnp.float32),
        pltpu.VMEM((2, 1, wide), jnp.float32),
        pltpu.VMEM((2, 1, wide), jnp.float32),
        pltpu.SemaphoreType.DMA((count,)),
        pltpu.SemaphoreType.DMA((count,)),
    ]
    hbm = pl.BlockSpec(memory_space=pltpu.HBM)
    ends = 0 in distances
    if ends:
        dq_shapes = (jax.ShapeDtypeStruct((2, rows, head_dim), jnp.bfloat16),) * slots
        dq_specs = (hbm,) * slots
        scratch += [pltpu.VMEM((team, rows, head_dim), jnp.bfloat16), pltpu.SemaphoreType.DMA((2, slots))]
    else:
        dq_shapes = (jax.ShapeDtypeStruct((q_blocks, wide, head_dim), jnp.float32),)
        dq_specs = (VMEM,)
    before = [] if dq_before is None else [dq_before]
    pairs = q_blocks * count
    out = pl.pallas_call(
        functools.partial(
            planes_kernel, rows=rows, tok=tok, q_blocks=q_blocks, scale=scale, distances=distances, planes=planes
        ),
        out_shape=dq_shapes + (jax.ShapeDtypeStruct(kv[0].shape, jnp.bfloat16),) * count,
        in_specs=[SMEM, VMEM] + [hbm if ends else VMEM] * count + [VMEM] * len(before),
        out_specs=dq_specs + (hbm if ends else VMEM,) * count,
        scratch_shapes=scratch,
        compiler_params=pltpu.CompilerParams(vmem_limit_bytes=PART_LIMIT),
        cost_estimate=pl.CostEstimate(
            flops=pairs * 10 * BLK * wide * head_dim,
            bytes_accessed=4 * 1024 * 1024,
            transcendentals=pairs * BLK * wide,
        ),
        name="attention_" + "_".join(str(d) for d in distances),
    )(meta, pkg, *kv, *before)
    dq, grads = out[:-count], out[-count:]
    return (dq if ends else dq[0]), grads


def sum_kernel(*refs):
    *terms, out = refs
    out[...] = sum(x[...].astype(jnp.float32) for x in terms)


def sum_of(*terms):
    return pl.pallas_call(
        sum_kernel,
        out_shape=jax.ShapeDtypeStruct(terms[0].shape, jnp.float32),
        in_specs=[VMEM] * len(terms),
        out_specs=VMEM,
        compiler_params=pltpu.CompilerParams(vmem_limit_bytes=SMALL_LIMIT),
        name="sum_dkv",
    )(*terms)


def place_dq_kernel(place, *refs):
    *arrived, swapped, out = refs
    slots = len(arrived)
    core, slot = place[0], place[1]
    for d, blocks in enumerate(arrived):
        out[:, core * slots + (slot ^ d)] = blocks[core]
        out[:, (1 - core) * slots + (slot ^ d)] = swapped[d]


def place_dq(place, arrived, swapped, tok):
    slots, rows, head_dim = swapped.shape
    fan = rows // tok
    out = pl.pallas_call(
        place_dq_kernel,
        out_shape=jax.ShapeDtypeStruct((tok, 2 * slots, fan, head_dim), jnp.bfloat16),
        in_specs=[SMEM] + [VMEM] * (slots + 1),
        out_specs=VMEM,
        compiler_params=pltpu.CompilerParams(vmem_limit_bytes=SMALL_LIMIT),
        name="place_dq",
    )(place, *[x.reshape(2, tok, fan, head_dim) for x in arrived], swapped.reshape(slots, tok, fan, head_dim))
    return out.reshape(tok, 2 * slots * fan, head_dim)


def place_dkv_kernel(parts, dk, dv, wide):
    halves, kv_heads = parts.shape[:2]
    for n, out in enumerate((dk, dv)):
        for h in range(kv_heads):
            wide[:, h, :] = sum(parts[p, h, n].astype(jnp.float32) for p in range(halves))
        out[...] = wide[...].astype(jnp.bfloat16)


def place_dkv(parts):
    _, kv_heads, _, tok, head_dim = parts.shape
    shape = (tok, kv_heads, head_dim)
    dk, dv = pl.pallas_call(
        place_dkv_kernel,
        out_shape=(jax.ShapeDtypeStruct(shape, jnp.bfloat16),) * 2,
        in_specs=[VMEM],
        out_specs=(VMEM, VMEM),
        scratch_shapes=[pltpu.VMEM(shape, jnp.float32)],
        compiler_params=pltpu.CompilerParams(vmem_limit_bytes=SMALL_LIMIT),
        name="place_dkv",
    )(parts)
    return dk, dv


def pieces(x):
    high = lax.reduce_precision(x, 8, 7)
    rest = x - high
    mid = lax.reduce_precision(rest, 8, 7)
    low = rest - mid
    return [part.astype(jnp.bfloat16) for part in (high, mid, low)]


def add(*terms):
    return sum(x.astype(jnp.float32) for x in terms).astype(jnp.bfloat16)


def dq_by_token(dq, tok, fan):
    kv_heads, _, head_dim = dq.shape
    return dq.reshape(kv_heads, tok, fan, head_dim).transpose(1, 0, 2, 3).reshape(tok, kv_heads * fan, head_dim)


def dkv_by_token(parts):
    dkv = parts.astype(jnp.float32).sum(axis=0).astype(jnp.bfloat16).transpose(1, 2, 0, 3)
    return dkv[0], dkv[1]


def per_device(queries, keys, values, outputs, out_grads, log_norms, block_doc):
    tok, heads, head_dim = queries.shape
    kv_heads = keys.shape[1]
    fan = heads // kv_heads
    n_ctx, n_head = lax.axis_size("ctx"), lax.axis_size("head")
    slots = kv_heads // 2
    planes = n_head // slots
    rows = tok * fan
    scale = head_dim**-0.5
    ctx, head = lax.axis_index("ctx"), lax.axis_index("head")
    both = ("ctx", "head")
    teams = [
        [(2 * c + b) * n_head + z * slots + r for b in range(2) for r in range(slots)]
        for c in range(n_ctx // 2)
        for z in range(planes)
    ]
    pairs = [
        [(2 * c + b) * n_head + h for b in range(2) for h in range(n_head)]
        for c in range(n_ctx // 2)
    ]

    by_plane = n_ctx == 2 and planes == 4 and slots * tok == 2 * BLK

    def across(x, distance):
        step = distance * slots
        return lax.ppermute(x, "head", [(h, h ^ step) for h in range(n_head)])

    kv = jnp.stack([keys, values], axis=0).transpose(2, 0, 1, 3)
    if by_plane:
        kv = lax.all_to_all(kv, both, 0, 0, axis_index_groups=teams, tiled=True)
        second, first = across(kv, 2), across(kv, 1)
        kv = (kv, first, second, across(second, 1))
    else:
        kv = kv.reshape(2, 1, slots, 2, tok, head_dim)
        kv = jnp.broadcast_to(kv, (2, planes, slots, 2, tok, head_dim))
        kv = kv.reshape(2 * n_head, 2, tok, head_dim)
        kv = lax.all_to_all(kv, both, 0, 0, axis_index_groups=pairs, tiled=True)

    def by_group(x):
        return x.reshape(tok, kv_heads, fan, head_dim).transpose(1, 0, 2, 3).reshape(kv_heads, rows, head_dim)

    deltas = jnp.sum(out_grads.astype(jnp.float32) * outputs.astype(jnp.float32), axis=-1)
    stats = jnp.stack(pieces(log_norms) + pieces(deltas), axis=0)
    stats = stats.reshape(6, tok, kv_heads, fan).transpose(2, 0, 1, 3)
    stats = stats.reshape(kv_heads, 6 * rows // 128, 128)
    stats = jnp.pad(stats, ((0, 0), (0, STAT_ROWS - stats.shape[1]), (0, 0)))
    pkg = jnp.concatenate([by_group(queries), by_group(out_grads), stats], axis=1)
    pkg = lax.all_to_all(pkg, both, 0, 0, axis_index_groups=teams, tiled=True)

    pair, plane = lax.div(ctx, 2), lax.div(head, slots)
    range_blocks = n_head * tok // BLK
    team_blocks = slots * tok // BLK
    at = jnp.stack(
        [(2 * pair + b) * range_blocks + plane * team_blocks + j for b in range(2) for j in range(team_blocks)]
    )
    first_block = jnp.sum(block_doc[None, :] < block_doc[at][:, None], axis=1, dtype=jnp.int32)
    ranges_before = 1 if n_ctx > 2 else 0
    base = (2 * pair - ranges_before) * range_blocks
    meta = jnp.concatenate([at - base, first_block - base, plane[None], lax.rem(head, slots)[None]]).astype(jnp.int32)

    if by_plane:
        def part(distances, dq_before):
            return attention_part(
                meta, pkg, [kv[d] for d in distances], distances, dq_before, rows, scale, planes
            )

        dq, (grads_3,) = part((3,), None)
        relayed = across(grads_3, 1)
        dq, (grads_0, grads_1, grads_2) = part((0, 1, 2), dq)
        far = add(grads_2, relayed)
        far, *dq = lax.optimization_barrier((far, *dq))
        far = across(far, 2)
        close = across(grads_1, 1)
        dq = [lax.ppermute(x, "head", [(h, h ^ d) for h in range(n_head)]) if d else x for d, x in enumerate(dq)]
        dkv = add(sum_of(grads_0, close), far)
        dkv, *dq = lax.optimization_barrier((dkv, *dq))
        dkv = lax.all_to_all(dkv, both, 0, 0, axis_index_groups=teams, tiled=True)
        other = jnp.where(ctx == 0, jnp.stack([x[1] for x in dq]), jnp.stack([x[0] for x in dq]))
        swapped = lax.ppermute(other, "ctx", [(0, 1), (1, 0)])
        dq = place_dq(jnp.stack([ctx, lax.rem(head, slots)]), dq, swapped, tok)
        dkv, dq = lax.optimization_barrier((dkv, dq))
        return (dq,) + place_dkv(dkv[None])

    if ranges_before:
        prior = lax.ppermute(kv[n_head:], "ctx", [(c, c + 2) for c in range(n_ctx - 2)])
        kv = jnp.concatenate([prior, kv], axis=0)
    dq, dkv = attention(meta, pkg, kv, rows, scale)
    if ranges_before:
        later = lax.ppermute(dkv[:n_head], "ctx", [(c + 2, c) for c in range(n_ctx - 2)])
        dkv = jnp.concatenate([dkv[n_head : 2 * n_head], add(dkv[2 * n_head :], later)], axis=0)

    dkv = lax.all_to_all(dkv, both, 0, 0, axis_index_groups=pairs, tiled=True)
    dq = lax.all_to_all(dq, both, 0, 0, axis_index_groups=teams, tiled=True)
    dkv = dkv.reshape(2, planes, slots, 2, tok, head_dim).transpose(1, 0, 2, 3, 4, 5)
    return (dq_by_token(dq, tok, fan),) + dkv_by_token(dkv.reshape(planes, kv_heads, 2, tok, head_dim))


def solution(mesh):
    tokens = P(("ctx", "head"), None, None)
    return jax.shard_map(
        per_device,
        mesh=mesh,
        in_specs=(tokens,) * 5 + (P(("ctx", "head"), None), P()),
        out_specs=(tokens,) * 3,
        check_vma=False,
    )
```

```python
import functools

import jax
import jax.numpy as jnp
from jax import lax
from jax.experimental import pallas as pl
from jax.experimental.pallas import tpu as pltpu
from jax.sharding import PartitionSpec as P

BLK = 128
LOG2E = 1.4426950408889634
LIMIT = 56 * 1024 * 1024
PART_LIMIT = 12 * 1024 * 1024
SMALL_LIMIT = 6 * 1024 * 1024


def stats_of(stats, sources, chunks):
    stats = stats.astype(jnp.float32)
    sums = (
        stats[:, base : base + chunks] + stats[:, base + chunks : base + 2 * chunks]
        for base in (0, 2 * chunks)
    )
    lse, delta = (
        jnp.concatenate([x[s, c : c + 1, :] for s in range(sources) for c in range(chunks)], axis=1)
        for x in sums
    )
    return lse * LOG2E, delta


def block_pair(q, g, lse, delta, k, v, group, scale, mask):
    s = lax.dot_general(k, q, (((1,), (1,)), ((), ())), preferred_element_type=jnp.float32)
    p = jnp.exp2(s * (scale * LOG2E) - lse)
    if mask is not None:
        lead, from_key = mask
        key_at = lax.broadcasted_iota(jnp.int32, p.shape, 0)
        query_at = lax.broadcasted_iota(jnp.int32, p.shape, 1) // group + lead
        p = jnp.where((query_at >= key_at) & (key_at >= from_key), p, 0.0)
    dp = lax.dot_general(v, g, (((1,), (1,)), ((), ())), preferred_element_type=jnp.float32)
    ds = (p * (dp - delta)).astype(jnp.bfloat16)
    dv = jnp.dot(p.astype(jnp.bfloat16), g, preferred_element_type=jnp.float32)
    dk = jnp.dot(ds, q, preferred_element_type=jnp.float32)
    dq = lax.dot_general(ds, k, (((0,), (0,)), ((), ())), preferred_element_type=jnp.float32)
    return dq, dk, dv


def whole_kernel(meta, pkg, kv, dq, dkv, dk_acc, dv_acc, dq_acc, *, rows, tok, q_blocks, scale):
    sources = BLK // tok
    wide = sources * rows
    dk_acc[...] = jnp.zeros_like(dk_acc)
    dv_acc[...] = jnp.zeros_like(dv_acc)

    def over_queries(i, _):
        last, first = meta[i], meta[q_blocks + i]
        mine = pl.ds(sources * i, sources)
        q = pkg[mine, 0:rows, :].reshape(wide, 128)
        g = pkg[mine, rows : 2 * rows, :].reshape(wide, 128)
        lse, delta = stats_of(pkg[mine, 2 * rows :, :], sources, rows // 128)
        dq_acc[...] = jnp.zeros_like(dq_acc)

        def step(j, masked):
            k = kv[pl.ds(sources * j, sources), 0].reshape(BLK, 128)
            v = kv[pl.ds(sources * j, sources), 1].reshape(BLK, 128)
            dq_part, dk, dv = block_pair(q, g, lse, delta, k, v, rows // tok, scale, (0, 0) if masked else None)
            at = pl.ds(pl.multiple_of(j * BLK, BLK), BLK)
            dv_acc[at, :] += dv
            dk_acc[at, :] += dk
            dq_acc[...] += dq_part

        def inner(j, _):
            step(j, False)
            return 0

        lax.fori_loop(first, last, inner, 0)
        step(last, True)
        dq[mine] = (dq_acc[...] * scale).astype(jnp.bfloat16).reshape(sources, rows, 128)
        return 0

    lax.fori_loop(0, q_blocks, over_queries, 0)
    shards = dkv.shape[0]
    dkv[:, 0] = (dk_acc[...] * scale).astype(jnp.bfloat16).reshape(shards, tok, 128)
    dkv[:, 1] = dv_acc[...].astype(jnp.bfloat16).reshape(shards, tok, 128)


def planes_kernel(meta, pkg, *refs, rows, tok, q_blocks, scale, distances, planes):
    team = pkg.shape[0]
    slots = team // 2
    count = len(distances)
    starts, ends = planes - 1 in distances, 0 in distances
    near, refs = refs[:count], refs[count:]
    if not starts:
        dq_before, refs = refs[0], refs[1:]
    outs = slots if ends else 1
    dq_out, grads_out, refs = refs[:outs], refs[outs : outs + count], refs[outs + count :]
    kv, grads, dk_acc, dv_acc, dq_acc, lse, delta, kv_sems, grad_sems = refs[:9]
    if ends:
        dq, out_sems = refs[9:]
    sources = BLK // tok
    wide = sources * rows
    group = rows // tok
    plane, slot = meta[2 * q_blocks], meta[2 * q_blocks + 1]
    range_blocks = 2 * planes
    dk_acc[...] = jnp.zeros_like(dk_acc)
    dv_acc[...] = jnp.zeros_like(dv_acc)
    if ends:
        loads = [pltpu.make_async_copy(near[n], kv.at[n], kv_sems.at[n]) for n in range(count)]
        for copy in loads:
            copy.start()
        for copy in loads:
            copy.wait()

    def over_range(r, _):
        lasts = [meta[2 * r + x] for x in range(2)]
        firsts = [meta[q_blocks + 2 * r + x] for x in range(2)]
        for x in range(2):
            stats = pkg[pl.ds(sources * (2 * r + x), sources), 2 * rows :, :]
            lse[x], delta[x] = stats_of(stats, sources, rows // 128)
            dq_acc[x] = jnp.zeros_like(dq_acc[x]) if starts else dq_before[2 * r + x]

        def queries(x):
            mine = pl.ds(sources * (2 * r + x), sources)
            q = pkg[mine, 0:rows, :].reshape(wide, 128)
            g = pkg[mine, rows : 2 * rows, :].reshape(wide, 128)
            return q, g, lse[x], delta[x]

        def keys(n, block, blocks):
            at = pl.ds(sources * block, sources * blocks)
            held = kv.at[n] if ends else near[0]
            return held[at, 0].reshape(blocks * BLK, 128), held[at, 1].reshape(blocks * BLK, 128)

        def add_keys(n, block, dk, dv):
            at = pl.ds(pl.multiple_of(block * BLK, BLK), dk.shape[0])
            dk_acc[n, at, :] += dk
            dv_acc[n, at, :] += dv

        def both(n, half):
            k, v = keys(n, 2 * half, 2)
            parts = [block_pair(*queries(x), k, v, group, scale, None) for x in range(2)]
            for x in range(2):
                dq_acc[x] += parts[x][0]
            add_keys(n, 2 * half, parts[0][1] + parts[1][1], parts[0][2] + parts[1][2])

        def one(x, n, block):
            dq_part, dk, dv = block_pair(*queries(x), *keys(n, block, 1), group, scale, None)
            dq_acc[x] += dq_part
            add_keys(n, block, dk, dv)

        def inner(t, _):
            half, n = lax.div(t, count), lax.rem(t, count)
            base = half * range_blocks + 2 * ((n + distances[0]) ^ plane)
            seen = [
                [(base + y >= firsts[x]) & (base + y <= lasts[x]) for y in range(2)] for x in range(2)
            ]
            every = seen[0][0] & seen[0][1] & seen[1][0] & seen[1][1]
            if ends:
                own = base == lasts[0]
                every = every & jnp.logical_not(own)

            @pl.when(every)
            def _():
                both(n, half)

            some = seen[0][0] | seen[0][1] | seen[1][0] | seen[1][1]
            some = some & jnp.logical_not(every)
            if ends:
                some = some & jnp.logical_not(own)

            @pl.when(some)
            def _():
                def single(at, _):
                    x, y = at // 2, at % 2
                    last, first = meta[2 * r + x], meta[q_blocks + 2 * r + x]

                    @pl.when((base + y >= first) & (base + y <= last))
                    def _():
                        one(x, n, 2 * half + y)

                    return 0

                lax.fori_loop(0, 4, single, 0)

            return 0

        lax.fori_loop(0, (r + 1) * count, inner, 0)
        if ends:
            n = distances.index(0)
            from_key = jnp.where(firsts[1] <= lasts[0], 0, BLK)
            dq_0, dk, dv = block_pair(*queries(0), *keys(n, 2 * r, 1), group, scale, (0, 0))
            dq_1, dk_1, dv_1 = block_pair(*queries(1), *keys(n, 2 * r, 2), group, scale, (BLK, from_key))
            dq_acc[0] += dq_0
            dq_acc[1] += dq_1
            add_keys(n, 2 * r, dk + dk_1[0:BLK], dv + dv_1[0:BLK])
            add_keys(n, 2 * r + 1, dk_1[BLK:], dv_1[BLK:])
        for x in range(2):
            if ends:
                done = (dq_acc[x] * scale).astype(jnp.bfloat16).reshape(sources, rows, 128)
                dq[pl.ds(sources * (2 * r + x), sources)] = done
            else:
                dq_out[0][2 * r + x] = dq_acc[x]
        return 0

    lax.fori_loop(0, 2, over_range, 0)
    if ends:
        stores = [
            pltpu.make_async_copy(dq.at[b * slots + (slot ^ d)], dq_out[d].at[b], out_sems.at[b, d])
            for b in range(2)
            for d in range(slots)
        ]
        for copy in stores:
            copy.start()
    if not ends:
        grads_out[0][:, 0] = (dk_acc[0] * scale).astype(jnp.bfloat16).reshape(team, tok, 128)
        grads_out[0][:, 1] = dv_acc[0].astype(jnp.bfloat16).reshape(team, tok, 128)
        return
    grad_stores = [pltpu.make_async_copy(grads.at[n], grads_out[n], grad_sems.at[n]) for n in range(count)]
    for n in reversed(range(count)):
        grads[n, :, 0] = (dk_acc[n] * scale).astype(jnp.bfloat16).reshape(team, tok, 128)
        grads[n, :, 1] = dv_acc[n].astype(jnp.bfloat16).reshape(team, tok, 128)
        grad_stores[n].start()
    for copy in stores + grad_stores:
        copy.wait()


VMEM = pl.BlockSpec(memory_space=pltpu.VMEM)
SMEM = pl.BlockSpec(memory_space=pltpu.SMEM)


def totals(shards, tok, wide, head_dim):
    return [
        pltpu.VMEM((shards * tok, head_dim), jnp.float32),
        pltpu.VMEM((shards * tok, head_dim), jnp.float32),
        pltpu.VMEM((wide, head_dim), jnp.float32),
    ]


def attention(meta, pkg, kv, rows, scale):
    shards, _, tok, head_dim = kv.shape
    team = pkg.shape[0]
    q_blocks = team * tok // BLK
    return pl.pallas_call(
        functools.partial(whole_kernel, rows=rows, tok=tok, q_blocks=q_blocks, scale=scale),
        out_shape=(
            jax.ShapeDtypeStruct((team, rows, head_dim), jnp.bfloat16),
            jax.ShapeDtypeStruct(kv.shape, jnp.bfloat16),
        ),
        in_specs=[SMEM, VMEM, VMEM],
        out_specs=(VMEM, VMEM),
        scratch_shapes=totals(shards, tok, rows * (BLK // tok), head_dim),
        compiler_params=pltpu.CompilerParams(vmem_limit_bytes=LIMIT),
        name="attention_grads",
    )(meta, pkg, kv)


def attention_part(meta, pkg, kv, distances, dq_before, rows, scale, planes):
    team, _, tok, head_dim = kv[0].shape
    slots = team // 2
    count = len(distances)
    q_blocks = team * tok // BLK
    wide = rows * (BLK // tok)
    scratch = [
        pltpu.VMEM((count,) + kv[0].shape, jnp.bfloat16),
        pltpu.VMEM((count,) + kv[0].shape, jnp.bfloat16),
        pltpu.VMEM((count, team * tok, head_dim), jnp.float32),
        pltpu.VMEM((count, team * tok, head_dim), jnp.float32),
        pltpu.VMEM((2, wide, head_dim), jnp.float32),
        pltpu.VMEM((2, 1, wide), jnp.float32),
        pltpu.VMEM((2, 1, wide), jnp.float32),
        pltpu.SemaphoreType.DMA((count,)),
        pltpu.SemaphoreType.DMA((count,)),
    ]
    hbm = pl.BlockSpec(memory_space=pltpu.HBM)
    ends = 0 in distances
    if ends:
        dq_shapes = (jax.ShapeDtypeStruct((2, rows, head_dim), jnp.bfloat16),) * slots
        dq_specs = (hbm,) * slots
        scratch += [pltpu.VMEM((team, rows, head_dim), jnp.bfloat16), pltpu.SemaphoreType.DMA((2, slots))]
    else:
        dq_shapes = (jax.ShapeDtypeStruct((q_blocks, wide, head_dim), jnp.float32),)
        dq_specs = (VMEM,)
    before = [] if dq_before is None else [dq_before]
    pairs = q_blocks * count
    out = pl.pallas_call(
        functools.partial(
            planes_kernel, rows=rows, tok=tok, q_blocks=q_blocks, scale=scale, distances=distances, planes=planes
        ),
        out_shape=dq_shapes + (jax.ShapeDtypeStruct(kv[0].shape, jnp.bfloat16),) * count,
        in_specs=[SMEM, VMEM] + [hbm if ends else VMEM] * count + [VMEM] * len(before),
        out_specs=dq_specs + (hbm if ends else VMEM,) * count,
        scratch_shapes=scratch,
        compiler_params=pltpu.CompilerParams(vmem_limit_bytes=PART_LIMIT),
        cost_estimate=pl.CostEstimate(
            flops=pairs * 10 * BLK * wide * head_dim,
            bytes_accessed=4 * 1024 * 1024,
            transcendentals=pairs * BLK * wide,
        ),
        name="attention_" + "_".join(str(d) for d in distances),
    )(meta, pkg, *kv, *before)
    dq, grads = out[:-count], out[-count:]
    return (dq if ends else dq[0]), grads


def sum_kernel(*refs):
    *terms, out = refs
    out[...] = sum(x[...].astype(jnp.float32) for x in terms)


def sum_of(*terms):
    return pl.pallas_call(
        sum_kernel,
        out_shape=jax.ShapeDtypeStruct(terms[0].shape, jnp.float32),
        in_specs=[VMEM] * len(terms),
        out_specs=VMEM,
        compiler_params=pltpu.CompilerParams(vmem_limit_bytes=SMALL_LIMIT),
        name="sum_dkv",
    )(*terms)


def place_dq_kernel(place, *refs):
    *arrived, swapped, out = refs
    slots = len(arrived)
    core, slot = place[0], place[1]
    for d, blocks in enumerate(arrived):
        out[:, core * slots + (slot ^ d)] = blocks[core]
        out[:, (1 - core) * slots + (slot ^ d)] = swapped[d]


def place_dq(place, arrived, swapped, tok):
    slots, rows, head_dim = swapped.shape
    fan = rows // tok
    out = pl.pallas_call(
        place_dq_kernel,
        out_shape=jax.ShapeDtypeStruct((tok, 2 * slots, fan, head_dim), jnp.bfloat16),
        in_specs=[SMEM] + [VMEM] * (slots + 1),
        out_specs=VMEM,
        compiler_params=pltpu.CompilerParams(vmem_limit_bytes=SMALL_LIMIT),
        name="place_dq",
    )(place, *[x.reshape(2, tok, fan, head_dim) for x in arrived], swapped.reshape(slots, tok, fan, head_dim))
    return out.reshape(tok, 2 * slots * fan, head_dim)


def place_dkv_kernel(parts, dk, dv, wide):
    halves, kv_heads = parts.shape[:2]
    for n, out in enumerate((dk, dv)):
        for h in range(kv_heads):
            wide[:, h, :] = sum(parts[p, h, n].astype(jnp.float32) for p in range(halves))
        out[...] = wide[...].astype(jnp.bfloat16)


def place_dkv(parts):
    _, kv_heads, _, tok, head_dim = parts.shape
    shape = (tok, kv_heads, head_dim)
    dk, dv = pl.pallas_call(
        place_dkv_kernel,
        out_shape=(jax.ShapeDtypeStruct(shape, jnp.bfloat16),) * 2,
        in_specs=[VMEM],
        out_specs=(VMEM, VMEM),
        scratch_shapes=[pltpu.VMEM(shape, jnp.float32)],
        compiler_params=pltpu.CompilerParams(vmem_limit_bytes=SMALL_LIMIT),
        name="place_dkv",
    )(parts)
    return dk, dv


def pieces(x):
    high = lax.reduce_precision(x, 8, 7)
    return [part.astype(jnp.bfloat16) for part in (high, x - high)]


def add(*terms):
    return sum(x.astype(jnp.float32) for x in terms).astype(jnp.bfloat16)


def dq_by_token(dq, tok, fan):
    kv_heads, _, head_dim = dq.shape
    return dq.reshape(kv_heads, tok, fan, head_dim).transpose(1, 0, 2, 3).reshape(tok, kv_heads * fan, head_dim)


def dkv_by_token(parts):
    dkv = parts.astype(jnp.float32).sum(axis=0).astype(jnp.bfloat16).transpose(1, 2, 0, 3)
    return dkv[0], dkv[1]


def per_device(queries, keys, values, outputs, out_grads, log_norms, block_doc):
    tok, heads, head_dim = queries.shape
    kv_heads = keys.shape[1]
    fan = heads // kv_heads
    n_ctx, n_head = lax.axis_size("ctx"), lax.axis_size("head")
    slots = kv_heads // 2
    planes = n_head // slots
    rows = tok * fan
    scale = head_dim**-0.5
    ctx, head = lax.axis_index("ctx"), lax.axis_index("head")
    both = ("ctx", "head")
    teams = [
        [(2 * c + b) * n_head + z * slots + r for b in range(2) for r in range(slots)]
        for c in range(n_ctx // 2)
        for z in range(planes)
    ]
    pairs = [
        [(2 * c + b) * n_head + h for b in range(2) for h in range(n_head)]
        for c in range(n_ctx // 2)
    ]

    by_plane = n_ctx == 2 and planes == 4 and slots * tok == 2 * BLK

    def across(x, distance):
        step = distance * slots
        return lax.ppermute(x, "head", [(h, h ^ step) for h in range(n_head)])

    kv = jnp.stack([keys, values], axis=0).transpose(2, 0, 1, 3)
    if by_plane:
        kv = lax.all_to_all(kv, both, 0, 0, axis_index_groups=teams, tiled=True)
        second, first = across(kv, 2), across(kv, 1)
        kv = (kv, first, second, across(second, 1))
    else:
        kv = kv.reshape(2, 1, slots, 2, tok, head_dim)
        kv = jnp.broadcast_to(kv, (2, planes, slots, 2, tok, head_dim))
        kv = kv.reshape(2 * n_head, 2, tok, head_dim)
        kv = lax.all_to_all(kv, both, 0, 0, axis_index_groups=pairs, tiled=True)

    def by_group(x):
        return x.reshape(tok, kv_heads, fan, head_dim).transpose(1, 0, 2, 3).reshape(kv_heads, rows, head_dim)

    deltas = jnp.sum(out_grads.astype(jnp.float32) * outputs.astype(jnp.float32), axis=-1)
    stats = jnp.stack(pieces(log_norms) + pieces(deltas), axis=0)
    stats = stats.reshape(4, tok, kv_heads, fan).transpose(2, 0, 1, 3)
    stats = stats.reshape(kv_heads, 4 * rows // 128, 128)
    pkg = jnp.concatenate([by_group(queries), by_group(out_grads), stats], axis=1)
    pkg = lax.all_to_all(pkg, both, 0, 0, axis_index_groups=teams, tiled=True)

    pair, plane = lax.div(ctx, 2), lax.div(head, slots)
    range_blocks = n_head * tok // BLK
    team_blocks = slots * tok // BLK
    at = jnp.stack(
        [(2 * pair + b) * range_blocks + plane * team_blocks + j for b in range(2) for j in range(team_blocks)]
    )
    first_block = jnp.sum(block_doc[None, :] < block_doc[at][:, None], axis=1, dtype=jnp.int32)
    ranges_before = 1 if n_ctx > 2 else 0
    base = (2 * pair - ranges_before) * range_blocks
    meta = jnp.concatenate([at - base, first_block - base, plane[None], lax.rem(head, slots)[None]]).astype(jnp.int32)

    if by_plane:
        def part(distances, dq_before):
            return attention_part(
                meta, pkg, [kv[d] for d in distances], distances, dq_before, rows, scale, planes
            )

        dq, (grads_3,) = part((3,), None)
        relayed = across(grads_3, 1)
        dq, (grads_0, grads_1, grads_2) = part((0, 1, 2), dq)
        far = add(grads_2, relayed)
        far, grads_1, *dq = lax.optimization_barrier((far, grads_1, *dq))
        far = across(far, 2)
        close = across(grads_1, 1)
        dq = [lax.ppermute(x, "head", [(h, h ^ d) for h in range(n_head)]) if d else x for d, x in enumerate(dq)]
        dkv = add(sum_of(grads_0, close), far)
        dkv, *dq = lax.optimization_barrier((dkv, *dq))
        dkv = lax.all_to_all(dkv, both, 0, 0, axis_index_groups=teams, tiled=True)
        other = jnp.where(ctx == 0, jnp.stack([x[1] for x in dq]), jnp.stack([x[0] for x in dq]))
        swapped = lax.ppermute(other, "ctx", [(0, 1), (1, 0)])
        dq = place_dq(jnp.stack([ctx, lax.rem(head, slots)]), dq, swapped, tok)
        dkv, dq = lax.optimization_barrier((dkv, dq))
        return (dq,) + place_dkv(dkv[None])

    if ranges_before:
        prior = lax.ppermute(kv[n_head:], "ctx", [(c, c + 2) for c in range(n_ctx - 2)])
        kv = jnp.concatenate([prior, kv], axis=0)
    dq, dkv = attention(meta, pkg, kv, rows, scale)
    if ranges_before:
        later = lax.ppermute(dkv[:n_head], "ctx", [(c + 2, c) for c in range(n_ctx - 2)])
        dkv = jnp.concatenate([dkv[n_head : 2 * n_head], add(dkv[2 * n_head :], later)], axis=0)

    dkv = lax.all_to_all(dkv, both, 0, 0, axis_index_groups=pairs, tiled=True)
    dq = lax.all_to_all(dq, both, 0, 0, axis_index_groups=teams, tiled=True)
    dkv = dkv.reshape(2, planes, slots, 2, tok, head_dim).transpose(1, 0, 2, 3, 4, 5)
    return (dq_by_token(dq, tok, fan),) + dkv_by_token(dkv.reshape(planes, kv_heads, 2, tok, head_dim))


def solution(mesh):
    tokens = P(("ctx", "head"), None, None)
    return jax.shard_map(
        per_device,
        mesh=mesh,
        in_specs=(tokens,) * 5 + (P(("ctx", "head"), None), P()),
        out_specs=(tokens,) * 3,
        check_vma=False,
    )
```

```python
import functools

import jax
import jax.numpy as jnp
from jax import lax
from jax.experimental import pallas as pl
from jax.experimental.pallas import tpu as pltpu
from jax.sharding import PartitionSpec as P

BLK = 128
LOG2E = 1.4426950408889634
LIMIT = 56 * 1024 * 1024
PART_LIMIT = 12 * 1024 * 1024
SMALL_LIMIT = 6 * 1024 * 1024


def stats_of(stats, sources, chunks):
    stats = stats.astype(jnp.float32)
    sums = (
        stats[:, base : base + chunks] + stats[:, base + chunks : base + 2 * chunks]
        for base in (0, 2 * chunks)
    )
    lse, delta = (
        jnp.concatenate([x[s, c : c + 1, :] for s in range(sources) for c in range(chunks)], axis=1)
        for x in sums
    )
    return lse * LOG2E, delta


def block_pair(q, g, lse, delta, k, v, group, scale, mask):
    s = lax.dot_general(k, q, (((1,), (1,)), ((), ())), preferred_element_type=jnp.float32)
    p = jnp.exp2(s * (scale * LOG2E) - lse)
    if mask is not None:
        lead, from_key = mask
        key_at = lax.broadcasted_iota(jnp.int32, p.shape, 0)
        query_at = lax.broadcasted_iota(jnp.int32, p.shape, 1) // group + lead
        p = jnp.where((query_at >= key_at) & (key_at >= from_key), p, 0.0)
    dp = lax.dot_general(v, g, (((1,), (1,)), ((), ())), preferred_element_type=jnp.float32)
    ds = (p * (dp - delta)).astype(jnp.bfloat16)
    dv = jnp.dot(p.astype(jnp.bfloat16), g, preferred_element_type=jnp.float32)
    dk = jnp.dot(ds, q, preferred_element_type=jnp.float32)
    dq = lax.dot_general(ds, k, (((0,), (0,)), ((), ())), preferred_element_type=jnp.float32)
    return dq, dk, dv


def whole_kernel(meta, pkg, kv, dq, dkv, dk_acc, dv_acc, dq_acc, *, rows, tok, q_blocks, scale):
    sources = BLK // tok
    wide = sources * rows
    dk_acc[...] = jnp.zeros_like(dk_acc)
    dv_acc[...] = jnp.zeros_like(dv_acc)

    def over_queries(i, _):
        last, first = meta[i], meta[q_blocks + i]
        mine = pl.ds(sources * i, sources)
        q = pkg[mine, 0:rows, :].reshape(wide, 128)
        g = pkg[mine, rows : 2 * rows, :].reshape(wide, 128)
        lse, delta = stats_of(pkg[mine, 2 * rows :, :], sources, rows // 128)
        dq_acc[...] = jnp.zeros_like(dq_acc)

        def step(j, masked):
            k = kv[pl.ds(sources * j, sources), 0].reshape(BLK, 128)
            v = kv[pl.ds(sources * j, sources), 1].reshape(BLK, 128)
            dq_part, dk, dv = block_pair(q, g, lse, delta, k, v, rows // tok, scale, (0, 0) if masked else None)
            at = pl.ds(pl.multiple_of(j * BLK, BLK), BLK)
            dv_acc[at, :] += dv
            dk_acc[at, :] += dk
            dq_acc[...] += dq_part

        def inner(j, _):
            step(j, False)
            return 0

        lax.fori_loop(first, last, inner, 0)
        step(last, True)
        dq[mine] = (dq_acc[...] * scale).astype(jnp.bfloat16).reshape(sources, rows, 128)
        return 0

    lax.fori_loop(0, q_blocks, over_queries, 0)
    shards = dkv.shape[0]
    dkv[:, 0] = (dk_acc[...] * scale).astype(jnp.bfloat16).reshape(shards, tok, 128)
    dkv[:, 1] = dv_acc[...].astype(jnp.bfloat16).reshape(shards, tok, 128)


def planes_kernel(meta, pkg, *refs, rows, tok, q_blocks, scale, distances, planes):
    team = pkg.shape[0]
    slots = team // 2
    count = len(distances)
    starts, ends = planes - 1 in distances, 0 in distances
    near, refs = refs[:count], refs[count:]
    if not starts:
        dq_before, refs = refs[0], refs[1:]
    outs = slots if ends else 1
    dq_out, grads_out, refs = refs[:outs], refs[outs : outs + count], refs[outs + count :]
    kv, grads, dk_acc, dv_acc, dq_acc, lse, delta, kv_sems, grad_sems = refs[:9]
    if ends:
        dq, out_sems = refs[9:]
    sources = BLK // tok
    wide = sources * rows
    group = rows // tok
    plane, slot = meta[2 * q_blocks], meta[2 * q_blocks + 1]
    range_blocks = 2 * planes
    dk_acc[...] = jnp.zeros_like(dk_acc)
    dv_acc[...] = jnp.zeros_like(dv_acc)
    if ends:
        loads = [pltpu.make_async_copy(near[n], kv.at[n], kv_sems.at[n]) for n in range(count)]
        for copy in loads:
            copy.start()
        for copy in loads:
            copy.wait()

    def over_range(r, _):
        lasts = [meta[2 * r + x] for x in range(2)]
        firsts = [meta[q_blocks + 2 * r + x] for x in range(2)]
        for x in range(2):
            stats = pkg[pl.ds(sources * (2 * r + x), sources), 2 * rows :, :]
            lse[x], delta[x] = stats_of(stats, sources, rows // 128)
            dq_acc[x] = jnp.zeros_like(dq_acc[x]) if starts else dq_before[2 * r + x]

        def queries(x):
            mine = pl.ds(sources * (2 * r + x), sources)
            q = pkg[mine, 0:rows, :].reshape(wide, 128)
            g = pkg[mine, rows : 2 * rows, :].reshape(wide, 128)
            return q, g, lse[x], delta[x]

        def keys(n, block, blocks):
            at = pl.ds(sources * block, sources * blocks)
            held = kv.at[n] if ends else near[0]
            return held[at, 0].reshape(blocks * BLK, 128), held[at, 1].reshape(blocks * BLK, 128)

        def add_keys(n, block, dk, dv):
            at = pl.ds(pl.multiple_of(block * BLK, BLK), dk.shape[0])
            dk_acc[n, at, :] += dk
            dv_acc[n, at, :] += dv

        def both(n, half):
            k, v = keys(n, 2 * half, 2)
            parts = [block_pair(*queries(x), k, v, group, scale, None) for x in range(2)]
            for x in range(2):
                dq_acc[x] += parts[x][0]
            add_keys(n, 2 * half, parts[0][1] + parts[1][1], parts[0][2] + parts[1][2])

        def one(x, n, block):
            dq_part, dk, dv = block_pair(*queries(x), *keys(n, block, 1), group, scale, None)
            dq_acc[x] += dq_part
            add_keys(n, block, dk, dv)

        def inner(t, _):
            half, n = lax.div(t, count), lax.rem(t, count)
            base = half * range_blocks + 2 * ((n + distances[0]) ^ plane)
            seen = [
                [(base + y >= firsts[x]) & (base + y <= lasts[x]) for y in range(2)] for x in range(2)
            ]
            every = seen[0][0] & seen[0][1] & seen[1][0] & seen[1][1]
            if ends:
                own = base == lasts[0]
                every = every & jnp.logical_not(own)

            @pl.when(every)
            def _():
                both(n, half)

            some = seen[0][0] | seen[0][1] | seen[1][0] | seen[1][1]
            some = some & jnp.logical_not(every)
            if ends:
                some = some & jnp.logical_not(own)

            @pl.when(some)
            def _():
                def single(at, _):
                    x, y = at // 2, at % 2
                    last, first = meta[2 * r + x], meta[q_blocks + 2 * r + x]

                    @pl.when((base + y >= first) & (base + y <= last))
                    def _():
                        one(x, n, 2 * half + y)

                    return 0

                lax.fori_loop(0, 4, single, 0)

            return 0

        lax.fori_loop(0, (r + 1) * count, inner, 0)
        if ends:
            n = distances.index(0)
            from_key = jnp.where(firsts[1] <= lasts[0], 0, BLK)
            dq_0, dk, dv = block_pair(*queries(0), *keys(n, 2 * r, 1), group, scale, (0, 0))
            dq_1, dk_1, dv_1 = block_pair(*queries(1), *keys(n, 2 * r, 2), group, scale, (BLK, from_key))
            dq_acc[0] += dq_0
            dq_acc[1] += dq_1
            add_keys(n, 2 * r, dk + dk_1[0:BLK], dv + dv_1[0:BLK])
            add_keys(n, 2 * r + 1, dk_1[BLK:], dv_1[BLK:])
        for x in range(2):
            if ends:
                done = (dq_acc[x] * scale).astype(jnp.bfloat16).reshape(sources, rows, 128)
                dq[pl.ds(sources * (2 * r + x), sources)] = done
            else:
                dq_out[0][2 * r + x] = dq_acc[x]
        return 0

    lax.fori_loop(0, 2, over_range, 0)
    if ends:
        stores = [
            pltpu.make_async_copy(dq.at[b * slots + (slot ^ d)], dq_out[d].at[b], out_sems.at[b, d])
            for b in range(2)
            for d in range(slots)
        ]
        for copy in stores:
            copy.start()
    if not ends:
        grads_out[0][:, 0] = (dk_acc[0] * scale).astype(jnp.bfloat16).reshape(team, tok, 128)
        grads_out[0][:, 1] = dv_acc[0].astype(jnp.bfloat16).reshape(team, tok, 128)
        return
    grad_stores = [pltpu.make_async_copy(grads.at[n], grads_out[n], grad_sems.at[n]) for n in range(count)]
    for n in reversed(range(count)):
        grads[n, :, 0] = (dk_acc[n] * scale).astype(jnp.bfloat16).reshape(team, tok, 128)
        grads[n, :, 1] = dv_acc[n].astype(jnp.bfloat16).reshape(team, tok, 128)
        grad_stores[n].start()
    for copy in stores + grad_stores:
        copy.wait()


VMEM = pl.BlockSpec(memory_space=pltpu.VMEM)
SMEM = pl.BlockSpec(memory_space=pltpu.SMEM)


def totals(shards, tok, wide, head_dim):
    return [
        pltpu.VMEM((shards * tok, head_dim), jnp.float32),
        pltpu.VMEM((shards * tok, head_dim), jnp.float32),
        pltpu.VMEM((wide, head_dim), jnp.float32),
    ]


def attention(meta, pkg, kv, rows, scale):
    shards, _, tok, head_dim = kv.shape
    team = pkg.shape[0]
    q_blocks = team * tok // BLK
    return pl.pallas_call(
        functools.partial(whole_kernel, rows=rows, tok=tok, q_blocks=q_blocks, scale=scale),
        out_shape=(
            jax.ShapeDtypeStruct((team, rows, head_dim), jnp.bfloat16),
            jax.ShapeDtypeStruct(kv.shape, jnp.bfloat16),
        ),
        in_specs=[SMEM, VMEM, VMEM],
        out_specs=(VMEM, VMEM),
        scratch_shapes=totals(shards, tok, rows * (BLK // tok), head_dim),
        compiler_params=pltpu.CompilerParams(vmem_limit_bytes=LIMIT),
        name="attention_grads",
    )(meta, pkg, kv)


def attention_part(meta, pkg, kv, distances, dq_before, rows, scale, planes):
    team, _, tok, head_dim = kv[0].shape
    slots = team // 2
    count = len(distances)
    q_blocks = team * tok // BLK
    wide = rows * (BLK // tok)
    scratch = [
        pltpu.VMEM((count,) + kv[0].shape, jnp.bfloat16),
        pltpu.VMEM((count,) + kv[0].shape, jnp.bfloat16),
        pltpu.VMEM((count, team * tok, head_dim), jnp.float32),
        pltpu.VMEM((count, team * tok, head_dim), jnp.float32),
        pltpu.VMEM((2, wide, head_dim), jnp.float32),
        pltpu.VMEM((2, 1, wide), jnp.float32),
        pltpu.VMEM((2, 1, wide), jnp.float32),
        pltpu.SemaphoreType.DMA((count,)),
        pltpu.SemaphoreType.DMA((count,)),
    ]
    hbm = pl.BlockSpec(memory_space=pltpu.HBM)
    ends = 0 in distances
    if ends:
        dq_shapes = (jax.ShapeDtypeStruct((2, rows, head_dim), jnp.bfloat16),) * slots
        dq_specs = (hbm,) * slots
        scratch += [pltpu.VMEM((team, rows, head_dim), jnp.bfloat16), pltpu.SemaphoreType.DMA((2, slots))]
    else:
        dq_shapes = (jax.ShapeDtypeStruct((q_blocks, wide, head_dim), jnp.float32),)
        dq_specs = (VMEM,)
    before = [] if dq_before is None else [dq_before]
    pairs = q_blocks * count
    out = pl.pallas_call(
        functools.partial(
            planes_kernel, rows=rows, tok=tok, q_blocks=q_blocks, scale=scale, distances=distances, planes=planes
        ),
        out_shape=dq_shapes + (jax.ShapeDtypeStruct(kv[0].shape, jnp.bfloat16),) * count,
        in_specs=[SMEM, VMEM] + [hbm if ends else VMEM] * count + [VMEM] * len(before),
        out_specs=dq_specs + (hbm if ends else VMEM,) * count,
        scratch_shapes=scratch,
        compiler_params=pltpu.CompilerParams(vmem_limit_bytes=PART_LIMIT),
        cost_estimate=pl.CostEstimate(
            flops=pairs * 10 * BLK * wide * head_dim,
            bytes_accessed=4 * 1024 * 1024,
            transcendentals=pairs * BLK * wide,
        ),
        name="attention_" + "_".join(str(d) for d in distances),
    )(meta, pkg, *kv, *before)
    dq, grads = out[:-count], out[-count:]
    return (dq if ends else dq[0]), grads


def sum_kernel(*refs):
    *terms, out = refs
    out[...] = sum(x[...].astype(jnp.float32) for x in terms)


def sum_of(*terms):
    return pl.pallas_call(
        sum_kernel,
        out_shape=jax.ShapeDtypeStruct(terms[0].shape, jnp.float32),
        in_specs=[VMEM] * len(terms),
        out_specs=VMEM,
        compiler_params=pltpu.CompilerParams(vmem_limit_bytes=SMALL_LIMIT),
        name="sum_dkv",
    )(*terms)


def place_dq_kernel(place, *refs):
    *arrived, swapped, out = refs
    slots = len(arrived)
    core, slot = place[0], place[1]
    for d, blocks in enumerate(arrived):
        out[:, core * slots + (slot ^ d)] = blocks[core]
        out[:, (1 - core) * slots + (slot ^ d)] = swapped[d]


def place_dq(place, arrived, swapped, tok):
    slots, rows, head_dim = swapped.shape
    fan = rows // tok
    out = pl.pallas_call(
        place_dq_kernel,
        out_shape=jax.ShapeDtypeStruct((tok, 2 * slots, fan, head_dim), jnp.bfloat16),
        in_specs=[SMEM] + [VMEM] * (slots + 1),
        out_specs=VMEM,
        compiler_params=pltpu.CompilerParams(vmem_limit_bytes=SMALL_LIMIT),
        name="place_dq",
    )(place, *[x.reshape(2, tok, fan, head_dim) for x in arrived], swapped.reshape(slots, tok, fan, head_dim))
    return out.reshape(tok, 2 * slots * fan, head_dim)


def place_dkv_kernel(parts, dk, dv, wide):
    halves, kv_heads = parts.shape[:2]
    for n, out in enumerate((dk, dv)):
        for h in range(kv_heads):
            wide[:, h, :] = sum(parts[p, h, n].astype(jnp.float32) for p in range(halves))
        out[...] = wide[...].astype(jnp.bfloat16)


def place_dkv(parts):
    _, kv_heads, _, tok, head_dim = parts.shape
    shape = (tok, kv_heads, head_dim)
    dk, dv = pl.pallas_call(
        place_dkv_kernel,
        out_shape=(jax.ShapeDtypeStruct(shape, jnp.bfloat16),) * 2,
        in_specs=[VMEM],
        out_specs=(VMEM, VMEM),
        scratch_shapes=[pltpu.VMEM(shape, jnp.float32)],
        compiler_params=pltpu.CompilerParams(vmem_limit_bytes=SMALL_LIMIT),
        name="place_dkv",
    )(parts)
    return dk, dv


def pieces(x):
    high = lax.reduce_precision(x, 8, 7)
    return [part.astype(jnp.bfloat16) for part in (high, x - high)]


def add(*terms):
    return sum(x.astype(jnp.float32) for x in terms).astype(jnp.bfloat16)


def dq_by_token(dq, tok, fan):
    kv_heads, _, head_dim = dq.shape
    return dq.reshape(kv_heads, tok, fan, head_dim).transpose(1, 0, 2, 3).reshape(tok, kv_heads * fan, head_dim)


def dkv_by_token(parts):
    dkv = parts.astype(jnp.float32).sum(axis=0).astype(jnp.bfloat16).transpose(1, 2, 0, 3)
    return dkv[0], dkv[1]


def per_device(queries, keys, values, outputs, out_grads, log_norms, block_doc):
    tok, heads, head_dim = queries.shape
    kv_heads = keys.shape[1]
    fan = heads // kv_heads
    n_ctx, n_head = lax.axis_size("ctx"), lax.axis_size("head")
    slots = kv_heads // 2
    planes = n_head // slots
    rows = tok * fan
    scale = head_dim**-0.5
    ctx, head = lax.axis_index("ctx"), lax.axis_index("head")
    both = ("ctx", "head")
    teams = [
        [(2 * c + b) * n_head + z * slots + r for b in range(2) for r in range(slots)]
        for c in range(n_ctx // 2)
        for z in range(planes)
    ]
    pairs = [
        [(2 * c + b) * n_head + h for b in range(2) for h in range(n_head)]
        for c in range(n_ctx // 2)
    ]

    by_plane = n_ctx == 2 and planes == 4 and slots * tok == 2 * BLK

    def across(x, distance):
        step = distance * slots
        return lax.ppermute(x, "head", [(h, h ^ step) for h in range(n_head)])

    kv = jnp.stack([keys, values], axis=0).transpose(2, 0, 1, 3)
    if by_plane:
        kv = lax.all_to_all(kv, both, 0, 0, axis_index_groups=teams, tiled=True)
        second, first = across(kv, 2), across(kv, 1)
        kv = (kv, first, second, across(second, 1))
    else:
        kv = kv.reshape(2, 1, slots, 2, tok, head_dim)
        kv = jnp.broadcast_to(kv, (2, planes, slots, 2, tok, head_dim))
        kv = kv.reshape(2 * n_head, 2, tok, head_dim)
        kv = lax.all_to_all(kv, both, 0, 0, axis_index_groups=pairs, tiled=True)

    def by_group(x):
        return x.reshape(tok, kv_heads, fan, head_dim).transpose(1, 0, 2, 3).reshape(kv_heads, rows, head_dim)

    deltas = jnp.sum(out_grads.astype(jnp.float32) * outputs.astype(jnp.float32), axis=-1)
    stats = jnp.stack(pieces(log_norms) + pieces(deltas), axis=0)
    stats = stats.reshape(4, tok, kv_heads, fan).transpose(2, 0, 1, 3)
    stats = stats.reshape(kv_heads, 4 * rows // 128, 128)
    pkg = jnp.concatenate([by_group(queries), by_group(out_grads), stats], axis=1)
    pkg = lax.all_to_all(pkg, both, 0, 0, axis_index_groups=teams, tiled=True)

    pair, plane = lax.div(ctx, 2), lax.div(head, slots)
    range_blocks = n_head * tok // BLK
    team_blocks = slots * tok // BLK
    at = jnp.stack(
        [(2 * pair + b) * range_blocks + plane * team_blocks + j for b in range(2) for j in range(team_blocks)]
    )
    first_block = jnp.sum(block_doc[None, :] < block_doc[at][:, None], axis=1, dtype=jnp.int32)
    ranges_before = 1 if n_ctx > 2 else 0
    base = (2 * pair - ranges_before) * range_blocks
    meta = jnp.concatenate([at - base, first_block - base, plane[None], lax.rem(head, slots)[None]]).astype(jnp.int32)

    if by_plane:
        def part(distances, dq_before):
            return attention_part(
                meta, pkg, [kv[d] for d in distances], distances, dq_before, rows, scale, planes
            )

        dq, (grads_3,) = part((3,), None)
        relayed = across(grads_3, 1)
        dq, (grads_0, grads_1, grads_2) = part((0, 1, 2), dq)
        far = add(grads_2, relayed)
        far, *dq = lax.optimization_barrier((far, *dq))
        far = across(far, 2)
        close = across(grads_1, 1)
        dq = [lax.ppermute(x, "head", [(h, h ^ d) for h in range(n_head)]) if d else x for d, x in enumerate(dq)]
        dkv = sum_of(grads_0, far)
        dkv, *dq = lax.optimization_barrier((dkv, *dq))
        dkv, close = lax.optimization_barrier((dkv, close))
        dkv = add(dkv, close)
        dkv = lax.all_to_all(dkv, both, 0, 0, axis_index_groups=teams, tiled=True)
        other = jnp.where(ctx == 0, jnp.stack([x[1] for x in dq]), jnp.stack([x[0] for x in dq]))
        swapped = lax.ppermute(other, "ctx", [(0, 1), (1, 0)])
        dq = place_dq(jnp.stack([ctx, lax.rem(head, slots)]), dq, swapped, tok)
        dkv, dq = lax.optimization_barrier((dkv, dq))
        return (dq,) + place_dkv(dkv[None])

    if ranges_before:
        prior = lax.ppermute(kv[n_head:], "ctx", [(c, c + 2) for c in range(n_ctx - 2)])
        kv = jnp.concatenate([prior, kv], axis=0)
    dq, dkv = attention(meta, pkg, kv, rows, scale)
    if ranges_before:
        later = lax.ppermute(dkv[:n_head], "ctx", [(c + 2, c) for c in range(n_ctx - 2)])
        dkv = jnp.concatenate([dkv[n_head : 2 * n_head], add(dkv[2 * n_head :], later)], axis=0)

    dkv = lax.all_to_all(dkv, both, 0, 0, axis_index_groups=pairs, tiled=True)
    dq = lax.all_to_all(dq, both, 0, 0, axis_index_groups=teams, tiled=True)
    dkv = dkv.reshape(2, planes, slots, 2, tok, head_dim).transpose(1, 0, 2, 3, 4, 5)
    return (dq_by_token(dq, tok, fan),) + dkv_by_token(dkv.reshape(planes, kv_heads, 2, tok, head_dim))


def solution(mesh):
    tokens = P(("ctx", "head"), None, None)
    return jax.shard_map(
        per_device,
        mesh=mesh,
        in_specs=(tokens,) * 5 + (P(("ctx", "head"), None), P()),
        out_specs=(tokens,) * 3,
        check_vma=False,
    )
```

```python
import functools

import jax
import jax.numpy as jnp
from jax import lax
from jax.experimental import pallas as pl
from jax.experimental.pallas import tpu as pltpu
from jax.sharding import PartitionSpec as P

BLK = 128
LOG2E = 1.4426950408889634
LIMIT = 56 * 1024 * 1024
PART_LIMIT = 20 * 1024 * 1024
SMALL_LIMIT = 6 * 1024 * 1024


def stats_of(stats, sources, chunks):
    stats = stats.astype(jnp.float32)
    sums = (
        stats[:, base : base + chunks] + stats[:, base + chunks : base + 2 * chunks]
        for base in (0, 2 * chunks)
    )
    lse, delta = (
        jnp.concatenate([x[s, c : c + 1, :] for s in range(sources) for c in range(chunks)], axis=1)
        for x in sums
    )
    return lse * LOG2E, delta


def block_pair(q, g, lse, delta, k, v, group, scale, mask):
    s = lax.dot_general(k, q, (((1,), (1,)), ((), ())), preferred_element_type=jnp.float32)
    p = jnp.exp2(s * (scale * LOG2E) - lse)
    if mask is not None:
        lead, from_key = mask
        key_at = lax.broadcasted_iota(jnp.int32, p.shape, 0)
        query_at = lax.broadcasted_iota(jnp.int32, p.shape, 1) // group + lead
        p = jnp.where((query_at >= key_at) & (key_at >= from_key), p, 0.0)
    dp = lax.dot_general(v, g, (((1,), (1,)), ((), ())), preferred_element_type=jnp.float32)
    ds = (p * (dp - delta)).astype(jnp.bfloat16)
    dv = jnp.dot(p.astype(jnp.bfloat16), g, preferred_element_type=jnp.float32)
    dk = jnp.dot(ds, q, preferred_element_type=jnp.float32)
    dq = lax.dot_general(ds, k, (((0,), (0,)), ((), ())), preferred_element_type=jnp.float32)
    return dq, dk, dv


def whole_kernel(meta, pkg, kv, dq, dkv, dk_acc, dv_acc, dq_acc, *, rows, tok, q_blocks, scale):
    sources = BLK // tok
    wide = sources * rows
    dk_acc[...] = jnp.zeros_like(dk_acc)
    dv_acc[...] = jnp.zeros_like(dv_acc)

    def over_queries(i, _):
        last, first = meta[i], meta[q_blocks + i]
        mine = pl.ds(sources * i, sources)
        q = pkg[mine, 0:rows, :].reshape(wide, 128)
        g = pkg[mine, rows : 2 * rows, :].reshape(wide, 128)
        lse, delta = stats_of(pkg[mine, 2 * rows :, :], sources, rows // 128)
        dq_acc[...] = jnp.zeros_like(dq_acc)

        def step(j, masked):
            k = kv[pl.ds(sources * j, sources), 0].reshape(BLK, 128)
            v = kv[pl.ds(sources * j, sources), 1].reshape(BLK, 128)
            dq_part, dk, dv = block_pair(q, g, lse, delta, k, v, rows // tok, scale, (0, 0) if masked else None)
            at = pl.ds(pl.multiple_of(j * BLK, BLK), BLK)
            dv_acc[at, :] += dv
            dk_acc[at, :] += dk
            dq_acc[...] += dq_part

        def inner(j, _):
            step(j, False)
            return 0

        lax.fori_loop(first, last, inner, 0)
        step(last, True)
        dq[mine] = (dq_acc[...] * scale).astype(jnp.bfloat16).reshape(sources, rows, 128)
        return 0

    lax.fori_loop(0, q_blocks, over_queries, 0)
    shards = dkv.shape[0]
    dkv[:, 0] = (dk_acc[...] * scale).astype(jnp.bfloat16).reshape(shards, tok, 128)
    dkv[:, 1] = dv_acc[...].astype(jnp.bfloat16).reshape(shards, tok, 128)


def planes_kernel(meta, pkg, *refs, rows, tok, q_blocks, scale, distances, planes):
    team = pkg.shape[0]
    slots = team // 2
    count = len(distances)
    starts, ends = planes - 1 in distances, 0 in distances
    near, refs = refs[:count], refs[count:]
    if not starts:
        dq_before, refs = refs[0], refs[1:]
    outs = slots if ends else 1
    dq_out, grads_out, refs = refs[:outs], refs[outs : outs + count], refs[outs + count :]
    kv, grads, dk_acc, dv_acc, dq_acc, lse, delta, kv_sems, grad_sems = refs[:9]
    if ends:
        dq, out_sems = refs[9:]
    sources = BLK // tok
    wide = sources * rows
    group = rows // tok
    plane, slot = meta[2 * q_blocks], meta[2 * q_blocks + 1]
    range_blocks = 2 * planes
    dk_acc[...] = jnp.zeros_like(dk_acc)
    dv_acc[...] = jnp.zeros_like(dv_acc)
    if ends:
        loads = [pltpu.make_async_copy(near[n], kv.at[n], kv_sems.at[n]) for n in range(count)]
        for copy in loads:
            copy.start()
        for copy in loads:
            copy.wait()

    def dq_store(b, d):
        return pltpu.make_async_copy(dq.at[b * slots + (slot ^ d)], dq_out[d].at[b], out_sems.at[b, d])

    def over_range(r, _):
        lasts = [meta[2 * r + x] for x in range(2)]
        firsts = [meta[q_blocks + 2 * r + x] for x in range(2)]
        for x in range(2):
            stats = pkg[pl.ds(sources * (2 * r + x), sources), 2 * rows :, :]
            lse[x], delta[x] = stats_of(stats, sources, rows // 128)
            dq_acc[x] = jnp.zeros_like(dq_acc[x]) if starts else dq_before[2 * r + x]

        def queries(x):
            mine = pl.ds(sources * (2 * r + x), sources)
            q = pkg[mine, 0:rows, :].reshape(wide, 128)
            g = pkg[mine, rows : 2 * rows, :].reshape(wide, 128)
            return q, g, lse[x], delta[x]

        def keys(n, block, blocks):
            at = pl.ds(sources * block, sources * blocks)
            held = kv.at[n] if ends else near[0]
            return held[at, 0].reshape(blocks * BLK, 128), held[at, 1].reshape(blocks * BLK, 128)

        def add_keys(n, block, dk, dv):
            at = pl.ds(pl.multiple_of(block * BLK, BLK), dk.shape[0])
            dk_acc[n, at, :] += dk
            dv_acc[n, at, :] += dv

        def both(n, half):
            k, v = keys(n, 2 * half, 2)
            parts = [block_pair(*queries(x), k, v, group, scale, None) for x in range(2)]
            for x in range(2):
                dq_acc[x] += parts[x][0]
            add_keys(n, 2 * half, parts[0][1] + parts[1][1], parts[0][2] + parts[1][2])

        def one(x, n, block):
            dq_part, dk, dv = block_pair(*queries(x), *keys(n, block, 1), group, scale, None)
            dq_acc[x] += dq_part
            add_keys(n, block, dk, dv)

        def inner(t, _):
            half, n = lax.div(t, count), lax.rem(t, count)
            base = half * range_blocks + 2 * ((n + distances[0]) ^ plane)
            seen = [
                [(base + y >= firsts[x]) & (base + y <= lasts[x]) for y in range(2)] for x in range(2)
            ]
            every = seen[0][0] & seen[0][1] & seen[1][0] & seen[1][1]
            if ends:
                own = base == lasts[0]
                every = every & jnp.logical_not(own)

            @pl.when(every)
            def _():
                both(n, half)

            some = seen[0][0] | seen[0][1] | seen[1][0] | seen[1][1]
            some = some & jnp.logical_not(every)
            if ends:
                some = some & jnp.logical_not(own)

            @pl.when(some)
            def _():
                def single(at, _):
                    x, y = at // 2, at % 2
                    last, first = meta[2 * r + x], meta[q_blocks + 2 * r + x]

                    @pl.when((base + y >= first) & (base + y <= last))
                    def _():
                        one(x, n, 2 * half + y)

                    return 0

                lax.fori_loop(0, 4, single, 0)

            return 0

        lax.fori_loop(0, (r + 1) * count, inner, 0)
        if ends:
            n = distances.index(0)
            from_key = jnp.where(firsts[1] <= lasts[0], 0, BLK)
            dq_0, dk, dv = block_pair(*queries(0), *keys(n, 2 * r, 1), group, scale, (0, 0))
            dq_1, dk_1, dv_1 = block_pair(*queries(1), *keys(n, 2 * r, 2), group, scale, (BLK, from_key))
            dq_acc[0] += dq_0
            dq_acc[1] += dq_1
            add_keys(n, 2 * r, dk + dk_1[0:BLK], dv + dv_1[0:BLK])
            add_keys(n, 2 * r + 1, dk_1[BLK:], dv_1[BLK:])
        for x in range(2):
            if ends:
                done = (dq_acc[x] * scale).astype(jnp.bfloat16).reshape(sources, rows, 128)
                dq[pl.ds(sources * (2 * r + x), sources)] = done
            else:
                dq_out[0][2 * r + x] = dq_acc[x]
        if ends:
            for d in range(slots):
                dq_store(r, d).start()
        return 0

    lax.fori_loop(0, 2, over_range, 0)
    stores = [dq_store(b, d) for b in range(2) for d in range(slots)] if ends else []
    if not ends:
        grads_out[0][:, 0] = (dk_acc[0] * scale).astype(jnp.bfloat16).reshape(team, tok, 128)
        grads_out[0][:, 1] = dv_acc[0].astype(jnp.bfloat16).reshape(team, tok, 128)
        return
    grad_stores = [pltpu.make_async_copy(grads.at[n], grads_out[n], grad_sems.at[n]) for n in range(count)]
    for n in reversed(range(count)):
        grads[n, :, 0] = (dk_acc[n] * scale).astype(jnp.bfloat16).reshape(team, tok, 128)
        grads[n, :, 1] = dv_acc[n].astype(jnp.bfloat16).reshape(team, tok, 128)
        grad_stores[n].start()
    for copy in stores + grad_stores:
        copy.wait()


VMEM = pl.BlockSpec(memory_space=pltpu.VMEM)
SMEM = pl.BlockSpec(memory_space=pltpu.SMEM)


def totals(shards, tok, wide, head_dim):
    return [
        pltpu.VMEM((shards * tok, head_dim), jnp.float32),
        pltpu.VMEM((shards * tok, head_dim), jnp.float32),
        pltpu.VMEM((wide, head_dim), jnp.float32),
    ]


def attention(meta, pkg, kv, rows, scale):
    shards, _, tok, head_dim = kv.shape
    team = pkg.shape[0]
    q_blocks = team * tok // BLK
    return pl.pallas_call(
        functools.partial(whole_kernel, rows=rows, tok=tok, q_blocks=q_blocks, scale=scale),
        out_shape=(
            jax.ShapeDtypeStruct((team, rows, head_dim), jnp.bfloat16),
            jax.ShapeDtypeStruct(kv.shape, jnp.bfloat16),
        ),
        in_specs=[SMEM, VMEM, VMEM],
        out_specs=(VMEM, VMEM),
        scratch_shapes=totals(shards, tok, rows * (BLK // tok), head_dim),
        compiler_params=pltpu.CompilerParams(vmem_limit_bytes=LIMIT),
        name="attention_grads",
    )(meta, pkg, kv)


def attention_part(meta, pkg, kv, distances, dq_before, rows, scale, planes):
    team, _, tok, head_dim = kv[0].shape
    slots = team // 2
    count = len(distances)
    q_blocks = team * tok // BLK
    wide = rows * (BLK // tok)
    scratch = [
        pltpu.VMEM((count,) + kv[0].shape, jnp.bfloat16),
        pltpu.VMEM((count,) + kv[0].shape, jnp.bfloat16),
        pltpu.VMEM((count, team * tok, head_dim), jnp.float32),
        pltpu.VMEM((count, team * tok, head_dim), jnp.float32),
        pltpu.VMEM((2, wide, head_dim), jnp.float32),
        pltpu.VMEM((2, 1, wide), jnp.float32),
        pltpu.VMEM((2, 1, wide), jnp.float32),
        pltpu.SemaphoreType.DMA((count,)),
        pltpu.SemaphoreType.DMA((count,)),
    ]
    hbm = pl.BlockSpec(memory_space=pltpu.HBM)
    ends = 0 in distances
    if ends:
        dq_shapes = (jax.ShapeDtypeStruct((2, rows, head_dim), jnp.bfloat16),) * slots
        dq_specs = (hbm,) * slots
        scratch += [pltpu.VMEM((team, rows, head_dim), jnp.bfloat16), pltpu.SemaphoreType.DMA((2, slots))]
    else:
        dq_shapes = (jax.ShapeDtypeStruct((q_blocks, wide, head_dim), jnp.float32),)
        dq_specs = (VMEM,)
    before = [] if dq_before is None else [dq_before]
    pairs = q_blocks * count
    out = pl.pallas_call(
        functools.partial(
            planes_kernel, rows=rows, tok=tok, q_blocks=q_blocks, scale=scale, distances=distances, planes=planes
        ),
        out_shape=dq_shapes + (jax.ShapeDtypeStruct(kv[0].shape, jnp.bfloat16),) * count,
        in_specs=[SMEM, VMEM] + [hbm if ends else VMEM] * count + [VMEM] * len(before),
        out_specs=dq_specs + (hbm if ends else VMEM,) * count,
        scratch_shapes=scratch,
        compiler_params=pltpu.CompilerParams(vmem_limit_bytes=PART_LIMIT),
        cost_estimate=pl.CostEstimate(
            flops=pairs * 10 * BLK * wide * head_dim,
            bytes_accessed=4 * 1024 * 1024,
            transcendentals=pairs * BLK * wide,
        ),
        name="attention_" + "_".join(str(d) for d in distances),
    )(meta, pkg, *kv, *before)
    dq, grads = out[:-count], out[-count:]
    return (dq if ends else dq[0]), grads


def place_dq_kernel(place, *refs):
    *arrived, swapped, out = refs
    slots = len(arrived)
    core, slot = place[0], place[1]
    for d, blocks in enumerate(arrived):
        out[:, core * slots + (slot ^ d)] = blocks[core]
        out[:, (1 - core) * slots + (slot ^ d)] = swapped[d]


def place_dq(place, arrived, swapped, tok):
    slots, rows, head_dim = swapped.shape
    fan = rows // tok
    out = pl.pallas_call(
        place_dq_kernel,
        out_shape=jax.ShapeDtypeStruct((tok, 2 * slots, fan, head_dim), jnp.bfloat16),
        in_specs=[SMEM] + [VMEM] * (slots + 1),
        out_specs=VMEM,
        compiler_params=pltpu.CompilerParams(vmem_limit_bytes=SMALL_LIMIT),
        name="place_dq",
    )(place, *[x.reshape(2, tok, fan, head_dim) for x in arrived], swapped.reshape(slots, tok, fan, head_dim))
    return out.reshape(tok, 2 * slots * fan, head_dim)


def place_dkv_kernel(parts, dk, dv, wide):
    halves, kv_heads = parts.shape[:2]
    for n, out in enumerate((dk, dv)):
        for h in range(kv_heads):
            wide[:, h, :] = sum(parts[p, h, n].astype(jnp.float32) for p in range(halves))
        out[...] = wide[...].astype(jnp.bfloat16)


def place_dkv(parts):
    _, kv_heads, _, tok, head_dim = parts.shape
    shape = (tok, kv_heads, head_dim)
    dk, dv = pl.pallas_call(
        place_dkv_kernel,
        out_shape=(jax.ShapeDtypeStruct(shape, jnp.bfloat16),) * 2,
        in_specs=[VMEM],
        out_specs=(VMEM, VMEM),
        scratch_shapes=[pltpu.VMEM(shape, jnp.float32)],
        compiler_params=pltpu.CompilerParams(vmem_limit_bytes=SMALL_LIMIT),
        name="place_dkv",
    )(parts)
    return dk, dv


def pieces(x):
    high = lax.reduce_precision(x, 8, 7)
    return [part.astype(jnp.bfloat16) for part in (high, x - high)]


def add(*terms):
    return sum(x.astype(jnp.float32) for x in terms).astype(jnp.bfloat16)


def dq_by_token(dq, tok, fan):
    kv_heads, _, head_dim = dq.shape
    return dq.reshape(kv_heads, tok, fan, head_dim).transpose(1, 0, 2, 3).reshape(tok, kv_heads * fan, head_dim)


def dkv_by_token(parts):
    dkv = parts.astype(jnp.float32).sum(axis=0).astype(jnp.bfloat16).transpose(1, 2, 0, 3)
    return dkv[0], dkv[1]


def per_device(queries, keys, values, outputs, out_grads, log_norms, block_doc):
    tok, heads, head_dim = queries.shape
    kv_heads = keys.shape[1]
    fan = heads // kv_heads
    n_ctx, n_head = lax.axis_size("ctx"), lax.axis_size("head")
    slots = kv_heads // 2
    planes = n_head // slots
    rows = tok * fan
    scale = head_dim**-0.5
    ctx, head = lax.axis_index("ctx"), lax.axis_index("head")
    both = ("ctx", "head")
    teams = [
        [(2 * c + b) * n_head + z * slots + r for b in range(2) for r in range(slots)]
        for c in range(n_ctx // 2)
        for z in range(planes)
    ]
    pairs = [
        [(2 * c + b) * n_head + h for b in range(2) for h in range(n_head)]
        for c in range(n_ctx // 2)
    ]

    by_plane = n_ctx == 2 and planes == 4 and slots * tok == 2 * BLK

    def across(x, distance):
        step = distance * slots
        return lax.ppermute(x, "head", [(h, h ^ step) for h in range(n_head)])

    kv = jnp.stack([keys, values], axis=0).transpose(2, 0, 1, 3)
    if by_plane:
        kv = lax.all_to_all(kv, both, 0, 0, axis_index_groups=teams, tiled=True)
        second, first = across(kv, 2), across(kv, 1)
        kv = (kv, first, second, across(second, 1))
    else:
        kv = kv.reshape(2, 1, slots, 2, tok, head_dim)
        kv = jnp.broadcast_to(kv, (2, planes, slots, 2, tok, head_dim))
        kv = kv.reshape(2 * n_head, 2, tok, head_dim)
        kv = lax.all_to_all(kv, both, 0, 0, axis_index_groups=pairs, tiled=True)

    def by_group(x):
        return x.reshape(tok, kv_heads, fan, head_dim).transpose(1, 0, 2, 3).reshape(kv_heads, rows, head_dim)

    deltas = jnp.sum(out_grads.astype(jnp.float32) * outputs.astype(jnp.float32), axis=-1)
    stats = jnp.stack(pieces(log_norms) + pieces(deltas), axis=0)
    stats = stats.reshape(4, tok, kv_heads, fan).transpose(2, 0, 1, 3)
    stats = stats.reshape(kv_heads, 4 * rows // 128, 128)
    pkg = jnp.concatenate([by_group(queries), by_group(out_grads), stats], axis=1)
    pkg = lax.all_to_all(pkg, both, 0, 0, axis_index_groups=teams, tiled=True)

    pair, plane = lax.div(ctx, 2), lax.div(head, slots)
    range_blocks = n_head * tok // BLK
    team_blocks = slots * tok // BLK
    at = jnp.stack(
        [(2 * pair + b) * range_blocks + plane * team_blocks + j for b in range(2) for j in range(team_blocks)]
    )
    first_block = jnp.sum(block_doc[None, :] < block_doc[at][:, None], axis=1, dtype=jnp.int32)
    ranges_before = 1 if n_ctx > 2 else 0
    base = (2 * pair - ranges_before) * range_blocks
    meta = jnp.concatenate([at - base, first_block - base, plane[None], lax.rem(head, slots)[None]]).astype(jnp.int32)

    if by_plane:
        def part(distances, dq_before):
            return attention_part(
                meta, pkg, [kv[d] for d in distances], distances, dq_before, rows, scale, planes
            )

        dq, (grads_3,) = part((3,), None)
        relayed = across(grads_3, 1)
        dq, (grads_0, grads_1, grads_2) = part((0, 1, 2), dq)
        far = add(grads_2, relayed)
        far, *dq = lax.optimization_barrier((far, *dq))
        far = across(far, 2)
        close = across(grads_1, 1)
        dq = [lax.ppermute(x, "head", [(h, h ^ d) for h in range(n_head)]) if d else x for d, x in enumerate(dq)]
        dkv = grads_0.astype(jnp.float32) + far.astype(jnp.float32)
        dkv, *dq = lax.optimization_barrier((dkv, *dq))
        dkv, close = lax.optimization_barrier((dkv, close))
        dkv = add(dkv, close)
        dkv = lax.all_to_all(dkv, both, 0, 0, axis_index_groups=teams, tiled=True)
        other = jnp.where(ctx == 0, jnp.stack([x[1] for x in dq]), jnp.stack([x[0] for x in dq]))
        swapped = lax.ppermute(other, "ctx", [(0, 1), (1, 0)])
        dq = place_dq(jnp.stack([ctx, lax.rem(head, slots)]), dq, swapped, tok)
        dkv, dq = lax.optimization_barrier((dkv, dq))
        return (dq,) + place_dkv(dkv[None])

    if ranges_before:
        prior = lax.ppermute(kv[n_head:], "ctx", [(c, c + 2) for c in range(n_ctx - 2)])
        kv = jnp.concatenate([prior, kv], axis=0)
    dq, dkv = attention(meta, pkg, kv, rows, scale)
    if ranges_before:
        later = lax.ppermute(dkv[:n_head], "ctx", [(c + 2, c) for c in range(n_ctx - 2)])
        dkv = jnp.concatenate([dkv[n_head : 2 * n_head], add(dkv[2 * n_head :], later)], axis=0)

    dkv = lax.all_to_all(dkv, both, 0, 0, axis_index_groups=pairs, tiled=True)
    dq = lax.all_to_all(dq, both, 0, 0, axis_index_groups=teams, tiled=True)
    dkv = dkv.reshape(2, planes, slots, 2, tok, head_dim).transpose(1, 0, 2, 3, 4, 5)
    return (dq_by_token(dq, tok, fan),) + dkv_by_token(dkv.reshape(planes, kv_heads, 2, tok, head_dim))


def solution(mesh):
    tokens = P(("ctx", "head"), None, None)
    return jax.shard_map(
        per_device,
        mesh=mesh,
        in_specs=(tokens,) * 5 + (P(("ctx", "head"), None), P()),
        out_specs=(tokens,) * 3,
        check_vma=False,
    )
```

```python
import functools

import jax
import jax.numpy as jnp
from jax import lax
from jax.experimental import pallas as pl
from jax.experimental.pallas import tpu as pltpu
from jax.sharding import PartitionSpec as P

BLK = 128
LOG2E = 1.4426950408889634
LIMIT = 56 * 1024 * 1024
PART_LIMIT = 20 * 1024 * 1024
SMALL_LIMIT = 6 * 1024 * 1024


def stats_of(stats, sources, chunks):
    stats = stats.astype(jnp.float32)
    sums = (
        stats[:, base : base + chunks] + stats[:, base + chunks : base + 2 * chunks]
        for base in (0, 2 * chunks)
    )
    lse, delta = (
        jnp.concatenate([x[s, c : c + 1, :] for s in range(sources) for c in range(chunks)], axis=1)
        for x in sums
    )
    return lse * LOG2E, delta


def block_pair(q, g, lse, delta, k, v, group, scale, mask):
    s = lax.dot_general(k, q, (((1,), (1,)), ((), ())), preferred_element_type=jnp.float32)
    p = jnp.exp2(s * (scale * LOG2E) - lse)
    if mask is not None:
        lead, from_key = mask
        key_at = lax.broadcasted_iota(jnp.int32, p.shape, 0)
        query_at = lax.broadcasted_iota(jnp.int32, p.shape, 1) // group + lead
        p = jnp.where((query_at >= key_at) & (key_at >= from_key), p, 0.0)
    dp = lax.dot_general(v, g, (((1,), (1,)), ((), ())), preferred_element_type=jnp.float32)
    ds = (p * (dp - delta)).astype(jnp.bfloat16)
    dv = jnp.dot(p.astype(jnp.bfloat16), g, preferred_element_type=jnp.float32)
    dk = jnp.dot(ds, q, preferred_element_type=jnp.float32)
    dq = lax.dot_general(ds, k, (((0,), (0,)), ((), ())), preferred_element_type=jnp.float32)
    return dq, dk, dv


def whole_kernel(meta, pkg, kv, dq, dkv, dk_acc, dv_acc, dq_acc, *, rows, tok, q_blocks, scale):
    sources = BLK // tok
    wide = sources * rows
    dk_acc[...] = jnp.zeros_like(dk_acc)
    dv_acc[...] = jnp.zeros_like(dv_acc)

    def over_queries(i, _):
        last, first = meta[i], meta[q_blocks + i]
        mine = pl.ds(sources * i, sources)
        q = pkg[mine, 0:rows, :].reshape(wide, 128)
        g = pkg[mine, rows : 2 * rows, :].reshape(wide, 128)
        lse, delta = stats_of(pkg[mine, 2 * rows :, :], sources, rows // 128)
        dq_acc[...] = jnp.zeros_like(dq_acc)

        def step(j, masked):
            k = kv[pl.ds(sources * j, sources), 0].reshape(BLK, 128)
            v = kv[pl.ds(sources * j, sources), 1].reshape(BLK, 128)
            dq_part, dk, dv = block_pair(q, g, lse, delta, k, v, rows // tok, scale, (0, 0) if masked else None)
            at = pl.ds(pl.multiple_of(j * BLK, BLK), BLK)
            dv_acc[at, :] += dv
            dk_acc[at, :] += dk
            dq_acc[...] += dq_part

        def inner(j, _):
            step(j, False)
            return 0

        lax.fori_loop(first, last, inner, 0)
        step(last, True)
        dq[mine] = (dq_acc[...] * scale).astype(jnp.bfloat16).reshape(sources, rows, 128)
        return 0

    lax.fori_loop(0, q_blocks, over_queries, 0)
    shards = dkv.shape[0]
    dkv[:, 0] = (dk_acc[...] * scale).astype(jnp.bfloat16).reshape(shards, tok, 128)
    dkv[:, 1] = dv_acc[...].astype(jnp.bfloat16).reshape(shards, tok, 128)


def planes_kernel(meta, pkg, *refs, rows, tok, q_blocks, scale, distances, planes):
    team = pkg.shape[0]
    slots = team // 2
    count = len(distances)
    starts, ends = planes - 1 in distances, 0 in distances
    near, refs = refs[:count], refs[count:]
    if not starts:
        dq_before, refs = refs[0], refs[1:]
    outs = slots if ends else 1
    dq_out, grads_out, refs = refs[:outs], refs[outs : outs + count], refs[outs + count :]
    kv, grads, dk_acc, dv_acc, dq_acc, lse, delta, kv_sems, grad_sems = refs[:9]
    if ends:
        dq, out_sems = refs[9:]
    sources = BLK // tok
    wide = sources * rows
    group = rows // tok
    plane, slot = meta[2 * q_blocks], meta[2 * q_blocks + 1]
    range_blocks = 2 * planes
    dk_acc[...] = jnp.zeros_like(dk_acc)
    dv_acc[...] = jnp.zeros_like(dv_acc)
    if ends:
        loads = [pltpu.make_async_copy(near[n], kv.at[n], kv_sems.at[n]) for n in range(count)]
        for copy in loads:
            copy.start()
        loads[distances.index(0)].wait()

    def dq_store(b, d):
        return pltpu.make_async_copy(dq.at[b * slots + (slot ^ d)], dq_out[d].at[b], out_sems.at[b, d])

    def over_range(r, _):
        lasts = [meta[2 * r + x] for x in range(2)]
        firsts = [meta[q_blocks + 2 * r + x] for x in range(2)]
        for x in range(2):
            stats = pkg[pl.ds(sources * (2 * r + x), sources), 2 * rows :, :]
            lse[x], delta[x] = stats_of(stats, sources, rows // 128)
            dq_acc[x] = jnp.zeros_like(dq_acc[x]) if starts else dq_before[2 * r + x]

        def queries(x):
            mine = pl.ds(sources * (2 * r + x), sources)
            q = pkg[mine, 0:rows, :].reshape(wide, 128)
            g = pkg[mine, rows : 2 * rows, :].reshape(wide, 128)
            return q, g, lse[x], delta[x]

        def keys(n, block, blocks):
            at = pl.ds(sources * block, sources * blocks)
            held = kv.at[n] if ends else near[0]
            return held[at, 0].reshape(blocks * BLK, 128), held[at, 1].reshape(blocks * BLK, 128)

        def add_keys(n, block, dk, dv):
            at = pl.ds(pl.multiple_of(block * BLK, BLK), dk.shape[0])
            dk_acc[n, at, :] += dk
            dv_acc[n, at, :] += dv

        def both(n, half):
            k, v = keys(n, 2 * half, 2)
            parts = [block_pair(*queries(x), k, v, group, scale, None) for x in range(2)]
            for x in range(2):
                dq_acc[x] += parts[x][0]
            add_keys(n, 2 * half, parts[0][1] + parts[1][1], parts[0][2] + parts[1][2])

        def one(x, n, block):
            dq_part, dk, dv = block_pair(*queries(x), *keys(n, block, 1), group, scale, None)
            dq_acc[x] += dq_part
            add_keys(n, block, dk, dv)

        def inner(t, _):
            half, n = lax.div(t, count), lax.rem(t, count)
            base = half * range_blocks + 2 * ((n + distances[0]) ^ plane)
            seen = [
                [(base + y >= firsts[x]) & (base + y <= lasts[x]) for y in range(2)] for x in range(2)
            ]
            every = seen[0][0] & seen[0][1] & seen[1][0] & seen[1][1]
            if ends:
                own = base == lasts[0]
                every = every & jnp.logical_not(own)

            @pl.when(every)
            def _():
                both(n, half)

            some = seen[0][0] | seen[0][1] | seen[1][0] | seen[1][1]
            some = some & jnp.logical_not(every)
            if ends:
                some = some & jnp.logical_not(own)

            @pl.when(some)
            def _():
                def single(at, _):
                    x, y = at // 2, at % 2
                    last, first = meta[2 * r + x], meta[q_blocks + 2 * r + x]

                    @pl.when((base + y >= first) & (base + y <= last))
                    def _():
                        one(x, n, 2 * half + y)

                    return 0

                lax.fori_loop(0, 4, single, 0)

            return 0

        if ends:
            n = distances.index(0)
            from_key = jnp.where(firsts[1] <= lasts[0], 0, BLK)
            dq_0, dk, dv = block_pair(*queries(0), *keys(n, 2 * r, 1), group, scale, (0, 0))
            dq_1, dk_1, dv_1 = block_pair(*queries(1), *keys(n, 2 * r, 2), group, scale, (BLK, from_key))
            dq_acc[0] += dq_0
            dq_acc[1] += dq_1
            add_keys(n, 2 * r, dk + dk_1[0:BLK], dv + dv_1[0:BLK])
            add_keys(n, 2 * r + 1, dk_1[BLK:], dv_1[BLK:])
        if ends:

            @pl.when(r == 0)
            def _():
                for n, copy in enumerate(loads):
                    if distances[n] != 0:
                        copy.wait()

        lax.fori_loop(0, (r + 1) * count, inner, 0)
        for x in range(2):
            if ends:
                done = (dq_acc[x] * scale).astype(jnp.bfloat16).reshape(sources, rows, 128)
                dq[pl.ds(sources * (2 * r + x), sources)] = done
            else:
                dq_out[0][2 * r + x] = dq_acc[x]
        if ends:
            for d in range(slots):
                dq_store(r, d).start()
        return 0

    lax.fori_loop(0, 2, over_range, 0)
    stores = [dq_store(b, d) for b in range(2) for d in range(slots)] if ends else []
    if not ends:
        grads_out[0][:, 0] = (dk_acc[0] * scale).astype(jnp.bfloat16).reshape(team, tok, 128)
        grads_out[0][:, 1] = dv_acc[0].astype(jnp.bfloat16).reshape(team, tok, 128)
        return
    grad_stores = [pltpu.make_async_copy(grads.at[n], grads_out[n], grad_sems.at[n]) for n in range(count)]
    for n in reversed(range(count)):
        grads[n, :, 0] = (dk_acc[n] * scale).astype(jnp.bfloat16).reshape(team, tok, 128)
        grads[n, :, 1] = dv_acc[n].astype(jnp.bfloat16).reshape(team, tok, 128)
        grad_stores[n].start()
    for copy in stores + grad_stores:
        copy.wait()


VMEM = pl.BlockSpec(memory_space=pltpu.VMEM)
SMEM = pl.BlockSpec(memory_space=pltpu.SMEM)


def totals(shards, tok, wide, head_dim):
    return [
        pltpu.VMEM((shards * tok, head_dim), jnp.float32),
        pltpu.VMEM((shards * tok, head_dim), jnp.float32),
        pltpu.VMEM((wide, head_dim), jnp.float32),
    ]


def attention(meta, pkg, kv, rows, scale):
    shards, _, tok, head_dim = kv.shape
    team = pkg.shape[0]
    q_blocks = team * tok // BLK
    return pl.pallas_call(
        functools.partial(whole_kernel, rows=rows, tok=tok, q_blocks=q_blocks, scale=scale),
        out_shape=(
            jax.ShapeDtypeStruct((team, rows, head_dim), jnp.bfloat16),
            jax.ShapeDtypeStruct(kv.shape, jnp.bfloat16),
        ),
        in_specs=[SMEM, VMEM, VMEM],
        out_specs=(VMEM, VMEM),
        scratch_shapes=totals(shards, tok, rows * (BLK // tok), head_dim),
        compiler_params=pltpu.CompilerParams(vmem_limit_bytes=LIMIT),
        name="attention_grads",
    )(meta, pkg, kv)


def attention_part(meta, pkg, kv, distances, dq_before, rows, scale, planes):
    team, _, tok, head_dim = kv[0].shape
    slots = team // 2
    count = len(distances)
    q_blocks = team * tok // BLK
    wide = rows * (BLK // tok)
    scratch = [
        pltpu.VMEM((count,) + kv[0].shape, jnp.bfloat16),
        pltpu.VMEM((count,) + kv[0].shape, jnp.bfloat16),
        pltpu.VMEM((count, team * tok, head_dim), jnp.float32),
        pltpu.VMEM((count, team * tok, head_dim), jnp.float32),
        pltpu.VMEM((2, wide, head_dim), jnp.float32),
        pltpu.VMEM((2, 1, wide), jnp.float32),
        pltpu.VMEM((2, 1, wide), jnp.float32),
        pltpu.SemaphoreType.DMA((count,)),
        pltpu.SemaphoreType.DMA((count,)),
    ]
    hbm = pl.BlockSpec(memory_space=pltpu.HBM)
    ends = 0 in distances
    if ends:
        dq_shapes = (jax.ShapeDtypeStruct((2, rows, head_dim), jnp.bfloat16),) * slots
        dq_specs = (hbm,) * slots
        scratch += [pltpu.VMEM((team, rows, head_dim), jnp.bfloat16), pltpu.SemaphoreType.DMA((2, slots))]
    else:
        dq_shapes = (jax.ShapeDtypeStruct((q_blocks, wide, head_dim), jnp.float32),)
        dq_specs = (VMEM,)
    before = [] if dq_before is None else [dq_before]
    pairs = q_blocks * count
    out = pl.pallas_call(
        functools.partial(
            planes_kernel, rows=rows, tok=tok, q_blocks=q_blocks, scale=scale, distances=distances, planes=planes
        ),
        out_shape=dq_shapes + (jax.ShapeDtypeStruct(kv[0].shape, jnp.bfloat16),) * count,
        in_specs=[SMEM, VMEM] + [hbm if ends else VMEM] * count + [VMEM] * len(before),
        out_specs=dq_specs + (hbm if ends else VMEM,) * count,
        scratch_shapes=scratch,
        compiler_params=pltpu.CompilerParams(vmem_limit_bytes=PART_LIMIT),
        cost_estimate=pl.CostEstimate(
            flops=pairs * 10 * BLK * wide * head_dim,
            bytes_accessed=4 * 1024 * 1024,
            transcendentals=pairs * BLK * wide,
        ),
        name="attention_" + "_".join(str(d) for d in distances),
    )(meta, pkg, *kv, *before)
    dq, grads = out[:-count], out[-count:]
    return (dq if ends else dq[0]), grads


def place_dq_kernel(place, *refs):
    *arrived, swapped, out = refs
    slots = len(arrived)
    core, slot = place[0], place[1]
    for d, blocks in enumerate(arrived):
        out[:, core * slots + (slot ^ d)] = blocks[core]
        out[:, (1 - core) * slots + (slot ^ d)] = swapped[d]


def place_dq(place, arrived, swapped, tok):
    slots, rows, head_dim = swapped.shape
    fan = rows // tok
    out = pl.pallas_call(
        place_dq_kernel,
        out_shape=jax.ShapeDtypeStruct((tok, 2 * slots, fan, head_dim), jnp.bfloat16),
        in_specs=[SMEM] + [VMEM] * (slots + 1),
        out_specs=VMEM,
        compiler_params=pltpu.CompilerParams(vmem_limit_bytes=SMALL_LIMIT),
        name="place_dq",
    )(place, *[x.reshape(2, tok, fan, head_dim) for x in arrived], swapped.reshape(slots, tok, fan, head_dim))
    return out.reshape(tok, 2 * slots * fan, head_dim)


def place_dkv_kernel(parts, dk, dv, wide):
    halves, kv_heads = parts.shape[:2]
    for n, out in enumerate((dk, dv)):
        for h in range(kv_heads):
            wide[:, h, :] = sum(parts[p, h, n].astype(jnp.float32) for p in range(halves))
        out[...] = wide[...].astype(jnp.bfloat16)


def place_dkv(parts):
    _, kv_heads, _, tok, head_dim = parts.shape
    shape = (tok, kv_heads, head_dim)
    dk, dv = pl.pallas_call(
        place_dkv_kernel,
        out_shape=(jax.ShapeDtypeStruct(shape, jnp.bfloat16),) * 2,
        in_specs=[VMEM],
        out_specs=(VMEM, VMEM),
        scratch_shapes=[pltpu.VMEM(shape, jnp.float32)],
        compiler_params=pltpu.CompilerParams(vmem_limit_bytes=SMALL_LIMIT),
        name="place_dkv",
    )(parts)
    return dk, dv


def pieces(x):
    high = lax.reduce_precision(x, 8, 7)
    return [part.astype(jnp.bfloat16) for part in (high, x - high)]


def add(*terms):
    return sum(x.astype(jnp.float32) for x in terms).astype(jnp.bfloat16)


def dq_by_token(dq, tok, fan):
    kv_heads, _, head_dim = dq.shape
    return dq.reshape(kv_heads, tok, fan, head_dim).transpose(1, 0, 2, 3).reshape(tok, kv_heads * fan, head_dim)


def dkv_by_token(parts):
    dkv = parts.astype(jnp.float32).sum(axis=0).astype(jnp.bfloat16).transpose(1, 2, 0, 3)
    return dkv[0], dkv[1]


def per_device(queries, keys, values, outputs, out_grads, log_norms, block_doc):
    tok, heads, head_dim = queries.shape
    kv_heads = keys.shape[1]
    fan = heads // kv_heads
    n_ctx, n_head = lax.axis_size("ctx"), lax.axis_size("head")
    slots = kv_heads // 2
    planes = n_head // slots
    rows = tok * fan
    scale = head_dim**-0.5
    ctx, head = lax.axis_index("ctx"), lax.axis_index("head")
    both = ("ctx", "head")
    teams = [
        [(2 * c + b) * n_head + z * slots + r for b in range(2) for r in range(slots)]
        for c in range(n_ctx // 2)
        for z in range(planes)
    ]
    pairs = [
        [(2 * c + b) * n_head + h for b in range(2) for h in range(n_head)]
        for c in range(n_ctx // 2)
    ]

    by_plane = n_ctx == 2 and planes == 4 and slots * tok == 2 * BLK

    def across(x, distance):
        step = distance * slots
        return lax.ppermute(x, "head", [(h, h ^ step) for h in range(n_head)])

    kv = jnp.stack([keys, values], axis=0).transpose(2, 0, 1, 3)
    if by_plane:
        kv = lax.all_to_all(kv, both, 0, 0, axis_index_groups=teams, tiled=True)
        second, first = across(kv, 2), across(kv, 1)
        kv = (kv, first, second, across(second, 1))
    else:
        kv = kv.reshape(2, 1, slots, 2, tok, head_dim)
        kv = jnp.broadcast_to(kv, (2, planes, slots, 2, tok, head_dim))
        kv = kv.reshape(2 * n_head, 2, tok, head_dim)
        kv = lax.all_to_all(kv, both, 0, 0, axis_index_groups=pairs, tiled=True)

    def by_group(x):
        return x.reshape(tok, kv_heads, fan, head_dim).transpose(1, 0, 2, 3).reshape(kv_heads, rows, head_dim)

    deltas = jnp.sum(out_grads.astype(jnp.float32) * outputs.astype(jnp.float32), axis=-1)
    stats = jnp.stack(pieces(log_norms) + pieces(deltas), axis=0)
    stats = stats.reshape(4, tok, kv_heads, fan).transpose(2, 0, 1, 3)
    stats = stats.reshape(kv_heads, 4 * rows // 128, 128)
    pkg = jnp.concatenate([by_group(queries), by_group(out_grads), stats], axis=1)
    pkg = lax.all_to_all(pkg, both, 0, 0, axis_index_groups=teams, tiled=True)

    pair, plane = lax.div(ctx, 2), lax.div(head, slots)
    range_blocks = n_head * tok // BLK
    team_blocks = slots * tok // BLK
    at = jnp.stack(
        [(2 * pair + b) * range_blocks + plane * team_blocks + j for b in range(2) for j in range(team_blocks)]
    )
    first_block = jnp.sum(block_doc[None, :] < block_doc[at][:, None], axis=1, dtype=jnp.int32)
    ranges_before = 1 if n_ctx > 2 else 0
    base = (2 * pair - ranges_before) * range_blocks
    meta = jnp.concatenate([at - base, first_block - base, plane[None], lax.rem(head, slots)[None]]).astype(jnp.int32)

    if by_plane:
        def part(distances, dq_before):
            return attention_part(
                meta, pkg, [kv[d] for d in distances], distances, dq_before, rows, scale, planes
            )

        dq, (grads_3,) = part((3,), None)
        relayed = across(grads_3, 1)
        dq, (grads_0, grads_1, grads_2) = part((0, 1, 2), dq)
        far = add(grads_2, relayed)
        far, *dq = lax.optimization_barrier((far, *dq))
        far = across(far, 2)
        close = across(grads_1, 1)
        dq = [lax.ppermute(x, "head", [(h, h ^ d) for h in range(n_head)]) if d else x for d, x in enumerate(dq)]
        dkv = grads_0.astype(jnp.float32) + far.astype(jnp.float32)
        dkv, *dq = lax.optimization_barrier((dkv, *dq))
        dkv, close = lax.optimization_barrier((dkv, close))
        dkv = add(dkv, close)
        dkv = lax.all_to_all(dkv, both, 0, 0, axis_index_groups=teams, tiled=True)
        other = jnp.where(ctx == 0, jnp.stack([x[1] for x in dq]), jnp.stack([x[0] for x in dq]))
        swapped = lax.ppermute(other, "ctx", [(0, 1), (1, 0)])
        dq = place_dq(jnp.stack([ctx, lax.rem(head, slots)]), dq, swapped, tok)
        dkv, dq = lax.optimization_barrier((dkv, dq))
        return (dq,) + place_dkv(dkv[None])

    if ranges_before:
        prior = lax.ppermute(kv[n_head:], "ctx", [(c, c + 2) for c in range(n_ctx - 2)])
        kv = jnp.concatenate([prior, kv], axis=0)
    dq, dkv = attention(meta, pkg, kv, rows, scale)
    if ranges_before:
        later = lax.ppermute(dkv[:n_head], "ctx", [(c + 2, c) for c in range(n_ctx - 2)])
        dkv = jnp.concatenate([dkv[n_head : 2 * n_head], add(dkv[2 * n_head :], later)], axis=0)

    dkv = lax.all_to_all(dkv, both, 0, 0, axis_index_groups=pairs, tiled=True)
    dq = lax.all_to_all(dq, both, 0, 0, axis_index_groups=teams, tiled=True)
    dkv = dkv.reshape(2, planes, slots, 2, tok, head_dim).transpose(1, 0, 2, 3, 4, 5)
    return (dq_by_token(dq, tok, fan),) + dkv_by_token(dkv.reshape(planes, kv_heads, 2, tok, head_dim))


def solution(mesh):
    tokens = P(("ctx", "head"), None, None)
    return jax.shard_map(
        per_device,
        mesh=mesh,
        in_specs=(tokens,) * 5 + (P(("ctx", "head"), None), P()),
        out_specs=(tokens,) * 3,
        check_vma=False,
    )
```
